32 devices in a mesh: frames: 4 (over z), mp: 4 (over x, core), dp: 2 (over y).
Axes of the slice: x: 2, y: 2, z: 4, core: 2. Of those that a mesh axis runs over, the one named last changes fastest.
Arguments:
- projections: bfloat16 [2, 8, 96, 3, 3584], P('dp', 'frames', None, None, 'mp'), may hold values from -18 to 18
- perturbation: bfloat16 [2, 8, 96, 3, 3584], P('dp', 'frames', None, None, 'mp'), may hold values from -44 to 44
- out_weight: bfloat16 [3584, 3584], P('frames', 'mp'), may hold values from -0.09375 to 0.09375
- norm_gain: float32 [3584], P('mp'), may hold values from 0.25 to 1.75
- live_counts: int32 [2, 8], P('dp'), may hold values from 72 to 96, as said below
Outputs:
- features: bfloat16 [2, 8, 96, 3584], P('dp', 'frames', None, 'mp')
- penalty: float32 [2], P('dp')
- gain_grad: float32 [3584], P('mp')
The draws below stay inside these ranges and needn't reach their ends.
Inputs may be any that keep to these rules, and one draw needn't show every extreme that they name: `live_counts`: in each clip one slot has all 96 tokens live and another has 72 live.
All inputs are finite; a program needn't handle non-finite values.
Results may differ from the reference program's by a relative error of at most 0.0057.
Values may be sent and summed in bfloat16 or wider, within the bound.
No kernel may reach another device: no remote copies, remote signals or barrier semaphores. Data moves between devices by JAX's collectives and lax.ppermute only.
A program may use at most 64 MiB of HBM per device.

```python
import math
import jax
import jax.numpy as jnp
from jax import lax

D = 3584
HEADS = 28
HEAD_DIM = 128
TILE = 96
FRAMES = 8
TOKENS = 768
CLIPS = 2


def draw_projections(key, part):
    key = jax.random.fold_in(key, 11)
    array_shape = (CLIPS, FRAMES, TILE, 3, D)
    values = jnp.clip(jax.random.normal(key, array_shape, jnp.float32), -6.0, 6.0)
    return values.astype(jnp.bfloat16)


def draw_perturbation(key, part):
    key = jax.random.fold_in(key, 23)
    array_shape = (CLIPS, FRAMES, TILE, 3, D)
    frame_pos = jnp.arange(FRAMES).astype(jnp.float32)[None, :, None, None, None]
    rising = 1.0 + 2.0 * frame_pos / (FRAMES - 1)
    values = jnp.clip(jax.random.normal(key, array_shape, jnp.float32), -6.0, 6.0) * rising
    return values.astype(jnp.bfloat16)


def draw_live_counts(key, part):
    key = jax.random.fold_in(key, 37)
    first_key, second_key = jax.random.split(key)
    counts = jax.random.randint(first_key, (CLIPS, FRAMES), 3 * TILE // 4, TILE + 1)
    chosen = jax.random.randint(second_key, (CLIPS, 1), 0, FRAMES)
    column = jnp.arange(FRAMES)[None, :]
    counts = jnp.where(column == chosen, TILE, counts)
    counts = jnp.where(column == (chosen + FRAMES // 2) % FRAMES, 3 * TILE // 4, counts)
    return counts.astype(jnp.int32)


def level_of(own_key, extent, pieces, low, high):
    def one(dim, parts):
        heights = jax.random.uniform(jax.random.fold_in(jax.random.fold_in(own_key, 6), dim), (parts,), jnp.float32, low / len(pieces), high / len(pieces))
        return jnp.repeat(jnp.exp(heights), extent[dim] // parts).reshape((-1,) + (1,) * (len(extent) - dim - 1))

    level = one(*pieces[0])
    for cut in pieces[1:]:
        level = level * one(*cut)
    return level


def noise(own_key, extent, deviation, limit, pieces=(), dtype=jnp.bfloat16):
    entries = jax.random.normal(own_key, extent, jnp.float32) * deviation
    if len(pieces) > 0:
        entries = level_of(own_key, extent, pieces, -0.22, 0.18) * entries
    return jnp.clip(entries, min=-limit, max=limit).astype(dtype)


def setup_inputs(seed: int = 0) -> dict:
    key_of = jax.random.split(jax.random.key(seed), 6)
    projections = draw_projections(jax.random.fold_in(key_of[5], 71), 0)
    perturbation = draw_perturbation(jax.random.fold_in(key_of[5], 71), 0)
    out_weight = noise(key_of[2], (D, D), D ** -0.5, 0.09375, ((0, 4), (1, 4)))
    norm_gain = jnp.clip(1.0 + 0.15 * jax.random.normal(key_of[3], (D,), jnp.float32), 0.25, 1.75)
    live_counts = draw_live_counts(jax.random.fold_in(key_of[5], 71), 0)
    return {"projections": projections, "perturbation": perturbation, "out_weight": out_weight, "norm_gain": norm_gain, "live_counts": live_counts}


sigma_noise = 0.25
epsilon = 1e-06

def attend(query_rows, key_rows, value_rows, key_live):
    scores = jnp.einsum('rhe,mhe->hrm', query_rows.astype(jnp.float32), key_rows.astype(jnp.float32)) * (1.0 / math.sqrt(HEAD_DIM))
    masked = jnp.where(key_live[None, None, :], scores, -1e+30)
    largest = lax.optimization_barrier(jnp.max(masked, axis=-1, keepdims=True))
    weights = jnp.exp(masked - largest) * key_live[None, None, :].astype(jnp.float32)
    probabilities = (weights / lax.optimization_barrier(jnp.sum(weights, axis=-1, keepdims=True))).astype(jnp.bfloat16)
    mixed = jnp.einsum('hrm,mhe->rhe', probabilities.astype(jnp.float32), value_rows.astype(jnp.float32))
    return mixed.astype(jnp.bfloat16)

def stream_attention(stream, counts):
    padded = jnp.pad(stream, ((1, 1), (0, 0), (0, 0), (0, 0)))
    padded_counts = jnp.pad(counts, (1, 1))
    live_tokens = jnp.arange(TILE)[None, :] < padded_counts[:, None]
    windows = padded.reshape((FRAMES + 2) // 2, 2 * TILE, 3, HEADS, HEAD_DIM)
    live_windows = live_tokens.reshape((FRAMES + 2) // 2, 2 * TILE)

    def one_window(item):
        block, window_live = item
        return attend(block[:, 0], block[:, 1], block[:, 2], window_live)
    result = lax.map(one_window, (windows, live_windows))
    return result.reshape(FRAMES + 2, TILE, D)[1:-1]

def reference(projections, perturbation, out_weight, norm_gain, live_counts):
    perturbed = (projections.astype(jnp.float32) + sigma_noise * perturbation.astype(jnp.float32)).astype(jnp.bfloat16)
    live_mask = (jnp.arange(TILE)[None, None, :] < live_counts[:, :, None]).astype(jnp.float32)[..., None]
    normed_list = []
    for stream in (projections, perturbed):
        attended = jnp.stack([stream_attention(stream[clip_index], live_counts[clip_index]) for clip_index in range(CLIPS)])
        projected = jnp.dot(attended.reshape(-1, D), out_weight, preferred_element_type=jnp.float32).reshape(CLIPS, FRAMES, TILE, D)
        squares = lax.optimization_barrier(jnp.sum(projected * projected, axis=-1, keepdims=True))
        normed_list.append(projected * lax.rsqrt(squares / D + epsilon))
    normed_clean, normed_perturbed = normed_list
    features = (normed_clean * norm_gain * live_mask).astype(jnp.bfloat16)
    difference = (normed_perturbed - normed_clean) * live_mask
    feature_sums = lax.optimization_barrier(jnp.sum(difference * difference, axis=(1, 2)))
    penalty = lax.optimization_barrier(jnp.sum(feature_sums * norm_gain * norm_gain, axis=-1)) / (sigma_noise * sigma_noise * TOKENS * D)
    gain_grad = norm_gain * lax.optimization_barrier(jnp.sum(feature_sums, axis=0)) / (sigma_noise * sigma_noise * TOKENS)
    return (features, penalty, gain_grad)
```

```python
import functools
import math

import jax
import jax.numpy as jnp
from jax import lax
from jax.experimental import pallas as pl
from jax.experimental.pallas import tpu as pltpu
from jax.sharding import PartitionSpec as P

HEAD_DIM = 128


sigma_noise = 0.25
epsilon = 1e-06


def perturb(clean, noise):
    return (clean.astype(jnp.float32) + sigma_noise * noise.astype(jnp.float32)).astype(jnp.bfloat16)


def attend_kernel(counts_ref, clean_ref, noise_ref, left_ref, right_ref, out_ref):
    tile_len = clean_ref.shape[2]
    slots = clean_ref.shape[0]
    token_pos = lax.broadcasted_iota(jnp.int32, (1, tile_len), 1)
    hidden = jnp.float32(-1e30)
    live = [token_pos < counts_ref[n] for n in range(slots + 2)]

    def half_scores(query, key, key_live):
        scores = lax.dot_general(
            query, key, (((1,), (1,)), ((), ())), preferred_element_type=jnp.float32
        ) * (1.0 / math.sqrt(HEAD_DIM))
        return jnp.where(key_live, scores, hidden)

    for slot in range(slots):
        for stream in range(2):

            def part(which, at=slot, stream=stream):
                clean = clean_ref[at, which]
                return clean if stream == 0 else perturb(clean, noise_ref[at, which])

            query = part(0)
            halo_ref = left_ref if slot == 0 else right_ref
            halo_live = live[0] if slot == 0 else live[slots + 1]
            own = half_scores(query, part(1), live[slot + 1])
            far = half_scores(query, halo_ref[stream, 0], halo_live)
            largest = jnp.max(jnp.maximum(own, far), axis=-1, keepdims=True)
            own = jnp.exp(own - largest)
            far = jnp.exp(far - largest)
            scale = 1.0 / jnp.sum(own + far, axis=-1, keepdims=True)
            mixed = jnp.dot(
                (own * scale).astype(jnp.bfloat16), part(2), preferred_element_type=jnp.float32
            ) + jnp.dot(
                (far * scale).astype(jnp.bfloat16),
                halo_ref[stream, 1],
                preferred_element_type=jnp.float32,
            )
            out_ref[stream, slot] = mixed.astype(jnp.bfloat16)


def attention(nearby, clean, noise, left, right):
    slots, _, tile_len, width = clean.shape
    heads = width // HEAD_DIM
    own_spec = pl.BlockSpec((slots, 3, tile_len, HEAD_DIM), lambda h, c: (0, 0, 0, h))
    halo_spec = pl.BlockSpec((2, 2, tile_len, HEAD_DIM), lambda h, c: (0, 0, 0, h))
    flops = 2 * slots * 2 * 2 * 2 * tile_len * 2 * tile_len * width
    return pl.pallas_call(
        attend_kernel,
        grid_spec=pltpu.PrefetchScalarGridSpec(
            num_scalar_prefetch=1,
            grid=(heads,),
            in_specs=[own_spec, own_spec, halo_spec, halo_spec],
            out_specs=pl.BlockSpec((2, slots, tile_len, HEAD_DIM), lambda h, c: (0, 0, 0, h)),
        ),
        out_shape=jax.ShapeDtypeStruct((2, slots, tile_len, width), jnp.bfloat16),
        compiler_params=pltpu.CompilerParams(vmem_limit_bytes=24 * 1024 * 1024),
        cost_estimate=pl.CostEstimate(
            flops=flops, bytes_accessed=12 * slots * tile_len * width * 2, transcendentals=0
        ),
        name="attention",
    )(nearby, clean, noise, left, right)


def swap(array, axis, distance):
    count = lax.axis_size(axis)
    return lax.ppermute(array, axis, [(i, i ^ distance) for i in range(count)])


def gather_heads(block, axis):
    blocks = [block]
    distance = 1
    while distance < lax.axis_size(axis):
        blocks = blocks + [swap(b, axis, distance) for b in blocks]
        distance *= 2
    return blocks


def local(projections, perturbation, out_weight, norm_gain, live_counts):
    tile_len = projections.shape[2]
    local_width = projections.shape[4]
    slots = projections.shape[1]
    slab_count = lax.axis_size("frames")
    slab_index = lax.axis_index("frames")
    model_count = lax.axis_size("mp")
    model_index = lax.axis_index("mp")
    clip_count = lax.axis_size("dp")
    clip_index = lax.axis_index("dp")
    model_width = local_width * model_count
    token_total = slots * slab_count * tile_len

    share = out_weight.shape[0] // clip_count
    own_share = lax.dynamic_slice_in_dim(out_weight, clip_index * share, share, axis=0)
    weight = lax.all_gather(own_share, ("frames", "dp"), axis=0, tiled=True)

    clean = projections[0].transpose(0, 2, 1, 3)
    noise = perturbation[0].transpose(0, 2, 1, 3)

    def both(slot):
        return jnp.stack([clean[slot, 1:], perturb(clean[slot, 1:], noise[slot, 1:])])

    up = [(i, i + 1) for i in range(slab_count - 1)]
    down = [(i + 1, i) for i in range(slab_count - 1)]
    left = lax.ppermute(both(slots - 1), "frames", up)
    right = lax.ppermute(both(0), "frames", down)
    padded_counts = jnp.pad(live_counts[0], (1, 1))
    nearby = lax.dynamic_slice_in_dim(padded_counts, slots * slab_index, slots + 2)
    attended = attention(nearby, clean, noise, left, right)

    blocks = gather_heads(attended.reshape(2 * slots * tile_len, local_width), "mp")
    projected = None
    for distance, block in enumerate(blocks):
        rows = lax.dynamic_slice_in_dim(
            weight, (model_index ^ distance) * local_width, local_width, axis=0
        )
        term = jnp.dot(block, rows, preferred_element_type=jnp.float32)
        projected = term if projected is None else projected + term
    projected = projected.reshape(2, slots, tile_len, local_width)

    squares = lax.psum(jnp.sum(projected * projected, axis=-1), "mp")
    normed = projected * lax.rsqrt(squares / model_width + epsilon)[..., None]
    own_counts = lax.dynamic_slice_in_dim(nearby, 1, slots)
    own_live = (jnp.arange(tile_len)[None, :] < own_counts[:, None]).astype(jnp.float32)[:, :, None]
    features = (normed[0] * norm_gain * own_live).astype(jnp.bfloat16)[None]
    difference = (normed[1] - normed[0]) * own_live
    feature_sums = jnp.sum(difference * difference, axis=(0, 1))
    local_penalty = jnp.sum(feature_sums * norm_gain * norm_gain).reshape(1)
    sums = lax.dynamic_update_slice_in_dim(
        jnp.zeros((model_width,), jnp.float32), feature_sums, model_index * local_width, axis=0
    )
    penalties = lax.dynamic_update_slice_in_dim(
        jnp.zeros((clip_count,), jnp.float32), local_penalty, clip_index, axis=0
    )
    total = lax.psum(jnp.concatenate([sums, penalties]), ("frames", "mp", "dp"))
    penalty = lax.dynamic_slice_in_dim(total, model_width + clip_index, 1, axis=0) / (
        sigma_noise * sigma_noise * token_total * model_width
    )
    gain_grad = (
        norm_gain
        * lax.dynamic_slice_in_dim(total, model_index * local_width, local_width, axis=0)
        / (sigma_noise * sigma_noise * token_total)
    )
    return (features, penalty, gain_grad)


def solution(mesh):
    placed = (
        P("dp", "frames", None, None, "mp"),
        P("dp", "frames", None, None, "mp"),
        P("frames", "mp"),
        P("mp"),
        P("dp", None),
    )
    return jax.shard_map(
        local,
        mesh=mesh,
        in_specs=placed,
        out_specs=(P("dp", "frames", None, "mp"), P("dp"), P("mp")),
        check_vma=False,
    )
```

```python
import math

import jax
import jax.numpy as jnp
from jax import lax
from jax.experimental import pallas as pl
from jax.experimental.pallas import tpu as pltpu
from jax.sharding import PartitionSpec as P

HEAD_DIM = 128
HEADS_AT_ONCE = 1


sigma_noise = 0.25
epsilon = 1e-06


def perturb(clean, noise):
    return (clean.astype(jnp.float32) + sigma_noise * noise.astype(jnp.float32)).astype(jnp.bfloat16)


def attend_kernel(counts_ref, own_ref, left_ref, right_ref, out_ref):
    slots, _, tile_len, width = own_ref.shape
    key_pos = lax.broadcasted_iota(jnp.int32, (1, 2 * tile_len), 1)
    live = []
    for slot in range(slots):
        own_count = counts_ref[slot + 1]
        far_count = counts_ref[0 if slot == 0 else slots + 1]
        live.append((key_pos < own_count) | ((key_pos >= tile_len) & (key_pos < tile_len + far_count)))
    units = [(slot, head) for head in range(width // HEAD_DIM) for slot in range(slots)]

    scores = []
    for slot, head in units:
        cols = pl.ds(head * HEAD_DIM, HEAD_DIM)
        halo_ref = left_ref if slot == 0 else right_ref
        keys = jnp.concatenate([own_ref[slot, 1, :, cols], halo_ref[0, :, cols]], axis=0)
        raw = lax.dot_general(
            own_ref[slot, 0, :, cols],
            keys,
            (((1,), (1,)), ((), ())),
            preferred_element_type=jnp.float32,
        )
        scores.append(jnp.where(live[slot], raw * (1.0 / math.sqrt(HEAD_DIM)), jnp.float32(-1e30)))
    largest = [jnp.max(s, axis=-1, keepdims=True) for s in scores]
    weights = [jnp.exp(s - top) for s, top in zip(scores, largest)]
    totals = [jnp.sum(w, axis=-1, keepdims=True) for w in weights]
    for (slot, head), weight, total in zip(units, weights, totals):
        cols = pl.ds(head * HEAD_DIM, HEAD_DIM)
        halo_ref = left_ref if slot == 0 else right_ref
        values = jnp.concatenate([own_ref[slot, 2, :, cols], halo_ref[1, :, cols]], axis=0)
        probabilities = (weight * (1.0 / total)).astype(jnp.bfloat16)
        out_ref[slot, :, cols] = jnp.dot(
            probabilities, values, preferred_element_type=jnp.float32
        ).astype(jnp.bfloat16)


def attention(nearby, own, left, right):
    slots, _, tile_len, width = own.shape
    block = HEADS_AT_ONCE * HEAD_DIM
    own_spec = pl.BlockSpec((slots, 3, tile_len, block), lambda h, c: (0, 0, 0, h))
    halo_spec = pl.BlockSpec((2, tile_len, block), lambda h, c: (0, 0, h))
    return pl.pallas_call(
        attend_kernel,
        grid_spec=pltpu.PrefetchScalarGridSpec(
            num_scalar_prefetch=1,
            grid=(width // block,),
            in_specs=[own_spec, halo_spec, halo_spec],
            out_specs=pl.BlockSpec((slots, tile_len, block), lambda h, c: (0, 0, h)),
        ),
        out_shape=jax.ShapeDtypeStruct((slots, tile_len, width), jnp.bfloat16),
        compiler_params=pltpu.CompilerParams(vmem_limit_bytes=24 * 1024 * 1024),
        cost_estimate=pl.CostEstimate(
            flops=16 * slots * tile_len * tile_len * width,
            bytes_accessed=12 * slots * tile_len * width,
            transcendentals=0,
        ),
        name="attention",
    )(nearby, own, left, right)


def project_kernel(shard_total, with_total, places_ref, *refs):
    rows_ref = refs[0]
    weight_refs = refs[1 : 1 + shard_total]
    out_ref = refs[-1]
    shard = pl.program_id(1)

    def add(weight_ref, first):
        term = jnp.dot(
            rows_ref[0, 0], weight_ref[...], preferred_element_type=jnp.float32
        )
        if not first:
            out_ref[0] = out_ref[0] + term
        elif with_total:
            out_ref[0] = refs[1 + shard_total][0] + term
        else:
            out_ref[0] = term

    for n in range(shard_total):
        pl.when(shard == n)(lambda n=n: add(weight_refs[n], n == 0))


def project(places, clip_index, rows, weights, total):
    _, clip_count, row_count, depth = rows.shape
    columns = weights[0].shape[1]
    shard_total = len(weights)
    scalars = jnp.concatenate([jnp.stack(places), clip_index[None]]).astype(jnp.int32)
    out_spec = pl.BlockSpec((1, row_count, columns), lambda c, j, s: (c, 0, 0))
    operands = [rows, *weights]
    in_specs = [
        pl.BlockSpec(
            (1, 1, row_count, depth), lambda c, j, s: (s[j], c ^ s[shard_total], 0, 0)
        )
    ] + [pl.BlockSpec((depth, columns), lambda c, j, s: (0, 0)) for _ in weights]
    if total is not None:
        operands.append(total)
        in_specs.append(out_spec)

    def kernel(*refs):
        project_kernel(shard_total, total is not None, *refs)

    return pl.pallas_call(
        kernel,
        grid_spec=pltpu.PrefetchScalarGridSpec(
            num_scalar_prefetch=1,
            grid=(clip_count, shard_total),
            in_specs=in_specs,
            out_specs=out_spec,
        ),
        out_shape=jax.ShapeDtypeStruct((clip_count, row_count, columns), jnp.float32),
        compiler_params=pltpu.CompilerParams(vmem_limit_bytes=40 * 1024 * 1024),
        cost_estimate=pl.CostEstimate(
            flops=2 * clip_count * row_count * depth * columns * shard_total,
            bytes_accessed=shard_total * depth * (clip_count * row_count + columns) * 2,
            transcendentals=0,
        ),
        name="project",
    )(scalars, *operands)


def swap(array, axis, distance):
    count = lax.axis_size(axis)
    return lax.ppermute(array, axis, [(i, i ^ distance) for i in range(count)])


def distances(axis):
    count = lax.axis_size(axis)
    return [(axis, 1 << bit) for bit in reversed(range(count.bit_length() - 1))]


def spread(block, order):
    blocks = {(0, 0): block}
    for axis, distance in order:
        for (model, clip), held in list(blocks.items()):
            key = (model ^ distance, clip) if axis == "mp" else (model, clip ^ distance)
            blocks[key] = swap(held, axis, distance)
    return blocks


def add_up(array, order):
    for axis, distance in order:
        array = array + swap(array, axis, distance)
    return array


def pick(options, index):
    return lax.select_n(index, *options) if len(options) > 1 else options[0]


def local(projections, perturbation, out_weight, norm_gain, live_counts):
    tile_len = projections.shape[2]
    local_width = projections.shape[4]
    slots = projections.shape[1]
    slab_count = lax.axis_size("frames")
    slab_index = lax.axis_index("frames")
    model_count = lax.axis_size("mp")
    model_index = lax.axis_index("mp")
    clip_count = lax.axis_size("dp")
    clip_index = lax.axis_index("dp")
    model_width = local_width * model_count
    token_total = slots * slab_count * tile_len
    half = local_width // clip_count
    near_rows = slots * tile_len

    def own_columns(array):
        return pick(
            [array[..., n * half : (n + 1) * half] for n in range(clip_count)], clip_index
        )

    clean = projections[0].transpose(0, 2, 1, 3)
    noise = perturbation[0].transpose(0, 2, 1, 3)
    perturbed = perturb(clean, noise)
    up = [(i, i + 1) for i in range(slab_count - 1)]
    down = [(i + 1, i) for i in range(slab_count - 1)]

    own_weight = own_columns(out_weight)
    shards = [(own_weight, slab_index)]
    line = slab_count == model_count
    if line:
        rising = falling = own_weight
        for step in range(1, slab_count):
            rising = lax.ppermute(rising, "frames", up[step - 1 :])
            falling = lax.ppermute(falling, "frames", down[: slab_count - step])
            shards += [
                (rising, jnp.maximum(slab_index - step, 0)),
                (falling, jnp.minimum(slab_index + step, slab_count - 1)),
            ]

    spread_counts = spread(live_counts[0], distances("dp"))
    counts = [
        pick([spread_counts[0, c ^ d] for d in range(clip_count)], clip_index)
        for c in range(clip_count)
    ]
    near_counts = [
        lax.dynamic_slice_in_dim(jnp.pad(n, (1, 1)), slots * slab_index, slots + 2) for n in counts
    ]
    nearby = pick(near_counts, clip_index)

    gathered = []
    for stream, order in (
        (clean, distances("dp") + distances("mp")),
        (perturbed, distances("mp")[:1] + distances("dp") + distances("mp")[1:]),
    ):
        left = lax.ppermute(stream[slots - 1, 1:], "frames", up)
        right = lax.ppermute(stream[0, 1:], "frames", down)
        attended = attention(nearby, stream, left, right)
        gathered.append(spread(attended.reshape(near_rows, local_width), order))
    rows = jnp.stack(
        [
            jnp.stack(
                [jnp.concatenate([g[m, c] for g in gathered], axis=0) for c in range(clip_count)]
            )
            for m in range(model_count)
        ]
    )

    if line:
        early, late = shards[:-2], shards[-2:]
        total = project(
            [place ^ model_index for _, place in early],
            clip_index,
            rows,
            [weight for weight, _ in early],
            None,
        )
        total = project(
            [place ^ model_index for _, place in late],
            clip_index,
            rows,
            [weight for weight, _ in late],
            total,
        )
    else:
        weight = lax.all_gather(own_weight, "frames", axis=0, tiled=True)
        weight = weight.reshape(model_count, local_width, half)
        total = project(
            [jnp.int32(m) for m in range(model_count)],
            clip_index,
            rows,
            [
                lax.dynamic_index_in_dim(weight, model_index ^ m, 0, keepdims=False)
                for m in range(model_count)
            ],
            None,
        )
    projected = total.reshape(clip_count, 2, slots, tile_len, half)

    everyone = distances("dp") + distances("mp")
    squares = add_up(jnp.sum(projected * projected, axis=-1), everyone)
    scale = lax.rsqrt(squares / model_width + epsilon)[..., None]
    own_counts = jnp.stack([n[1 : slots + 1] for n in near_counts])
    live = (jnp.arange(tile_len) < own_counts[..., None]).astype(jnp.float32)[..., None]
    gain = own_columns(norm_gain)
    normed = projected * scale
    features = (normed[:, 0] * gain * live).astype(jnp.bfloat16)
    difference = (normed[:, 1] - normed[:, 0]) * live
    feature_sums = jnp.sum(difference * difference, axis=(1, 2))
    penalties = jnp.sum(feature_sums * gain * gain, axis=-1)

    columns = [pick([features[d] for d in range(clip_count)], clip_index)]
    for distance in range(1, clip_count):
        sent = pick([features[d ^ distance] for d in range(clip_count)], clip_index)
        columns.append(swap(sent, "dp", distance))
    features = jnp.concatenate(
        [
            pick([columns[n ^ d] for d in range(clip_count)], clip_index)
            for n in range(clip_count)
        ],
        axis=-1,
    )[None]

    sums = jnp.concatenate([jnp.sum(feature_sums, axis=0), penalties])
    sums = add_up(sums, distances("frames"))
    gain_halves = spread(sums[:half] * gain, distances("dp"))
    gain_grad = jnp.concatenate(
        [
            pick([gain_halves[0, n ^ d] for d in range(clip_count)], clip_index)
            for n in range(clip_count)
        ]
    ) / (sigma_noise * sigma_noise * token_total)
    penalties = add_up(sums[half:], everyone)
    penalty = pick([penalties[d : d + 1] for d in range(clip_count)], clip_index) / (
        sigma_noise * sigma_noise * token_total * model_width
    )
    return (features, penalty, gain_grad)


def solution(mesh):
    placed = (
        P("dp", "frames", None, None, "mp"),
        P("dp", "frames", None, None, "mp"),
        P("frames", "mp"),
        P("mp"),
        P("dp", None),
    )
    return jax.shard_map(
        local,
        mesh=mesh,
        in_specs=placed,
        out_specs=(P("dp", "frames", None, "mp"), P("dp"), P("mp")),
        check_vma=False,
    )
```

```python
import math

import jax
import jax.numpy as jnp
from jax import lax
from jax.experimental import pallas as pl
from jax.experimental.pallas import tpu as pltpu
from jax.sharding import PartitionSpec as P

HEAD_DIM = 128
HEADS_AT_ONCE = 1


sigma_noise = 0.25
epsilon = 1e-06


def perturb(clean, noise):
    return (clean.astype(jnp.float32) + sigma_noise * noise.astype(jnp.float32)).astype(jnp.bfloat16)


def attend_kernel(counts_ref, own_ref, left_ref, right_ref, out_ref):
    slots, _, tile_len, width = own_ref.shape
    key_pos = lax.broadcasted_iota(jnp.int32, (1, 2 * tile_len), 1)
    live = []
    for slot in range(slots):
        own_count = counts_ref[slot + 1]
        far_count = counts_ref[0 if slot == 0 else slots + 1]
        live.append((key_pos < own_count) | ((key_pos >= tile_len) & (key_pos < tile_len + far_count)))
    units = [(slot, head) for head in range(width // HEAD_DIM) for slot in range(slots)]

    scores = []
    for slot, head in units:
        cols = pl.ds(head * HEAD_DIM, HEAD_DIM)
        halo_ref = left_ref if slot == 0 else right_ref
        keys = jnp.concatenate([own_ref[slot, 1, :, cols], halo_ref[0, :, cols]], axis=0)
        raw = lax.dot_general(
            own_ref[slot, 0, :, cols],
            keys,
            (((1,), (1,)), ((), ())),
            preferred_element_type=jnp.float32,
        )
        scores.append(jnp.where(live[slot], raw * (1.0 / math.sqrt(HEAD_DIM)), jnp.float32(-1e30)))
    largest = [jnp.max(s, axis=-1, keepdims=True) for s in scores]
    weights = [jnp.exp(s - top) for s, top in zip(scores, largest)]
    totals = [jnp.sum(w, axis=-1, keepdims=True) for w in weights]
    for (slot, head), weight, total in zip(units, weights, totals):
        cols = pl.ds(head * HEAD_DIM, HEAD_DIM)
        halo_ref = left_ref if slot == 0 else right_ref
        values = jnp.concatenate([own_ref[slot, 2, :, cols], halo_ref[1, :, cols]], axis=0)
        probabilities = (weight * (1.0 / total)).astype(jnp.bfloat16)
        out_ref[slot, :, cols] = jnp.dot(
            probabilities, values, preferred_element_type=jnp.float32
        ).astype(jnp.bfloat16)


def attention(nearby, own, left, right):
    slots, _, tile_len, width = own.shape
    block = HEADS_AT_ONCE * HEAD_DIM
    own_spec = pl.BlockSpec((slots, 3, tile_len, block), lambda h, c: (0, 0, 0, h))
    halo_spec = pl.BlockSpec((2, tile_len, block), lambda h, c: (0, 0, h))
    return pl.pallas_call(
        attend_kernel,
        grid_spec=pltpu.PrefetchScalarGridSpec(
            num_scalar_prefetch=1,
            grid=(width // block,),
            in_specs=[own_spec, halo_spec, halo_spec],
            out_specs=pl.BlockSpec((slots, tile_len, block), lambda h, c: (0, 0, h)),
        ),
        out_shape=jax.ShapeDtypeStruct((slots, tile_len, width), jnp.bfloat16),
        compiler_params=pltpu.CompilerParams(vmem_limit_bytes=48 * 1024 * 1024),
        cost_estimate=pl.CostEstimate(
            flops=300 * slots * tile_len * tile_len * width,
            bytes_accessed=12 * slots * tile_len * width,
            transcendentals=0,
        ),
        name="attention",
    )(nearby, own, left, right)


def project(places, valid, clip_index, blocks, weights, total):
    clip_count, stream_count = len(blocks[0]), len(blocks[0][0])
    block_rows, depth = blocks[0][0][0].shape
    columns = weights[0].shape[0]
    row_count = stream_count * block_rows
    shard_total = len(weights)
    scalars = jnp.stack([jnp.int32(n) for n in (*places, *valid, clip_index)])
    flat = [block for place in blocks for clip in place for block in clip]

    def kernel(scalars_ref, *refs):
        block_refs = refs[: len(flat)]
        weight_refs = refs[len(flat) : len(flat) + shard_total]
        total_ref = refs[len(flat) + shard_total] if total is not None else None
        out_ref, rows, held, row_sem, weight_sem = refs[-5:]

        def weight_copy(shard):
            return pltpu.make_async_copy(weight_refs[shard], held.at[shard], weight_sem.at[shard])

        def row_copy(place, shard, clip, stream):
            source = block_refs[(place * clip_count + clip) * stream_count + stream]
            first = pl.multiple_of(
                (clip ^ scalars_ref[2 * shard_total]) * row_count + stream * block_rows, 16
            )
            return pltpu.make_async_copy(
                source,
                rows.at[shard, pl.ds(first, block_rows)],
                row_sem.at[shard, clip, stream],
            )

        for shard in range(shard_total):

            @pl.when(scalars_ref[shard_total + shard] == 1)
            def _():
                weight_copy(shard).start()
                for place in range(len(blocks)):

                    @pl.when(scalars_ref[shard] == place)
                    def _():
                        for clip in range(clip_count):
                            for stream in range(stream_count):
                                row_copy(place, shard, clip, stream).start()

        if total is not None:
            out_ref[...] = total_ref[...]
        else:
            out_ref[...] = jnp.zeros_like(out_ref)

        for shard in range(shard_total):

            @pl.when(scalars_ref[shard_total + shard] == 1)
            def _():
                weight_copy(shard).wait()
                for clip in range(clip_count):
                    for stream in range(stream_count):
                        row_copy(0, shard, clip, stream).wait()
                for clip in range(clip_count):
                    out_ref[clip] += lax.dot_general(
                        rows[shard, pl.ds(clip * row_count, row_count)],
                        held[shard],
                        (((1,), (1,)), ((), ())),
                        preferred_element_type=jnp.float32,
                    )

    operands = [*flat, *weights]
    in_specs = [pl.BlockSpec(memory_space=pl.ANY) for _ in operands]
    if total is not None:
        operands.append(total)
        in_specs.append(pl.BlockSpec(memory_space=pltpu.VMEM))
    return pl.pallas_call(
        kernel,
        in_specs=[pl.BlockSpec(memory_space=pltpu.SMEM)] + in_specs,
        out_specs=pl.BlockSpec(memory_space=pltpu.VMEM),
        out_shape=jax.ShapeDtypeStruct((clip_count, row_count, columns), jnp.float32),
        scratch_shapes=[
            pltpu.VMEM((shard_total, clip_count * row_count, depth), jnp.bfloat16),
            pltpu.VMEM((shard_total, columns, depth), jnp.bfloat16),
            pltpu.SemaphoreType.DMA((shard_total, clip_count, stream_count)),
            pltpu.SemaphoreType.DMA((shard_total,)),
        ],
        compiler_params=pltpu.CompilerParams(vmem_limit_bytes=56 * 1024 * 1024),
        cost_estimate=pl.CostEstimate(
            flops=2 * clip_count * row_count * depth * columns * shard_total,
            bytes_accessed=shard_total * depth * (clip_count * row_count + columns) * 2,
            transcendentals=0,
        ),
        name="project",
    )(scalars, *operands)


def swap(array, axis, distance):
    count = lax.axis_size(axis)
    return lax.ppermute(array, axis, [(i, i ^ distance) for i in range(count)])


def distances(axis):
    count = lax.axis_size(axis)
    return [(axis, 1 << bit) for bit in reversed(range(count.bit_length() - 1))]


def spread(block, order):
    blocks = {(0, 0): block}
    for axis, distance in order:
        for (model, clip), held in list(blocks.items()):
            key = (model ^ distance, clip) if axis == "mp" else (model, clip ^ distance)
            blocks[key] = swap(held, axis, distance)
    return blocks


def collect(array, axes):
    copies = jnp.broadcast_to(array[None], (lax.axis_size(axes),) + array.shape)
    return lax.all_to_all(copies, axes, split_axis=0, concat_axis=0, tiled=True)


def pick(options, index):
    return lax.select_n(index, *options) if len(options) > 1 else options[0]


def local(projections, perturbation, out_weight, norm_gain, live_counts):
    tile_len = projections.shape[2]
    local_width = projections.shape[4]
    slots = projections.shape[1]
    slab_count = lax.axis_size("frames")
    slab_index = lax.axis_index("frames")
    model_count = lax.axis_size("mp")
    model_index = lax.axis_index("mp")
    clip_count = lax.axis_size("dp")
    clip_index = lax.axis_index("dp")
    model_width = local_width * model_count
    token_total = slots * slab_count * tile_len
    half = local_width // clip_count
    near_rows = slots * tile_len

    def own_columns(array):
        return pick(
            [array[..., n * half : (n + 1) * half] for n in range(clip_count)], clip_index
        )

    clean = projections[0].transpose(0, 2, 1, 3)
    noise = perturbation[0].transpose(0, 2, 1, 3)
    perturbed = perturb(clean, noise)
    up = [(i, i + 1) for i in range(slab_count - 1)]
    down = [(i + 1, i) for i in range(slab_count - 1)]

    own_weight = own_columns(out_weight).T
    shards = [(own_weight, slab_index, jnp.int32(1))]
    line = slab_count == model_count
    if line:
        rising = falling = own_weight
        for step in range(1, slab_count):
            rising = lax.ppermute(rising, "frames", up[step - 1 :])
            falling = lax.ppermute(falling, "frames", down[: slab_count - step])
            shards += [
                (rising, jnp.maximum(slab_index - step, 0), slab_index >= step),
                (
                    falling,
                    jnp.minimum(slab_index + step, slab_count - 1),
                    slab_index < slab_count - step,
                ),
            ]

    spread_counts = spread(live_counts[0], distances("dp"))
    counts = [
        pick([spread_counts[0, c ^ d] for d in range(clip_count)], clip_index)
        for c in range(clip_count)
    ]
    near_counts = [
        lax.dynamic_slice_in_dim(jnp.pad(n, (1, 1)), slots * slab_index, slots + 2) for n in counts
    ]
    nearby = pick(near_counts, clip_index)

    gathered = []
    for stream, order in (
        (clean, distances("dp") + distances("mp")),
        (perturbed, distances("mp")[:1] + distances("dp") + distances("mp")[1:]),
    ):
        left = lax.ppermute(stream[slots - 1, 1:], "frames", up)
        right = lax.ppermute(stream[0, 1:], "frames", down)
        attended = attention(nearby, stream, left, right)
        gathered.append(spread(attended.reshape(near_rows, local_width), order))
    blocks = [
        [[g[m, c] for g in gathered] for c in range(clip_count)] for m in range(model_count)
    ]

    def project_shards(some, total):
        return project(
            [place ^ model_index for _, place, _ in some],
            [exists for _, _, exists in some],
            clip_index,
            blocks,
            [weight for weight, _, _ in some],
            total,
        )

    if line:
        total = project_shards(shards[:-2], None)
        total = project_shards(shards[-2:], total)
    else:
        weight = lax.all_gather(own_weight, "frames", axis=1, tiled=True)
        shards = [
            (
                lax.dynamic_slice_in_dim(weight, m * local_width, local_width, axis=1),
                jnp.int32(m),
                jnp.int32(1),
            )
            for m in range(model_count)
        ]
        total = project_shards(shards, None)
    projected = total.reshape(clip_count, 2, slots, tile_len, half)

    squares = jnp.sum(collect(jnp.sum(projected * projected, axis=-1), ("mp", "dp")), axis=0)
    scale = lax.rsqrt(squares / model_width + epsilon)[..., None]
    own_counts = jnp.stack([n[1 : slots + 1] for n in near_counts])
    live = (jnp.arange(tile_len) < own_counts[..., None]).astype(jnp.float32)[..., None]
    gain = own_columns(norm_gain)
    normed = projected * scale
    features = (normed[:, 0] * gain * live).astype(jnp.bfloat16)
    difference = (normed[:, 1] - normed[:, 0]) * live
    feature_sums = jnp.sum(difference * difference, axis=(1, 2))
    penalties = jnp.sum(feature_sums * gain * gain, axis=-1)

    columns = [pick([features[d] for d in range(clip_count)], clip_index)]
    for distance in range(1, clip_count):
        sent = pick([features[d ^ distance] for d in range(clip_count)], clip_index)
        columns.append(swap(sent, "dp", distance))
    features = jnp.concatenate(
        [
            pick([columns[n ^ d] for d in range(clip_count)], clip_index)
            for n in range(clip_count)
        ],
        axis=-1,
    )[None]

    sums = jnp.concatenate([jnp.sum(feature_sums, axis=0), penalties])
    sums = collect(sums, ("frames", "mp", "dp"))
    penalties = jnp.sum(sums[:, half:], axis=0)
    penalty = pick([penalties[d : d + 1] for d in range(clip_count)], clip_index) / (
        sigma_noise * sigma_noise * token_total * model_width
    )
    sums = sums[:, :half].reshape(slab_count, model_count, local_width)
    sums = lax.dynamic_index_in_dim(jnp.sum(sums, axis=0), model_index, 0, keepdims=False)
    gain_grad = norm_gain * sums / (sigma_noise * sigma_noise * token_total)
    return (features, penalty, gain_grad)


def solution(mesh):
    placed = (
        P("dp", "frames", None, None, "mp"),
        P("dp", "frames", None, None, "mp"),
        P("frames", "mp"),
        P("mp"),
        P("dp", None),
    )
    return jax.shard_map(
        local,
        mesh=mesh,
        in_specs=placed,
        out_specs=(P("dp", "frames", None, "mp"), P("dp"), P("mp")),
        check_vma=False,
    )
```

```python
import math

import jax
import jax.numpy as jnp
from jax import lax
from jax.experimental import pallas as pl
from jax.experimental.pallas import tpu as pltpu
from jax.sharding import PartitionSpec as P

HEAD_DIM = 128
HEADS_AT_ONCE = 1


sigma_noise = 0.25
epsilon = 1e-06


def perturb(clean, noise):
    return (clean.astype(jnp.float32) + sigma_noise * noise.astype(jnp.float32)).astype(jnp.bfloat16)


def attend_kernel(counts_ref, own_ref, left_ref, right_ref, out_ref):
    slots, _, tile_len, width = own_ref.shape
    key_pos = lax.broadcasted_iota(jnp.int32, (1, 2 * tile_len), 1)
    live = []
    for slot in range(slots):
        own_count = counts_ref[slot + 1]
        far_count = counts_ref[0 if slot == 0 else slots + 1]
        live.append((key_pos < own_count) | ((key_pos >= tile_len) & (key_pos < tile_len + far_count)))
    units = [(slot, head) for head in range(width // HEAD_DIM) for slot in range(slots)]

    scores = []
    for slot, head in units:
        cols = pl.ds(head * HEAD_DIM, HEAD_DIM)
        halo_ref = left_ref if slot == 0 else right_ref
        keys = jnp.concatenate([own_ref[slot, 1, :, cols], halo_ref[0, :, cols]], axis=0)
        raw = lax.dot_general(
            own_ref[slot, 0, :, cols],
            keys,
            (((1,), (1,)), ((), ())),
            preferred_element_type=jnp.float32,
        )
        scores.append(jnp.where(live[slot], raw * (1.0 / math.sqrt(HEAD_DIM)), jnp.float32(-1e30)))
    largest = [jnp.max(s, axis=-1, keepdims=True) for s in scores]
    weights = [jnp.exp(s - top) for s, top in zip(scores, largest)]
    totals = [jnp.sum(w, axis=-1, keepdims=True) for w in weights]
    for (slot, head), weight, total in zip(units, weights, totals):
        cols = pl.ds(head * HEAD_DIM, HEAD_DIM)
        halo_ref = left_ref if slot == 0 else right_ref
        values = jnp.concatenate([own_ref[slot, 2, :, cols], halo_ref[1, :, cols]], axis=0)
        probabilities = (weight * (1.0 / total)).astype(jnp.bfloat16)
        out_ref[slot, :, cols] = jnp.dot(
            probabilities, values, preferred_element_type=jnp.float32
        ).astype(jnp.bfloat16)


def attention(nearby, own, left, right):
    slots, _, tile_len, width = own.shape
    block = HEADS_AT_ONCE * HEAD_DIM
    own_spec = pl.BlockSpec((slots, 3, tile_len, block), lambda h, c: (0, 0, 0, h))
    halo_spec = pl.BlockSpec((2, tile_len, block), lambda h, c: (0, 0, h))
    return pl.pallas_call(
        attend_kernel,
        grid_spec=pltpu.PrefetchScalarGridSpec(
            num_scalar_prefetch=1,
            grid=(width // block,),
            in_specs=[own_spec, halo_spec, halo_spec],
            out_specs=pl.BlockSpec((slots, tile_len, block), lambda h, c: (0, 0, h)),
        ),
        out_shape=jax.ShapeDtypeStruct((slots, tile_len, width), jnp.bfloat16),
        compiler_params=pltpu.CompilerParams(vmem_limit_bytes=48 * 1024 * 1024),
        cost_estimate=pl.CostEstimate(
            flops=300 * slots * tile_len * tile_len * width,
            bytes_accessed=12 * slots * tile_len * width,
            transcendentals=0,
        ),
        name="attention",
    )(nearby, own, left, right)


def project(places, valid, clip_index, blocks, weights, total):
    clip_count, stream_count = len(blocks[0]), len(blocks[0][0])
    block_rows, depth = blocks[0][0][0].shape
    columns = weights[0].shape[0]
    row_count = stream_count * block_rows
    shard_total = len(weights)
    scalars = jnp.stack([jnp.int32(n) for n in (*places, *valid, clip_index)])
    flat = [block for place in blocks for clip in place for block in clip]

    def kernel(scalars_ref, *refs):
        block_refs = refs[: len(flat)]
        weight_refs = refs[len(flat) : len(flat) + shard_total]
        total_ref = refs[len(flat) + shard_total] if total is not None else None
        out_ref, squares_ref, rows, held, row_sem, weight_sem, total_sem = refs[-7:]

        def weight_copy(shard):
            return pltpu.make_async_copy(weight_refs[shard], held.at[shard], weight_sem.at[shard])

        def row_copy(place, shard, clip, stream):
            source = block_refs[(place * clip_count + clip) * stream_count + stream]
            first = pl.multiple_of(
                (clip ^ scalars_ref[2 * shard_total]) * row_count + stream * block_rows, 16
            )
            return pltpu.make_async_copy(
                source,
                rows.at[shard, pl.ds(first, block_rows)],
                row_sem.at[shard, clip, stream],
            )

        for shard in range(shard_total):

            @pl.when(scalars_ref[shard_total + shard] == 1)
            def _():
                weight_copy(shard).start()
                for place in range(len(blocks)):

                    @pl.when(scalars_ref[shard] == place)
                    def _():
                        for clip in range(clip_count):
                            for stream in range(stream_count):
                                row_copy(place, shard, clip, stream).start()

        if total is not None:
            total_copy = pltpu.make_async_copy(total_ref, out_ref, total_sem)
            total_copy.start()
            total_copy.wait()
        else:
            out_ref[...] = jnp.zeros_like(out_ref)

        for shard in range(shard_total):

            @pl.when(scalars_ref[shard_total + shard] == 1)
            def _():
                weight_copy(shard).wait()
                for clip in range(clip_count):
                    for stream in range(stream_count):
                        row_copy(0, shard, clip, stream).wait()
                for clip in range(clip_count):
                    out_ref[clip] += lax.dot_general(
                        rows[shard, pl.ds(clip * row_count, row_count)],
                        held[shard],
                        (((1,), (1,)), ((), ())),
                        preferred_element_type=jnp.float32,
                    )

        ones = jnp.ones((8, columns), jnp.float32)
        for clip in range(clip_count):
            squares_ref[clip] = lax.dot_general(
                ones,
                out_ref[clip] * out_ref[clip],
                (((1,), (1,)), ((), ())),
                precision=lax.Precision.HIGHEST,
                preferred_element_type=jnp.float32,
            )

    operands = [*flat, *weights]
    if total is not None:
        operands.append(total)
    in_specs = [pl.BlockSpec(memory_space=pl.ANY) for _ in operands]
    total, squares = pl.pallas_call(
        kernel,
        in_specs=[pl.BlockSpec(memory_space=pltpu.SMEM)] + in_specs,
        out_specs=[pl.BlockSpec(memory_space=pltpu.VMEM)] * 2,
        out_shape=[
            jax.ShapeDtypeStruct((clip_count, row_count, columns), jnp.float32),
            jax.ShapeDtypeStruct((clip_count, 8, row_count), jnp.float32),
        ],
        scratch_shapes=[
            pltpu.VMEM((shard_total, clip_count * row_count, depth), jnp.bfloat16),
            pltpu.VMEM((shard_total, columns, depth), jnp.bfloat16),
            pltpu.SemaphoreType.DMA((shard_total, clip_count, stream_count)),
            pltpu.SemaphoreType.DMA((shard_total,)),
            pltpu.SemaphoreType.DMA,
        ],
        compiler_params=pltpu.CompilerParams(vmem_limit_bytes=56 * 1024 * 1024),
        cost_estimate=pl.CostEstimate(
            flops=2 * clip_count * row_count * depth * columns * shard_total,
            bytes_accessed=shard_total * depth * (clip_count * row_count + columns) * 2,
            transcendentals=0,
        ),
        name="project",
    )(scalars, *operands)
    return total, squares[:, 0]


def swap(array, axis, distance):
    count = lax.axis_size(axis)
    return lax.ppermute(array, axis, [(i, i ^ distance) for i in range(count)])


def distances(axis):
    count = lax.axis_size(axis)
    return [(axis, 1 << bit) for bit in reversed(range(count.bit_length() - 1))]


def spread(block, order):
    blocks = {(0, 0): block}
    for axis, distance in order:
        for (model, clip), held in list(blocks.items()):
            key = (model ^ distance, clip) if axis == "mp" else (model, clip ^ distance)
            blocks[key] = swap(held, axis, distance)
    return blocks


def collect(array, axes):
    copies = jnp.broadcast_to(array[None], (lax.axis_size(axes),) + array.shape)
    return lax.all_to_all(copies, axes, split_axis=0, concat_axis=0, tiled=True)


def pick(options, index):
    return lax.select_n(index, *options) if len(options) > 1 else options[0]


def local(projections, perturbation, out_weight, norm_gain, live_counts):
    tile_len = projections.shape[2]
    local_width = projections.shape[4]
    slots = projections.shape[1]
    slab_count = lax.axis_size("frames")
    slab_index = lax.axis_index("frames")
    model_count = lax.axis_size("mp")
    model_index = lax.axis_index("mp")
    clip_count = lax.axis_size("dp")
    clip_index = lax.axis_index("dp")
    model_width = local_width * model_count
    token_total = slots * slab_count * tile_len
    half = local_width // clip_count
    near_rows = slots * tile_len

    def own_columns(array):
        return pick(
            [array[..., n * half : (n + 1) * half] for n in range(clip_count)], clip_index
        )

    clean = projections[0].transpose(0, 2, 1, 3)
    noise = perturbation[0].transpose(0, 2, 1, 3)
    perturbed = perturb(clean, noise)
    up = [(i, i + 1) for i in range(slab_count - 1)]
    down = [(i + 1, i) for i in range(slab_count - 1)]

    streams = (clean, perturbed)
    tails = [stream[slots - 1, 1:] for stream in streams]
    heads = [stream[0, 1:] for stream in streams]
    tails, heads, out_weight = lax.optimization_barrier((tails, heads, out_weight))
    left = [lax.ppermute(tail, "frames", up) for tail in tails]
    right = [lax.ppermute(head, "frames", down) for head in heads]

    own_weight = own_columns(out_weight).T
    shards = [(own_weight, slab_index, jnp.int32(1))]
    line = slab_count == model_count and slab_count > 2
    if line:
        rising = falling = own_weight
        last = slab_count - 1
        across = None
        for step in range(1, last):
            rising = lax.ppermute(rising, "frames", up[step - 1 :])
            falling = lax.ppermute(falling, "frames", down[: slab_count - step])
            shards += [
                (rising, jnp.maximum(slab_index - step, 0), slab_index >= step),
                (falling, jnp.minimum(slab_index + step, last), slab_index < slab_count - step),
            ]
            if across is None:
                across = lax.ppermute(own_weight, "frames", [(0, last), (last, 0)])
        at_end = (slab_index == 0) | (slab_index == last)
        shards.append((across, jnp.where(slab_index == 0, last, 0), at_end))

    spread_counts = spread(live_counts[0], distances("dp"))
    counts = [
        pick([spread_counts[0, c ^ d] for d in range(clip_count)], clip_index)
        for c in range(clip_count)
    ]
    near_counts = [
        lax.dynamic_slice_in_dim(jnp.pad(n, (1, 1)), slots * slab_index, slots + 2) for n in counts
    ]
    nearby = pick(near_counts, clip_index)

    gathered = []
    orders = (
        distances("dp") + distances("mp"),
        distances("mp")[:1] + distances("dp") + distances("mp")[1:],
    )
    for n, order in enumerate(orders):
        attended = attention(nearby, streams[n], left[n], right[n])
        gathered.append(spread(attended.reshape(near_rows, local_width), order))
    blocks = [
        [[g[m, c] for g in gathered] for c in range(clip_count)] for m in range(model_count)
    ]

    def project_shards(some, total):
        return project(
            [place ^ model_index for _, place, _ in some],
            [exists for _, _, exists in some],
            clip_index,
            blocks,
            [weight for weight, _, _ in some],
            total,
        )

    if line:
        total, _ = project_shards(shards[:3], None)
        total, squares = project_shards(shards[3:], total)
    else:
        weight = lax.all_gather(own_weight, "frames", axis=1, tiled=True)
        shards = [
            (
                lax.dynamic_slice_in_dim(weight, m * local_width, local_width, axis=1),
                jnp.int32(m),
                jnp.int32(1),
            )
            for m in range(model_count)
        ]
        total, squares = project_shards(shards, None)
    projected = total.reshape(clip_count, 2, slots, tile_len, half)

    squares = jnp.sum(collect(squares, ("mp", "dp")), axis=0)
    squares = squares.reshape(clip_count, 2, slots, tile_len, 1)
    scale = lax.rsqrt(squares / model_width + epsilon)
    own_counts = jnp.stack([n[1 : slots + 1] for n in near_counts])
    live = (jnp.arange(tile_len) < own_counts[..., None]).astype(jnp.float32)[..., None]
    gain = own_columns(norm_gain)
    normed = projected * scale
    features = (normed[:, 0] * gain * live).astype(jnp.bfloat16)
    difference = (normed[:, 1] - normed[:, 0]) * live
    feature_sums = jnp.sum(difference * difference, axis=(1, 2))
    penalties = jnp.sum(feature_sums * gain * gain, axis=-1)

    columns = [pick([features[d] for d in range(clip_count)], clip_index)]
    for distance in range(1, clip_count):
        sent = pick([features[d ^ distance] for d in range(clip_count)], clip_index)
        columns.append(swap(sent, "dp", distance))
    features = jnp.concatenate(
        [
            pick([columns[n ^ d] for d in range(clip_count)], clip_index)
            for n in range(clip_count)
        ],
        axis=-1,
    )[None]

    sums = jnp.concatenate([jnp.sum(feature_sums, axis=0), penalties])
    sums = collect(sums, ("frames", "mp", "dp"))
    penalties = jnp.sum(sums[:, half:], axis=0)
    penalty = pick([penalties[d : d + 1] for d in range(clip_count)], clip_index) / (
        sigma_noise * sigma_noise * token_total * model_width
    )
    sums = sums[:, :half].reshape(slab_count, model_count, local_width)
    sums = lax.dynamic_index_in_dim(jnp.sum(sums, axis=0), model_index, 0, keepdims=False)
    gain_grad = norm_gain * sums / (sigma_noise * sigma_noise * token_total)
    return (features, penalty, gain_grad)


def solution(mesh):
    placed = (
        P("dp", "frames", None, None, "mp"),
        P("dp", "frames", None, None, "mp"),
        P("frames", "mp"),
        P("mp"),
        P("dp", None),
    )
    return jax.shard_map(
        local,
        mesh=mesh,
        in_specs=placed,
        out_specs=(P("dp", "frames", None, "mp"), P("dp"), P("mp")),
        check_vma=False,
    )
```

```python
import math

import jax
import jax.numpy as jnp
from jax import lax
from jax.experimental import pallas as pl
from jax.experimental.pallas import tpu as pltpu
from jax.sharding import PartitionSpec as P

HEAD_DIM = 128
HEADS_AT_ONCE = 1


sigma_noise = 0.25
epsilon = 1e-06


def perturb(clean, noise):
    return (clean.astype(jnp.float32) + sigma_noise * noise.astype(jnp.float32)).astype(jnp.bfloat16)


def attend_kernel(counts_ref, own_ref, left_ref, right_ref, out_ref):
    slots, _, tile_len, width = own_ref.shape
    key_pos = lax.broadcasted_iota(jnp.int32, (1, 2 * tile_len), 1)
    live = []
    for slot in range(slots):
        own_count = counts_ref[slot + 1]
        far_count = counts_ref[0 if slot == 0 else slots + 1]
        live.append((key_pos < own_count) | ((key_pos >= tile_len) & (key_pos < tile_len + far_count)))
    row_pos = lax.broadcasted_iota(jnp.int32, (tile_len, 1), 0)
    units = [(slot, head) for head in range(width // HEAD_DIM) for slot in range(slots)]

    scores = []
    for slot, head in units:
        cols = pl.ds(head * HEAD_DIM, HEAD_DIM)
        halo_ref = left_ref if slot == 0 else right_ref
        keys = jnp.concatenate([own_ref[slot, 1, :, cols], halo_ref[0, :, cols]], axis=0)
        raw = lax.dot_general(
            own_ref[slot, 0, :, cols],
            keys,
            (((1,), (1,)), ((), ())),
            preferred_element_type=jnp.float32,
        )
        scores.append(jnp.where(live[slot], raw * (1.0 / math.sqrt(HEAD_DIM)), jnp.float32(-1e30)))
    largest = [jnp.max(s, axis=-1, keepdims=True) for s in scores]
    weights = [jnp.exp(s - top) for s, top in zip(scores, largest)]
    totals = [jnp.sum(w, axis=-1, keepdims=True) for w in weights]
    for (slot, head), weight, total in zip(units, weights, totals):
        cols = pl.ds(head * HEAD_DIM, HEAD_DIM)
        halo_ref = left_ref if slot == 0 else right_ref
        values = jnp.concatenate([own_ref[slot, 2, :, cols], halo_ref[1, :, cols]], axis=0)
        probabilities = (weight * (1.0 / total)).astype(jnp.bfloat16)
        mixed = jnp.dot(probabilities, values, preferred_element_type=jnp.float32)
        out_ref[slot, :, cols] = jnp.where(row_pos < counts_ref[slot + 1], mixed, 0.0).astype(
            jnp.bfloat16
        )


def attention(nearby, own, left, right, stream):
    slots, _, tile_len, width = own.shape
    block = HEADS_AT_ONCE * HEAD_DIM
    own_spec = pl.BlockSpec((slots, 3, tile_len, block), lambda h, c: (0, 0, 0, h))
    halo_spec = pl.BlockSpec((None, 2, tile_len, block), lambda h, c: (stream, 0, 0, h))
    return pl.pallas_call(
        attend_kernel,
        grid_spec=pltpu.PrefetchScalarGridSpec(
            num_scalar_prefetch=1,
            grid=(width // block,),
            in_specs=[own_spec, halo_spec, halo_spec],
            out_specs=pl.BlockSpec((slots, tile_len, block), lambda h, c: (0, 0, h)),
        ),
        out_shape=jax.ShapeDtypeStruct((slots, tile_len, width), jnp.bfloat16),
        compiler_params=pltpu.CompilerParams(vmem_limit_bytes=48 * 1024 * 1024),
        cost_estimate=pl.CostEstimate(
            flops=300 * slots * tile_len * tile_len * width,
            bytes_accessed=12 * slots * tile_len * width,
            transcendentals=0,
        ),
        name="attention",
    )(nearby, own, left, right)


def project(places, valid, clip_index, gathered, weights, total):
    stream_count = len(gathered)
    keys = gathered[0][0]
    clip_count = 1 + max(clip for _, clip in keys)
    place_count = 1 + max(place for place, _ in keys)
    _, block_rows, depth = gathered[0][1][0].shape
    columns = sum(part.shape[0] for part in weights[0])
    row_count = stream_count * block_rows
    shard_total = len(weights)
    part_total = sum(len(parts) for parts in weights)
    scalars = jnp.stack([jnp.int32(n) for n in (*places, *valid, clip_index)])
    flat = [stack for _, stacks in gathered for stack in stacks]

    def kernel(scalars_ref, *refs):
        block_refs = refs[: len(flat)]
        weight_refs = refs[len(flat) : len(flat) + part_total]
        total_ref = refs[len(flat) + part_total] if total is not None else None
        out_ref, squares_ref, rows, held, row_sem, weight_sem, total_sem = refs[-7:]

        def weight_copies(shard):
            parts = len(weights[shard])
            for n in range(parts):
                size = columns // parts
                yield pltpu.make_async_copy(
                    weight_refs[shard * parts + n],
                    held.at[shard, pl.ds(n * size, size)],
                    weight_sem.at[shard, n],
                )

        def row_copy(place, shard, clip, stream):
            at = gathered[stream][0].index((place, clip))
            near = gathered[stream][1][0].shape[0]
            source = block_refs[2 * stream + at // near].at[at % near]
            first = pl.multiple_of(
                (clip ^ scalars_ref[2 * shard_total]) * row_count + stream * block_rows, 16
            )
            return pltpu.make_async_copy(
                source,
                rows.at[shard, pl.ds(first, block_rows)],
                row_sem.at[shard, clip, stream],
            )

        for shard in range(shard_total):

            @pl.when(scalars_ref[shard_total + shard] == 1)
            def _():
                for copy in weight_copies(shard):
                    copy.start()
                for place in range(place_count):

                    @pl.when(scalars_ref[shard] == place)
                    def _():
                        for clip in range(clip_count):
                            for stream in range(stream_count):
                                row_copy(place, shard, clip, stream).start()

        if total is not None:
            total_copy = pltpu.make_async_copy(total_ref, out_ref, total_sem)
            total_copy.start()
            total_copy.wait()
        else:
            out_ref[...] = jnp.zeros_like(out_ref)

        for shard in range(shard_total):

            @pl.when(scalars_ref[shard_total + shard] == 1)
            def _():
                for copy in weight_copies(shard):
                    copy.wait()
                for clip in range(clip_count):
                    for stream in range(stream_count):
                        row_copy(0, shard, clip, stream).wait()
                for clip in range(clip_count):
                    out_ref[clip] += lax.dot_general(
                        rows[shard, pl.ds(clip * row_count, row_count)],
                        held[shard],
                        (((1,), (1,)), ((), ())),
                        preferred_element_type=jnp.float32,
                    )

        ones = jnp.ones((8, columns), jnp.float32)
        for clip in range(clip_count):
            squares_ref[clip] = lax.dot_general(
                ones,
                out_ref[clip] * out_ref[clip],
                (((1,), (1,)), ((), ())),
                precision=lax.Precision.HIGHEST,
                preferred_element_type=jnp.float32,
            )

    operands = [*flat, *(part for parts in weights for part in parts)]
    if total is not None:
        operands.append(total)
    in_specs = [pl.BlockSpec(memory_space=pl.ANY) for _ in operands]
    total, squares = pl.pallas_call(
        kernel,
        in_specs=[pl.BlockSpec(memory_space=pltpu.SMEM)] + in_specs,
        out_specs=[pl.BlockSpec(memory_space=pltpu.VMEM)] * 2,
        out_shape=[
            jax.ShapeDtypeStruct((clip_count, row_count, columns), jnp.float32),
            jax.ShapeDtypeStruct((clip_count, 8, row_count), jnp.float32),
        ],
        scratch_shapes=[
            pltpu.VMEM((shard_total, clip_count * row_count, depth), jnp.bfloat16),
            pltpu.VMEM((shard_total, columns, depth), jnp.bfloat16),
            pltpu.SemaphoreType.DMA((shard_total, clip_count, stream_count)),
            pltpu.SemaphoreType.DMA((shard_total, len(weights[0]))),
            pltpu.SemaphoreType.DMA,
        ],
        compiler_params=pltpu.CompilerParams(vmem_limit_bytes=56 * 1024 * 1024),
        cost_estimate=pl.CostEstimate(
            flops=2 * clip_count * row_count * depth * columns * shard_total,
            bytes_accessed=shard_total * depth * (clip_count * row_count + columns) * 2,
            transcendentals=0,
        ),
        name="project",
    )(scalars, *operands)
    return total, squares[:, 0]


def swap(array, axis, distance):
    count = lax.axis_size(axis)
    return lax.ppermute(array, axis, [(i, i ^ distance) for i in range(count)])


def distances(axis):
    count = lax.axis_size(axis)
    return [(axis, 1 << bit) for bit in reversed(range(count.bit_length() - 1))]


def spread(block, order, before_step):
    keys = [(0, 0)]
    held = block[None]
    received = held[:0]
    for step, (axis, distance) in enumerate(order):
        held = jnp.concatenate([held, received]) if received.shape[0] else held
        held = before_step(step, held)
        received = swap(held, axis, distance)
        keys += [(m ^ distance, c) if axis == "mp" else (m, c ^ distance) for m, c in keys]
    return keys, (held, received)


def collect(array, axes):
    copies = jnp.broadcast_to(array[None], (lax.axis_size(axes),) + array.shape)
    return lax.all_to_all(copies, axes, split_axis=0, concat_axis=0, tiled=True)


def pick(options, index):
    return lax.select_n(index, *options) if len(options) > 1 else options[0]


def local(projections, perturbation, out_weight, norm_gain, live_counts):
    tile_len = projections.shape[2]
    local_width = projections.shape[4]
    slots = projections.shape[1]
    slab_count = lax.axis_size("frames")
    slab_index = lax.axis_index("frames")
    model_count = lax.axis_size("mp")
    model_index = lax.axis_index("mp")
    clip_count = lax.axis_size("dp")
    clip_index = lax.axis_index("dp")
    model_width = local_width * model_count
    token_total = slots * slab_count * tile_len
    half = local_width // clip_count
    near_rows = slots * tile_len

    def own_columns(array):
        return pick(
            [array[..., n * half : (n + 1) * half] for n in range(clip_count)], clip_index
        )

    clean = projections[0].transpose(0, 2, 1, 3)
    noise = perturbation[0].transpose(0, 2, 1, 3)
    perturbed = perturb(clean, noise)
    up = [(i, i + 1) for i in range(slab_count - 1)]
    down = [(i + 1, i) for i in range(slab_count - 1)]

    streams = (clean, perturbed)
    tail = jnp.stack([stream[slots - 1, 1:] for stream in streams])
    head = jnp.stack([stream[0, 1:] for stream in streams])
    tail, head, out_weight = lax.optimization_barrier((tail, head, out_weight))
    left = lax.ppermute(tail, "frames", up)
    right = lax.ppermute(head, "frames", down)

    own_weight = own_columns(out_weight).T
    line = slab_count == model_count and slab_count == 4
    last = slab_count - 1
    part = half // 2
    whole = [own_weight[:part], own_weight[part:]]
    near, passed, across = {}, {}, {}

    def send_near(step):
        near[step] = [
            lax.ppermute(whole[step], "frames", up),
            lax.ppermute(whole[step], "frames", down),
        ]

    def send_passed(step):
        passed[step] = [
            lax.ppermute(near[step][0], "frames", up[1:]),
            lax.ppermute(near[step][1], "frames", down[:2]),
        ]

    def send_across(step):
        across[step] = lax.ppermute(whole[step], "frames", [(0, last), (last, 0)])

    def before_attention(stream, value):
        if line and stream == 0:
            send_near(0)
            send_across(0)
            value, near[0] = lax.optimization_barrier((value, near[0]))
            send_passed(0)
        return value

    def before_step(stream, step, value):
        if line and stream == 1 and step == 2:
            value, across[1] = lax.optimization_barrier((value, across[1]))
        if line and stream == 1 and step == 0:
            value, across[0] = lax.optimization_barrier((value, across[0]))
        if line and stream == 0 and step == 1:
            value, passed[0], whole[1] = lax.optimization_barrier((value, passed[0], whole[1]))
            send_near(1)
            send_across(1)
        if line and stream == 0 and step == 2:
            value, near[1] = lax.optimization_barrier((value, near[1]))
            send_passed(1)
        return value

    counts = jnp.pad(live_counts[0], (1, 1))
    nearby = lax.dynamic_slice_in_dim(counts, slots * slab_index, slots + 2)

    gathered = []
    orders = (
        distances("dp") + distances("mp"),
        distances("mp")[:1] + distances("dp") + distances("mp")[1:],
    )
    for n, order in enumerate(orders):
        own = before_attention(n, streams[n])
        attended = attention(nearby, own, left, right, n).reshape(near_rows, local_width)
        gathered.append(
            spread(attended, order, lambda step, value, n=n: before_step(n, step, value))
        )

    if line:
        at_end = (slab_index == 0) | (slab_index == last)
        far = (slab_index + 2) % slab_count
        shards = [
            (whole, slab_index, jnp.int32(1)),
            ([near[n][0] for n in range(2)], jnp.maximum(slab_index - 1, 0), slab_index > 0),
            ([near[n][1] for n in range(2)], jnp.minimum(slab_index + 1, last), slab_index < last),
            ([passed[n][0] for n in range(2)], far, slab_index >= 2),
            ([passed[n][1] for n in range(2)], far, slab_index < 2),
            ([across[n] for n in range(2)], last - slab_index, at_end),
        ]

    def project_shards(some, total):
        return project(
            [place ^ model_index for _, place, _ in some],
            [exists for _, _, exists in some],
            clip_index,
            gathered,
            [weight for weight, _, _ in some],
            total,
        )

    if line:
        total, _ = project_shards(shards[:3], None)
        total, squares = project_shards(shards[3:], total)
    else:
        weight = lax.all_gather(own_weight, "frames", axis=1, tiled=True)
        shards = [
            (
                [lax.dynamic_slice_in_dim(weight, m * local_width, local_width, axis=1)],
                jnp.int32(m),
                jnp.int32(1),
            )
            for m in range(model_count)
        ]
        total, squares = project_shards(shards, None)
    projected = total.reshape(clip_count, 2, slots, tile_len, half)

    squares = jnp.sum(collect(squares, ("mp", "dp")), axis=0)
    squares = squares.reshape(clip_count, 2, slots, tile_len, 1)
    scale = lax.rsqrt(squares / model_width + epsilon)
    gain = own_columns(norm_gain)
    normed = projected * scale
    features = (normed[:, 0] * gain).astype(jnp.bfloat16)
    difference = normed[:, 1] - normed[:, 0]
    feature_sums = jnp.sum(difference * difference, axis=(1, 2))
    penalties = jnp.sum(feature_sums * gain * gain, axis=-1)

    columns = [pick([features[d] for d in range(clip_count)], clip_index)]
    for distance in range(1, clip_count):
        sent = pick([features[d ^ distance] for d in range(clip_count)], clip_index)
        columns.append(swap(sent, "dp", distance))
    features = jnp.concatenate(
        [
            pick([columns[n ^ d] for d in range(clip_count)], clip_index)
            for n in range(clip_count)
        ],
        axis=-1,
    )[None]

    sums = jnp.concatenate([jnp.sum(feature_sums, axis=0), penalties])
    sums = collect(sums, ("frames", "mp", "dp"))
    penalties = jnp.sum(sums[:, half:], axis=0)
    penalty = pick([penalties[d : d + 1] for d in range(clip_count)], clip_index) / (
        sigma_noise * sigma_noise * token_total * model_width
    )
    sums = sums[:, :half].reshape(slab_count, model_count, local_width)
    sums = lax.dynamic_index_in_dim(jnp.sum(sums, axis=0), model_index, 0, keepdims=False)
    gain_grad = norm_gain * sums / (sigma_noise * sigma_noise * token_total)
    return (features, penalty, gain_grad)


def solution(mesh):
    placed = (
        P("dp", "frames", None, None, "mp"),
        P("dp", "frames", None, None, "mp"),
        P("frames", "mp"),
        P("mp"),
        P("dp", None),
    )
    return jax.shard_map(
        local,
        mesh=mesh,
        in_specs=placed,
        out_specs=(P("dp", "frames", None, "mp"), P("dp"), P("mp")),
        check_vma=False,
    )
```

```python
import math

import jax
import jax.numpy as jnp
from jax import lax
from jax.experimental import pallas as pl
from jax.experimental.pallas import tpu as pltpu
from jax.sharding import PartitionSpec as P

HEAD_DIM = 128
HEADS_AT_ONCE = 1
LANES = 128


sigma_noise = 0.25
epsilon = 1e-06


def perturb(clean, noise):
    return (clean.astype(jnp.float32) + sigma_noise * noise.astype(jnp.float32)).astype(jnp.bfloat16)


def attend_kernel(counts_ref, own_ref, left_ref, right_ref, out_ref):
    slots, _, tile_len, width = own_ref.shape
    key_pos = lax.broadcasted_iota(jnp.int32, (1, 2 * tile_len), 1)
    live = []
    for slot in range(slots):
        own_count = counts_ref[slot + 1]
        far_count = counts_ref[0 if slot == 0 else slots + 1]
        live.append((key_pos < own_count) | ((key_pos >= tile_len) & (key_pos < tile_len + far_count)))
    row_pos = lax.broadcasted_iota(jnp.int32, (tile_len, 1), 0)
    units = [(slot, head) for head in range(width // HEAD_DIM) for slot in range(slots)]

    scores = []
    for slot, head in units:
        cols = pl.ds(head * HEAD_DIM, HEAD_DIM)
        halo_ref = left_ref if slot == 0 else right_ref
        keys = jnp.concatenate([own_ref[slot, 1, :, cols], halo_ref[0, :, cols]], axis=0)
        raw = lax.dot_general(
            own_ref[slot, 0, :, cols],
            keys,
            (((1,), (1,)), ((), ())),
            preferred_element_type=jnp.float32,
        )
        scores.append(jnp.where(live[slot], raw * (1.0 / math.sqrt(HEAD_DIM)), jnp.float32(-1e30)))
    largest = [jnp.max(s, axis=-1, keepdims=True) for s in scores]
    weights = [jnp.exp(s - top) for s, top in zip(scores, largest)]
    totals = [jnp.sum(w, axis=-1, keepdims=True) for w in weights]
    for (slot, head), weight, total in zip(units, weights, totals):
        cols = pl.ds(head * HEAD_DIM, HEAD_DIM)
        halo_ref = left_ref if slot == 0 else right_ref
        values = jnp.concatenate([own_ref[slot, 2, :, cols], halo_ref[1, :, cols]], axis=0)
        probabilities = (weight * (1.0 / total)).astype(jnp.bfloat16)
        mixed = jnp.dot(probabilities, values, preferred_element_type=jnp.float32)
        out_ref[slot, :, cols] = jnp.where(row_pos < counts_ref[slot + 1], mixed, 0.0).astype(
            jnp.bfloat16
        )


def attention(nearby, own, left, right, stream):
    slots, _, tile_len, width = own.shape
    block = HEADS_AT_ONCE * HEAD_DIM
    own_spec = pl.BlockSpec((slots, 3, tile_len, block), lambda h, c: (0, 0, 0, h))
    halo_spec = pl.BlockSpec((None, 2, tile_len, block), lambda h, c: (stream, 0, 0, h))
    return pl.pallas_call(
        attend_kernel,
        grid_spec=pltpu.PrefetchScalarGridSpec(
            num_scalar_prefetch=1,
            grid=(width // block,),
            in_specs=[own_spec, halo_spec, halo_spec],
            out_specs=pl.BlockSpec((slots, tile_len, block), lambda h, c: (0, 0, h)),
        ),
        out_shape=jax.ShapeDtypeStruct((slots, tile_len, width), jnp.bfloat16),
        compiler_params=pltpu.CompilerParams(vmem_limit_bytes=48 * 1024 * 1024),
        cost_estimate=pl.CostEstimate(
            flops=0 * slots * tile_len * tile_len * width,
            bytes_accessed=0 * slots * tile_len * width,
            transcendentals=0,
        ),
        name="attention",
    )(nearby, own, left, right)


def whole_lanes(columns):
    return -(-columns // LANES) * LANES


def on_diagonal():
    row = lax.broadcasted_iota(jnp.int32, (LANES, LANES), 0)
    return row == lax.broadcasted_iota(jnp.int32, (LANES, LANES), 1)


def project(places, valid, clip_index, gathered, weights, total, peers):
    stream_count = len(gathered)
    keys = gathered[0][0]
    clip_count = 1 + max(clip for _, clip in keys)
    place_count = 1 + max(place for place, _ in keys)
    _, block_rows, depth = gathered[0][1][0].shape
    columns = sum(part.shape[0] for part in weights[0])
    lanes = whole_lanes(columns)
    row_count = stream_count * block_rows
    shard_total = len(weights)
    part_total = sum(len(parts) for parts in weights)
    scalars = jnp.stack([jnp.int32(n) for n in (*places, *valid, clip_index)])
    flat = [stack for _, stacks in gathered for stack in stacks]

    def kernel(scalars_ref, *refs):
        block_refs = refs[: len(flat)]
        weight_refs = refs[len(flat) : len(flat) + part_total]
        total_ref = refs[len(flat) + part_total] if total is not None else None
        rows, held, row_sem, weight_sem, total_sem = refs[-5:]
        out_ref = refs[len(operands)]
        squares_ref = refs[len(operands) + 1]

        def weight_copies(shard):
            parts = len(weights[shard])
            for n in range(parts):
                size = columns // parts
                yield pltpu.make_async_copy(
                    weight_refs[sum(len(p) for p in weights[:shard]) + n],
                    held.at[shard, pl.ds(n * size, size)],
                    weight_sem.at[shard, n],
                )

        def row_copy(place, shard, clip, stream):
            at = gathered[stream][0].index((place, clip))
            near = gathered[stream][1][0].shape[0]
            source = block_refs[2 * stream + at // near].at[at % near]
            first = pl.multiple_of(
                (clip ^ scalars_ref[2 * shard_total]) * row_count + stream * block_rows, 16
            )
            return pltpu.make_async_copy(
                source,
                rows.at[shard, pl.ds(first, block_rows)],
                row_sem.at[shard, clip, stream],
            )

        if total is not None:
            pltpu.make_async_copy(total_ref, out_ref, total_sem).start()
        for shard in range(shard_total):

            @pl.when(scalars_ref[shard_total + shard] == 1)
            def _():
                for copy in weight_copies(shard):
                    copy.start()
                for place in range(place_count):

                    @pl.when(scalars_ref[shard] == place)
                    def _():
                        for clip in range(clip_count):
                            for stream in range(stream_count):
                                row_copy(place, shard, clip, stream).start()

        if total is not None:
            pltpu.make_async_copy(total_ref, out_ref, total_sem).wait()
        else:
            out_ref[...] = jnp.zeros_like(out_ref)

        for shard in range(shard_total):

            @pl.when(scalars_ref[shard_total + shard] == 1)
            def _():
                for copy in weight_copies(shard):
                    copy.wait()
                for clip in range(clip_count):
                    for stream in range(stream_count):
                        row_copy(0, shard, clip, stream).wait()
                if lanes > columns:
                    held[shard, columns:] = jnp.zeros((lanes - columns, depth), held.dtype)
                for clip in range(clip_count):
                    out_ref[clip] += lax.dot_general(
                        rows[shard, pl.ds(clip * row_count, row_count)],
                        held[shard],
                        (((1,), (1,)), ((), ())),
                        preferred_element_type=jnp.float32,
                    )

        if peers:
            diagonal = on_diagonal()
            for clip in range(clip_count):
                for first in range(0, row_count, LANES):
                    piece = out_ref[clip, pl.ds(first, LANES)]
                    sums = jnp.sum(piece * piece, axis=1, keepdims=True)
                    sums = jnp.sum(jnp.where(diagonal, sums, 0.0), axis=0, keepdims=True)
                    squares_ref[:, pl.ds(clip * row_count + first, LANES)] = jnp.broadcast_to(
                        sums, (peers, LANES)
                    )

    operands = [*flat, *(part for parts in weights for part in parts)]
    if total is not None:
        operands.append(total)
    in_specs = [pl.BlockSpec(memory_space=pl.ANY) for _ in operands]
    out_shape = [jax.ShapeDtypeStruct((clip_count, row_count, lanes), jnp.float32)]
    if peers:
        out_shape.append(jax.ShapeDtypeStruct((peers, clip_count * row_count), jnp.float32))
    return pl.pallas_call(
        kernel,
        in_specs=[pl.BlockSpec(memory_space=pltpu.SMEM)] + in_specs,
        out_specs=[pl.BlockSpec(memory_space=pltpu.VMEM)] * len(out_shape),
        out_shape=out_shape,
        scratch_shapes=[
            pltpu.VMEM((shard_total, clip_count * row_count, depth), jnp.bfloat16),
            pltpu.VMEM((shard_total, lanes, depth), jnp.bfloat16),
            pltpu.SemaphoreType.DMA((shard_total, clip_count, stream_count)),
            pltpu.SemaphoreType.DMA((shard_total, max(len(parts) for parts in weights))),
            pltpu.SemaphoreType.DMA,
        ],
        compiler_params=pltpu.CompilerParams(vmem_limit_bytes=56 * 1024 * 1024),
        cost_estimate=pl.CostEstimate(
            flops=2 * clip_count * row_count * depth * columns * shard_total,
            bytes_accessed=shard_total * depth * (clip_count * row_count + columns) * 2,
            transcendentals=0,
        ),
        name="project",
    )(scalars, *operands)


def finish(total, squares, gain, model_width, devices):
    clip_count, row_count, lanes = total.shape
    columns = gain.shape[0]
    near_rows = row_count // 2
    gain = jnp.pad(gain, (0, lanes - columns))[None]

    def kernel(total_ref, squares_ref, gain_ref, features_ref, row_ref):
        clip = pl.program_id(0)
        diagonal = on_diagonal()
        scales = []
        for first in range(0, row_count, LANES):
            at = pl.ds(pl.multiple_of(clip * row_count + first, LANES), LANES)
            mean = jnp.sum(squares_ref[:, at], axis=0, keepdims=True) / model_width
            scale = jnp.broadcast_to(lax.rsqrt(mean + epsilon), (LANES, LANES))
            scales.append(jnp.sum(jnp.where(diagonal, scale, 0.0), axis=1, keepdims=True))
        scale = jnp.concatenate(scales, axis=0)
        clean = total_ref[0, :near_rows] * scale[:near_rows]
        features_ref[0] = (clean * gain_ref[...]).astype(jnp.bfloat16)
        difference = total_ref[0, near_rows:] * scale[near_rows:] - clean
        sums = jnp.sum(difference * difference, axis=0, keepdims=True)
        penalty = jnp.sum(sums * gain_ref[...] * gain_ref[...], axis=1, keepdims=True)
        lane = lax.broadcasted_iota(jnp.int32, (1, lanes), 1)
        sums = sums + jnp.where(lane == columns + clip, penalty, 0.0)
        sums = jnp.broadcast_to(sums, row_ref.shape)

        @pl.when(clip == 0)
        def _():
            row_ref[...] = sums

        @pl.when(clip > 0)
        def _():
            row_ref[...] += sums

    return pl.pallas_call(
        kernel,
        grid=(clip_count,),
        in_specs=[
            pl.BlockSpec((1, row_count, lanes), lambda c: (c, 0, 0)),
            pl.BlockSpec(squares.shape, lambda c: (0, 0)),
            pl.BlockSpec((1, lanes), lambda c: (0, 0)),
        ],
        out_specs=[
            pl.BlockSpec((1, near_rows, lanes), lambda c: (c, 0, 0)),
            pl.BlockSpec((devices, lanes), lambda c: (0, 0)),
        ],
        out_shape=[
            jax.ShapeDtypeStruct((clip_count, near_rows, lanes), jnp.bfloat16),
            jax.ShapeDtypeStruct((devices, lanes), jnp.float32),
        ],
        compiler_params=pltpu.CompilerParams(vmem_limit_bytes=32 * 1024 * 1024),
        name="finish",
    )(total, squares, gain)


def conclude(rows, gain, model_index, clip_index, model_count, clip_count, tokens, model_width):
    devices, lanes = rows.shape
    columns = gain.shape[0] // clip_count

    def kernel(index_ref, rows_ref, gain_ref, penalty_ref, grad_ref):
        row = lax.broadcasted_iota(jnp.int32, (devices, lanes), 0)
        model = (row // clip_count) % model_count
        sums = []
        for clip in range(clip_count):
            mine = (model == index_ref[0]) & (row % clip_count == clip)
            sums.append(
                jnp.sum(jnp.where(mine, rows_ref[...], 0.0), axis=0, keepdims=True)[:, :columns]
            )
        sums = jnp.concatenate(sums, axis=1)
        grad_ref[...] = gain_ref[...] * sums / (sigma_noise * sigma_noise * tokens)
        lane = lax.broadcasted_iota(jnp.int32, (devices, lanes), 1)
        own = jnp.where(lane == columns + index_ref[1], rows_ref[...], 0.0)
        total = jnp.sum(jnp.sum(own, axis=0, keepdims=True), axis=1, keepdims=True)
        penalty_ref[...] = total / (sigma_noise * sigma_noise * tokens * model_width)

    penalty, grad = pl.pallas_call(
        kernel,
        in_specs=[pl.BlockSpec(memory_space=pltpu.SMEM)]
        + [pl.BlockSpec(memory_space=pltpu.VMEM)] * 2,
        out_specs=[pl.BlockSpec(memory_space=pltpu.VMEM)] * 2,
        out_shape=[
            jax.ShapeDtypeStruct((1, 1), jnp.float32),
            jax.ShapeDtypeStruct((1, gain.shape[0]), jnp.float32),
        ],
        name="conclude",
    )(jnp.stack([model_index, clip_index]).astype(jnp.int32), rows, gain[None])
    return penalty[0], grad[0]


def swap(array, axis, distance):
    count = lax.axis_size(axis)
    return lax.ppermute(array, axis, [(i, i ^ distance) for i in range(count)])


def distances(axis):
    count = lax.axis_size(axis)
    return [(axis, 1 << bit) for bit in reversed(range(count.bit_length() - 1))]


def spread(block, order, before_step):
    keys = [(0, 0)]
    held = block[None]
    received = held[:0]
    for step, (axis, distance) in enumerate(order):
        held = jnp.concatenate([held, received]) if received.shape[0] else held
        held = before_step(step, held)
        received = swap(held, axis, distance)
        keys += [(m ^ distance, c) if axis == "mp" else (m, c ^ distance) for m, c in keys]
    return keys, (held, received)


def collect(rows, axes):
    return lax.all_to_all(rows, axes, split_axis=0, concat_axis=0, tiled=True)


def pick(options, index):
    return lax.select_n(index, *options) if len(options) > 1 else options[0]


def local(projections, perturbation, out_weight, norm_gain, live_counts):
    tile_len = projections.shape[2]
    local_width = projections.shape[4]
    slots = projections.shape[1]
    slab_count = lax.axis_size("frames")
    slab_index = lax.axis_index("frames")
    model_count = lax.axis_size("mp")
    model_index = lax.axis_index("mp")
    clip_count = lax.axis_size("dp")
    clip_index = lax.axis_index("dp")
    model_width = local_width * model_count
    token_total = slots * slab_count * tile_len
    half = local_width // clip_count
    near_rows = slots * tile_len

    def own_columns(array):
        return pick(
            [array[..., n * half : (n + 1) * half] for n in range(clip_count)], clip_index
        )

    clean = projections[0].transpose(0, 2, 1, 3)
    noise = perturbation[0].transpose(0, 2, 1, 3)
    perturbed = perturb(clean, noise)
    up = [(i, i + 1) for i in range(slab_count - 1)]
    down = [(i + 1, i) for i in range(slab_count - 1)]

    streams = (clean, perturbed)
    tail = jnp.stack([stream[slots - 1, 1:] for stream in streams])
    head = jnp.stack([stream[0, 1:] for stream in streams])
    tail, head, out_weight = lax.optimization_barrier((tail, head, out_weight))
    left = lax.ppermute(tail, "frames", up)
    right = lax.ppermute(head, "frames", down)

    own_weight = own_columns(out_weight).T
    line = slab_count == model_count and slab_count == 4
    last = slab_count - 1
    part = half // 2
    near, passed, across = [], [], []

    if line:
        near = [lax.ppermute(own_weight, "frames", up), lax.ppermute(own_weight, "frames", down)]

    def before_step(stream, step, value):
        nonlocal near, passed, across
        if line and stream == 0 and step == 1:
            value, near = lax.optimization_barrier((value, near))
            passed = [
                lax.ppermute(near[0], "frames", up[1:]),
                lax.ppermute(near[1], "frames", down[:2]),
            ]
            across = [
                lax.ppermute(block, "frames", [(0, last), (last, 0)])
                for block in (own_weight[:part], own_weight[part:])
            ]
        if line and stream == 1 and step == 2:
            value, passed, across[0] = lax.optimization_barrier((value, passed, across[0]))
        return value

    counts = jnp.pad(live_counts[0], (1, 1))
    nearby = lax.dynamic_slice_in_dim(counts, slots * slab_index, slots + 2)

    gathered = []
    orders = (
        distances("dp") + distances("mp"),
        distances("mp")[:1] + distances("dp") + distances("mp")[1:],
    )
    for n, order in enumerate(orders):
        attended = attention(nearby, streams[n], left, right, n).reshape(near_rows, local_width)
        gathered.append(
            spread(attended, order, lambda step, value, n=n: before_step(n, step, value))
        )

    if line:
        at_end = (slab_index == 0) | (slab_index == last)
        far = (slab_index + 2) % slab_count
        shards = [
            ([own_weight], slab_index, jnp.int32(1)),
            ([near[0]], jnp.maximum(slab_index - 1, 0), slab_index > 0),
            ([near[1]], jnp.minimum(slab_index + 1, last), slab_index < last),
            ([passed[0]], far, slab_index >= 2),
            ([passed[1]], far, slab_index < 2),
            (across, last - slab_index, at_end),
        ]

    peers = model_count * clip_count

    def project_shards(some, total, peers):
        return project(
            [place ^ model_index for _, place, _ in some],
            [exists for _, _, exists in some],
            clip_index,
            gathered,
            [weight for weight, _, _ in some],
            total,
            peers,
        )

    if line:
        (total,) = project_shards(shards[:5], None, 0)
        total, squares = project_shards(shards[5:], total, peers)
    else:
        weight = lax.all_gather(own_weight, "frames", axis=1, tiled=True)
        shards = [
            (
                [lax.dynamic_slice_in_dim(weight, m * local_width, local_width, axis=1)],
                jnp.int32(m),
                jnp.int32(1),
            )
            for m in range(model_count)
        ]
        total, squares = project_shards(shards, None, peers)

    squares = collect(squares, ("mp", "dp"))
    features, sums = finish(
        total, squares, own_columns(norm_gain), model_width, slab_count * model_count * clip_count
    )
    sums = collect(sums, ("frames", "mp", "dp"))

    features = features[..., :half].reshape(clip_count, slots, tile_len, half)
    columns = [pick([features[d] for d in range(clip_count)], clip_index)]
    for distance in range(1, clip_count):
        sent = pick([features[d ^ distance] for d in range(clip_count)], clip_index)
        columns.append(swap(sent, "dp", distance))
    features = jnp.concatenate(
        [
            pick([columns[n ^ d] for d in range(clip_count)], clip_index)
            for n in range(clip_count)
        ],
        axis=-1,
    )[None]
    sums, features = lax.optimization_barrier((sums, features))
    penalty, gain_grad = conclude(
        sums,
        norm_gain,
        model_index,
        clip_index,
        model_count,
        clip_count,
        token_total,
        model_width,
    )
    return (features, penalty, gain_grad)


def solution(mesh):
    placed = (
        P("dp", "frames", None, None, "mp"),
        P("dp", "frames", None, None, "mp"),
        P("frames", "mp"),
        P("mp"),
        P("dp", None),
    )
    return jax.shard_map(
        local,
        mesh=mesh,
        in_specs=placed,
        out_specs=(P("dp", "frames", None, "mp"), P("dp"), P("mp")),
        check_vma=False,
    )
```

```python
import math

import jax
import jax.numpy as jnp
from jax import lax
from jax.experimental import pallas as pl
from jax.experimental.pallas import tpu as pltpu
from jax.sharding import PartitionSpec as P

HEAD_DIM = 128
HEADS_AT_ONCE = 1
LANES = 128


sigma_noise = 0.25
epsilon = 1e-06


def perturb(clean, noise):
    return (clean.astype(jnp.float32) + sigma_noise * noise.astype(jnp.float32)).astype(jnp.bfloat16)


def attend_kernel(counts_ref, own_ref, left_ref, right_ref, out_ref):
    slots, _, tile_len, width = own_ref.shape
    key_pos = lax.broadcasted_iota(jnp.int32, (1, 2 * tile_len), 1)
    live = []
    for slot in range(slots):
        own_count = counts_ref[slot + 1]
        far_count = counts_ref[0 if slot == 0 else slots + 1]
        live.append((key_pos < own_count) | ((key_pos >= tile_len) & (key_pos < tile_len + far_count)))
    row_pos = lax.broadcasted_iota(jnp.int32, (tile_len, 1), 0)
    units = [(slot, head) for head in range(width // HEAD_DIM) for slot in range(slots)]

    scores = []
    for slot, head in units:
        cols = pl.ds(head * HEAD_DIM, HEAD_DIM)
        halo_ref = left_ref if slot == 0 else right_ref
        keys = jnp.concatenate([own_ref[slot, 1, :, cols], halo_ref[0, :, cols]], axis=0)
        raw = lax.dot_general(
            own_ref[slot, 0, :, cols],
            keys,
            (((1,), (1,)), ((), ())),
            preferred_element_type=jnp.float32,
        )
        scores.append(jnp.where(live[slot], raw * (1.0 / math.sqrt(HEAD_DIM)), jnp.float32(-1e30)))
    largest = [jnp.max(s, axis=-1, keepdims=True) for s in scores]
    weights = [jnp.exp(s - top) for s, top in zip(scores, largest)]
    totals = [jnp.sum(w, axis=-1, keepdims=True) for w in weights]
    for (slot, head), weight, total in zip(units, weights, totals):
        cols = pl.ds(head * HEAD_DIM, HEAD_DIM)
        halo_ref = left_ref if slot == 0 else right_ref
        values = jnp.concatenate([own_ref[slot, 2, :, cols], halo_ref[1, :, cols]], axis=0)
        probabilities = (weight * (1.0 / total)).astype(jnp.bfloat16)
        mixed = jnp.dot(probabilities, values, preferred_element_type=jnp.float32)
        out_ref[slot, :, cols] = jnp.where(row_pos < counts_ref[slot + 1], mixed, 0.0).astype(
            jnp.bfloat16
        )


def attention(nearby, own, left, right, stream):
    slots, _, tile_len, width = own.shape
    block = HEADS_AT_ONCE * HEAD_DIM
    own_spec = pl.BlockSpec((slots, 3, tile_len, block), lambda h, c: (0, 0, 0, h))
    halo_spec = pl.BlockSpec((None, 2, tile_len, block), lambda h, c: (stream, 0, 0, h))
    return pl.pallas_call(
        attend_kernel,
        grid_spec=pltpu.PrefetchScalarGridSpec(
            num_scalar_prefetch=1,
            grid=(width // block,),
            in_specs=[own_spec, halo_spec, halo_spec],
            out_specs=pl.BlockSpec((slots, tile_len, block), lambda h, c: (0, 0, h)),
        ),
        out_shape=jax.ShapeDtypeStruct((slots, tile_len, width), jnp.bfloat16),
        compiler_params=pltpu.CompilerParams(vmem_limit_bytes=48 * 1024 * 1024),
        cost_estimate=pl.CostEstimate(
            flops=0 * slots * tile_len * tile_len * width,
            bytes_accessed=0 * slots * tile_len * width,
            transcendentals=0,
        ),
        name="attention",
    )(nearby, own, left, right)


def whole_lanes(columns):
    return -(-columns // LANES) * LANES


def on_diagonal():
    row = lax.broadcasted_iota(jnp.int32, (LANES, LANES), 0)
    return row == lax.broadcasted_iota(jnp.int32, (LANES, LANES), 1)


def project(places, valid, clip_index, gathered, weights, total, columns, peers):
    stream_count = len(gathered)
    home = [
        {key: (n, at) for n, (keys, _) in enumerate(stacks) for at, key in enumerate(keys)}
        for stacks in gathered
    ]
    clip_count = 1 + max(clip for _, clip in home[0])
    place_count = 1 + max(place for place, _ in home[0])
    _, block_rows, depth = gathered[0][0][1].shape
    lanes = whole_lanes(columns)
    row_count = stream_count * block_rows
    shard_total = len(weights)
    scalars = jnp.stack([jnp.int32(n) for n in (*places, *valid, clip_index)]).astype(jnp.int32)
    flat = [array for stacks in gathered for _, array in stacks]
    base = [sum(len(stacks) for stacks in gathered[:n]) for n in range(stream_count)]

    def kernel(scalars_ref, *refs):
        block_refs = refs[: len(flat)]
        weight_refs = refs[len(flat) : len(flat) + shard_total]
        total_ref = refs[len(flat) + shard_total] if total is not None else None
        rows, held, row_sem, weight_sem, total_sem = refs[-5:]
        out_ref = refs[len(operands)]
        squares_ref = refs[len(operands) + 1]

        def weight_copy(shard):
            size = weights[shard][1].shape[0]
            return pltpu.make_async_copy(
                weight_refs[shard], held.at[shard, pl.ds(0, size)], weight_sem.at[shard]
            )

        def row_copy(place, shard, clip, stream):
            stack, at = home[stream][place, clip]
            source = block_refs[base[stream] + stack].at[at]
            first = pl.multiple_of(
                (clip ^ scalars_ref[2 * shard_total]) * row_count + stream * block_rows, 16
            )
            return pltpu.make_async_copy(
                source,
                rows.at[shard, pl.ds(first, block_rows)],
                row_sem.at[shard, clip, stream],
            )

        if total is not None:
            pltpu.make_async_copy(total_ref, out_ref, total_sem).start()
        for shard in range(shard_total):

            @pl.when(scalars_ref[shard_total + shard] == 1)
            def _():
                weight_copy(shard).start()
                for place in range(place_count):

                    @pl.when(scalars_ref[shard] == place)
                    def _():
                        for clip in range(clip_count):
                            for stream in range(stream_count):
                                row_copy(place, shard, clip, stream).start()

        if total is not None:
            pltpu.make_async_copy(total_ref, out_ref, total_sem).wait()
        else:
            out_ref[...] = jnp.zeros_like(out_ref)

        for shard in range(shard_total):

            @pl.when(scalars_ref[shard_total + shard] == 1)
            def _():
                weight_copy(shard).wait()
                for clip in range(clip_count):
                    for stream in range(stream_count):
                        row_copy(0, shard, clip, stream).wait()
                first, array = weights[shard]
                size = array.shape[0]
                wide = whole_lanes(size)
                if wide > size:
                    held[shard, size:wide] = jnp.zeros((wide - size, depth), held.dtype)
                for clip in range(clip_count):
                    out_ref[clip, :, pl.ds(first, wide)] += lax.dot_general(
                        rows[shard, pl.ds(clip * row_count, row_count)],
                        held[shard, pl.ds(0, wide)],
                        (((1,), (1,)), ((), ())),
                        preferred_element_type=jnp.float32,
                    )

        if peers:
            diagonal = on_diagonal()
            for clip in range(clip_count):
                for first in range(0, row_count, LANES):
                    piece = out_ref[clip, pl.ds(first, LANES)]
                    sums = jnp.sum(piece * piece, axis=1, keepdims=True)
                    sums = jnp.sum(jnp.where(diagonal, sums, 0.0), axis=0, keepdims=True)
                    squares_ref[:, :, pl.ds(clip * row_count + first, LANES)] = jnp.broadcast_to(
                        sums[None], (peers, 1, LANES)
                    )

    operands = [*flat, *(array for _, array in weights)]
    if total is not None:
        operands.append(total)
    in_specs = [pl.BlockSpec(memory_space=pl.ANY) for _ in operands]
    out_shape = [jax.ShapeDtypeStruct((clip_count, row_count, lanes), jnp.float32)]
    if peers:
        out_shape.append(jax.ShapeDtypeStruct((peers, 1, clip_count * row_count), jnp.float32))
    return pl.pallas_call(
        kernel,
        in_specs=[pl.BlockSpec(memory_space=pltpu.SMEM)] + in_specs,
        out_specs=[pl.BlockSpec(memory_space=pltpu.VMEM)] * len(out_shape),
        out_shape=out_shape,
        scratch_shapes=[
            pltpu.VMEM((shard_total, clip_count * row_count, depth), jnp.bfloat16),
            pltpu.VMEM((shard_total, lanes, depth), jnp.bfloat16),
            pltpu.SemaphoreType.DMA((shard_total, clip_count, stream_count)),
            pltpu.SemaphoreType.DMA((shard_total,)),
            pltpu.SemaphoreType.DMA,
        ],
        compiler_params=pltpu.CompilerParams(vmem_limit_bytes=56 * 1024 * 1024),
        cost_estimate=pl.CostEstimate(
            flops=2 * clip_count * row_count * depth * columns * shard_total,
            bytes_accessed=shard_total * depth * (clip_count * row_count + columns) * 2,
            transcendentals=0,
        ),
        name="project",
    )(scalars, *operands)


def finish(total, squares, gain, model_width, devices):
    clip_count, row_count, lanes = total.shape
    columns = gain.shape[0]
    near_rows = row_count // 2
    gain = jnp.pad(gain, (0, lanes - columns))[None]

    def kernel(total_ref, squares_ref, gain_ref, features_ref, row_ref):
        clip = pl.program_id(0)
        diagonal = on_diagonal()
        scales = []
        for first in range(0, row_count, LANES):
            at = pl.ds(pl.multiple_of(clip * row_count + first, LANES), LANES)
            mean = jnp.sum(squares_ref[:, :, at], axis=0) / model_width
            scale = jnp.broadcast_to(lax.rsqrt(mean + epsilon), (LANES, LANES))
            scales.append(jnp.sum(jnp.where(diagonal, scale, 0.0), axis=1, keepdims=True))
        scale = jnp.concatenate(scales, axis=0)
        clean = total_ref[0, :near_rows] * scale[:near_rows]
        features_ref[0] = (clean * gain_ref[...]).astype(jnp.bfloat16)
        difference = total_ref[0, near_rows:] * scale[near_rows:] - clean
        sums = jnp.sum(difference * difference, axis=0, keepdims=True)
        penalty = jnp.sum(sums * gain_ref[...] * gain_ref[...], axis=1, keepdims=True)
        lane = lax.broadcasted_iota(jnp.int32, (1, lanes), 1)
        sums = sums + jnp.where(lane == columns + clip, penalty, 0.0)
        sums = jnp.broadcast_to(sums[None], row_ref.shape)

        @pl.when(clip == 0)
        def _():
            row_ref[...] = sums

        @pl.when(clip > 0)
        def _():
            row_ref[...] += sums

    return pl.pallas_call(
        kernel,
        grid=(clip_count,),
        in_specs=[
            pl.BlockSpec((1, row_count, lanes), lambda c: (c, 0, 0)),
            pl.BlockSpec(squares.shape, lambda c: (0, 0, 0)),
            pl.BlockSpec((1, lanes), lambda c: (0, 0)),
        ],
        out_specs=[
            pl.BlockSpec((1, near_rows, lanes), lambda c: (c, 0, 0)),
            pl.BlockSpec((devices, 1, lanes), lambda c: (0, 0, 0)),
        ],
        out_shape=[
            jax.ShapeDtypeStruct((clip_count, near_rows, lanes), jnp.bfloat16),
            jax.ShapeDtypeStruct((devices, 1, lanes), jnp.float32),
        ],
        compiler_params=pltpu.CompilerParams(vmem_limit_bytes=32 * 1024 * 1024),
        name="finish",
    )(total, squares, gain)


def conclude(rows, gain, model_index, clip_index, model_count, clip_count, tokens, model_width):
    devices, _, lanes = rows.shape
    columns = gain.shape[0] // clip_count

    def kernel(index_ref, rows_ref, gain_ref, penalty_ref, grad_ref):
        row = lax.broadcasted_iota(jnp.int32, (devices, 1, lanes), 0)
        model = (row // clip_count) % model_count
        sums = []
        for clip in range(clip_count):
            mine = (model == index_ref[0]) & (row % clip_count == clip)
            sums.append(
                jnp.sum(jnp.where(mine, rows_ref[...], 0.0), axis=0)[:, :columns]
            )
        sums = jnp.concatenate(sums, axis=1)
        grad_ref[...] = gain_ref[...] * sums / (sigma_noise * sigma_noise * tokens)
        lane = lax.broadcasted_iota(jnp.int32, (devices, 1, lanes), 2)
        own = jnp.where(lane == columns + index_ref[1], rows_ref[...], 0.0)
        total = jnp.sum(jnp.sum(own, axis=0), axis=1, keepdims=True)
        penalty_ref[...] = total / (sigma_noise * sigma_noise * tokens * model_width)

    penalty, grad = pl.pallas_call(
        kernel,
        in_specs=[pl.BlockSpec(memory_space=pltpu.SMEM)]
        + [pl.BlockSpec(memory_space=pltpu.VMEM)] * 2,
        out_specs=[pl.BlockSpec(memory_space=pltpu.VMEM)] * 2,
        out_shape=[
            jax.ShapeDtypeStruct((1, 1), jnp.float32),
            jax.ShapeDtypeStruct((1, gain.shape[0]), jnp.float32),
        ],
        name="conclude",
    )(jnp.stack([model_index, clip_index]).astype(jnp.int32), rows, gain[None])
    return penalty.reshape(1), grad.reshape(-1)


def swap(array, axis, distance):
    count = lax.axis_size(axis)
    return lax.ppermute(array, axis, [(i, i ^ distance) for i in range(count)])


def distances(axis):
    count = lax.axis_size(axis)
    return [(axis, 1 << bit) for bit in reversed(range(count.bit_length() - 1))]


def spread(block, order, before_step):
    stacks = [([(0, 0)], block[None])]
    for step, (axis, distance) in enumerate(order):
        if step < len(order) - 1 and len(stacks) > 1:
            keys = [key for some, _ in stacks for key in some]
            stacks = [(keys, jnp.concatenate([array for _, array in stacks]))]
        received = []
        for part, (keys, array) in enumerate(stacks):
            keys = [(m ^ distance, c) if axis == "mp" else (m, c ^ distance) for m, c in keys]
            received.append((keys, swap(before_step(step, part, array), axis, distance)))
        stacks = stacks + received
    return stacks


def collect(rows, axes):
    return lax.all_to_all(rows, axes, split_axis=0, concat_axis=0, tiled=True)


def pick(options, index):
    return lax.select_n(index, *options) if len(options) > 1 else options[0]


def local(projections, perturbation, out_weight, norm_gain, live_counts):
    tile_len = projections.shape[2]
    local_width = projections.shape[4]
    slots = projections.shape[1]
    slab_count = lax.axis_size("frames")
    slab_index = lax.axis_index("frames")
    model_count = lax.axis_size("mp")
    model_index = lax.axis_index("mp")
    clip_count = lax.axis_size("dp")
    clip_index = lax.axis_index("dp")
    model_width = local_width * model_count
    token_total = slots * slab_count * tile_len
    half = local_width // clip_count
    near_rows = slots * tile_len

    def own_columns(array):
        return pick(
            [array[..., n * half : (n + 1) * half] for n in range(clip_count)], clip_index
        )

    clean = projections[0].transpose(0, 2, 1, 3)
    noise = perturbation[0].transpose(0, 2, 1, 3)
    up = [(i, i + 1) for i in range(slab_count - 1)]
    down = [(i + 1, i) for i in range(slab_count - 1)]

    def keys_and_values(slot):
        keep = clean[slot, 1:]
        return jnp.stack([keep, perturb(keep, noise[slot, 1:])])

    tail, head = keys_and_values(slots - 1), keys_and_values(0)
    tail, head, clean, noise, out_weight = lax.optimization_barrier(
        (tail, head, clean, noise, out_weight)
    )
    streams = (clean, perturb(clean, noise))
    left = lax.ppermute(tail, "frames", up)
    right = lax.ppermute(head, "frames", down)

    own_weight = own_columns(out_weight).T
    line = slab_count == model_count and slab_count == 4
    last = slab_count - 1
    cut = whole_lanes(half) // 2
    near, passed, across = [], [], []

    if line:
        near = [lax.ppermute(own_weight, "frames", up), lax.ppermute(own_weight, "frames", down)]
        across = [
            lax.ppermute(block, "frames", [(0, last), (last, 0)])
            for block in (own_weight[:cut], own_weight[cut:])
        ]

    def before_step(stream, step, part, value):
        nonlocal near, passed
        if line and stream == 0 and step == 1:
            value, near = lax.optimization_barrier((value, near))
            passed = [
                lax.ppermute(near[0], "frames", up[1:]),
                lax.ppermute(near[1], "frames", down[:2]),
            ]
        if line and stream == 1 and step == 1:
            value, across[0] = lax.optimization_barrier((value, across[0]))
        if line and stream == 1 and step == 2 and part == 1:
            value, passed = lax.optimization_barrier((value, passed))
        return value

    counts = jnp.pad(live_counts[0], (1, 1))
    nearby = lax.dynamic_slice_in_dim(counts, slots * slab_index, slots + 2)

    gathered = []
    orders = (
        distances("dp") + distances("mp"),
        distances("mp")[:1] + distances("dp") + distances("mp")[1:],
    )
    for n, order in enumerate(orders):
        attended = attention(nearby, streams[n], left, right, n).reshape(near_rows, local_width)
        gathered.append(
            spread(attended, order, lambda *at, n=n: before_step(n, *at))
        )

    if line:
        at_end = (slab_index == 0) | (slab_index == last)
        far = (slab_index + 2) % slab_count
        shards = [
            (0, own_weight, slab_index, jnp.int32(1)),
            (0, near[0], jnp.maximum(slab_index - 1, 0), slab_index > 0),
            (0, near[1], jnp.minimum(slab_index + 1, last), slab_index < last),
            (0, passed[0], far, slab_index >= 2),
            (0, passed[1], far, slab_index < 2),
            (0, across[0], last - slab_index, at_end),
            (cut, across[1], last - slab_index, at_end),
        ]

    peers = model_count * clip_count

    def project_shards(some, total, peers):
        return project(
            [place ^ model_index for _, _, place, _ in some],
            [exists for _, _, _, exists in some],
            clip_index,
            gathered,
            [(first, weight) for first, weight, _, _ in some],
            total,
            half,
            peers,
        )

    if line:
        (total,) = project_shards(shards[:-1], None, 0)
        total, squares = project_shards(shards[-1:], total, peers)
    else:
        weight = lax.all_gather(own_weight, "frames", axis=1, tiled=True)
        shards = [
            (
                0,
                lax.dynamic_slice_in_dim(weight, m * local_width, local_width, axis=1),
                jnp.int32(m),
                jnp.int32(1),
            )
            for m in range(model_count)
        ]
        total, squares = project_shards(shards, None, peers)

    squares = collect(squares, ("mp", "dp"))
    features, sums = finish(
        total, squares, own_columns(norm_gain), model_width, slab_count * model_count * clip_count
    )
    sums = collect(sums, ("frames", "mp", "dp"))

    features = features[..., :half].reshape(clip_count, slots, tile_len, half)
    columns = [pick([features[d] for d in range(clip_count)], clip_index)]
    for distance in range(1, clip_count):
        sent = pick([features[d ^ distance] for d in range(clip_count)], clip_index)
        columns.append(swap(sent, "dp", distance))
    features = jnp.concatenate(
        [
            pick([columns[n ^ d] for d in range(clip_count)], clip_index)
            for n in range(clip_count)
        ],
        axis=-1,
    )[None]
    sums, features = lax.optimization_barrier((sums, features))
    penalty, gain_grad = conclude(
        sums,
        norm_gain,
        model_index,
        clip_index,
        model_count,
        clip_count,
        token_total,
        model_width,
    )
    return (features, penalty, gain_grad)


def solution(mesh):
    placed = (
        P("dp", "frames", None, None, "mp"),
        P("dp", "frames", None, None, "mp"),
        P("frames", "mp"),
        P("mp"),
        P("dp", None),
    )
    return jax.shard_map(
        local,
        mesh=mesh,
        in_specs=placed,
        out_specs=(P("dp", "frames", None, "mp"), P("dp"), P("mp")),
        check_vma=False,
    )
```

```python
import math

import jax
import jax.numpy as jnp
from jax import lax
from jax.experimental import pallas as pl
from jax.experimental.pallas import tpu as pltpu
from jax.sharding import PartitionSpec as P

HEAD_DIM = 128
HEADS_AT_ONCE = 1
LANES = 128


sigma_noise = 0.25
epsilon = 1e-06


def perturb(clean, noise):
    return (clean.astype(jnp.float32) + sigma_noise * noise.astype(jnp.float32)).astype(jnp.bfloat16)


def attend_kernel(where_ref, own_ref, left_ref, right_ref, out_ref):
    slots, _, tile_len, width = own_ref.shape
    key_pos = lax.broadcasted_iota(jnp.int32, (1, 2 * tile_len), 1)
    live = []
    for slot in range(slots):
        own_count = where_ref[4 + slot]
        far_count = where_ref[3 if slot == 0 else slots + 4]
        live.append((key_pos < own_count) | ((key_pos >= tile_len) & (key_pos < tile_len + far_count)))
    row_pos = lax.broadcasted_iota(jnp.int32, (tile_len, 1), 0)
    units = [(slot, head) for head in range(width // HEAD_DIM) for slot in range(slots)]

    scores = []
    for slot, head in units:
        cols = pl.ds(head * HEAD_DIM, HEAD_DIM)
        halo_ref = left_ref if slot == 0 else right_ref
        keys = jnp.concatenate([own_ref[slot, 1, :, cols], halo_ref[0, :, cols]], axis=0)
        raw = lax.dot_general(
            own_ref[slot, 0, :, cols],
            keys,
            (((1,), (1,)), ((), ())),
            preferred_element_type=jnp.float32,
        )
        scores.append(jnp.where(live[slot], raw * (1.0 / math.sqrt(HEAD_DIM)), jnp.float32(-1e30)))
    largest = [jnp.max(s, axis=-1, keepdims=True) for s in scores]
    weights = [jnp.exp(s - top) for s, top in zip(scores, largest)]
    totals = [jnp.sum(w, axis=-1, keepdims=True) for w in weights]
    for (slot, head), weight, total in zip(units, weights, totals):
        cols = pl.ds(head * HEAD_DIM, HEAD_DIM)
        halo_ref = left_ref if slot == 0 else right_ref
        values = jnp.concatenate([own_ref[slot, 2, :, cols], halo_ref[1, :, cols]], axis=0)
        probabilities = (weight * (1.0 / total)).astype(jnp.bfloat16)
        mixed = jnp.dot(probabilities, values, preferred_element_type=jnp.float32)
        out_ref[slot, :, cols] = jnp.where(row_pos < where_ref[4 + slot], mixed, 0.0).astype(
            jnp.bfloat16
        )


def attention(where, own, left, right):
    slots, _, tile_len, width = own.shape
    block = HEADS_AT_ONCE * HEAD_DIM
    own_spec = pl.BlockSpec((slots, 3, tile_len, block), lambda h, c: (0, 0, 0, h))
    halo_spec = pl.BlockSpec((2, tile_len, block), lambda h, c: (0, 0, h))
    return pl.pallas_call(
        attend_kernel,
        grid_spec=pltpu.PrefetchScalarGridSpec(
            num_scalar_prefetch=1,
            grid=(width // block,),
            in_specs=[own_spec, halo_spec, halo_spec],
            out_specs=pl.BlockSpec((slots, tile_len, block), lambda h, c: (0, 0, h)),
        ),
        out_shape=jax.ShapeDtypeStruct((slots, tile_len, width), jnp.bfloat16),
        compiler_params=pltpu.CompilerParams(vmem_limit_bytes=48 * 1024 * 1024),
        cost_estimate=pl.CostEstimate(
            flops=0 * slots * tile_len * tile_len * width,
            bytes_accessed=0 * slots * tile_len * width,
            transcendentals=0,
        ),
        name="attention",
    )(where, own, left, right)


def whole_lanes(columns):
    return -(-columns // LANES) * LANES


def on_diagonal():
    row = lax.broadcasted_iota(jnp.int32, (LANES, LANES), 0)
    return row == lax.broadcasted_iota(jnp.int32, (LANES, LANES), 1)


def project(where, gathered, shards, total, columns, peers):
    stream_count = len(gathered)
    home = [
        {key: (n, at) for n, (keys, _) in enumerate(stacks) for at, key in enumerate(keys)}
        for stacks in gathered
    ]
    clip_count = 1 + max(clip for _, clip in home[0])
    place_count = 1 + max(place for place, _ in home[0])
    _, block_rows, depth = gathered[0][0][1].shape
    lanes = whole_lanes(columns)
    row_count = stream_count * block_rows
    shard_total = len(shards)
    flat = [array for stacks in gathered for _, array in stacks]
    base = [sum(len(stacks) for stacks in gathered[:n]) for n in range(stream_count)]

    def kernel(where_ref, *refs):
        slab, model, own_clip = where_ref[0], where_ref[1], where_ref[2]
        block_refs = refs[: len(flat)]
        weight_refs = refs[len(flat) : len(flat) + shard_total]
        total_ref = refs[len(flat) + shard_total] if total is not None else None
        rows, held, row_sem, weight_sem = refs[-4:]
        out_ref = refs[len(operands)]
        squares_ref = refs[len(operands) + 1]

        def weight_copy(shard):
            size = shards[shard][1].shape[0]
            return pltpu.make_async_copy(
                weight_refs[shard], held.at[shard, pl.ds(0, size)], weight_sem.at[shard]
            )

        def row_copy(place, shard, clip, stream):
            stack, at = home[stream][place, clip]
            source = block_refs[base[stream] + stack].at[at]
            first = pl.multiple_of(
                (clip ^ own_clip) * row_count + stream * block_rows, 16
            )
            return pltpu.make_async_copy(
                source,
                rows.at[shard, pl.ds(first, block_rows)],
                row_sem.at[shard, clip, stream],
            )

        for shard in range(shard_total):

            @pl.when(shards[shard][3](slab))
            def _():
                weight_copy(shard).start()
                for place in range(place_count):

                    @pl.when((shards[shard][2](slab) ^ model) == place)
                    def _():
                        for clip in range(clip_count):
                            for stream in range(stream_count):
                                row_copy(place, shard, clip, stream).start()

        if total is None:
            out_ref[...] = jnp.zeros_like(out_ref)
        else:
            out_ref[...] = total_ref[...]

        for shard in range(shard_total):

            @pl.when(shards[shard][3](slab))
            def _():
                weight_copy(shard).wait()
                for clip in range(clip_count):
                    for stream in range(stream_count):
                        row_copy(0, shard, clip, stream).wait()
                first, array = shards[shard][:2]
                size = array.shape[0]
                wide = whole_lanes(size)
                if wide > size:
                    held[shard, size:wide] = jnp.zeros((wide - size, depth), held.dtype)
                for clip in range(clip_count):
                    out_ref[clip, :, pl.ds(first, wide)] += lax.dot_general(
                        rows[shard, pl.ds(clip * row_count, row_count)],
                        held[shard, pl.ds(0, wide)],
                        (((1,), (1,)), ((), ())),
                        preferred_element_type=jnp.float32,
                    )

        if peers:
            diagonal = on_diagonal()
            for clip in range(clip_count):
                for first in range(0, row_count, LANES):
                    piece = out_ref[clip, pl.ds(first, LANES)]
                    sums = jnp.sum(piece * piece, axis=1, keepdims=True)
                    sums = jnp.sum(jnp.where(diagonal, sums, 0.0), axis=0, keepdims=True)
                    squares_ref[:, :, pl.ds(clip * row_count + first, LANES)] = jnp.broadcast_to(
                        sums[None], (peers, 1, LANES)
                    )

    operands = [*flat, *(array for _, array, _, _ in shards)]
    in_specs = [pl.BlockSpec(memory_space=pl.ANY) for _ in operands]
    aliases = {}
    if total is not None:
        operands.append(total)
        in_specs.append(pl.BlockSpec(memory_space=pltpu.VMEM))
        aliases = {len(operands): 0}
    out_shape = [jax.ShapeDtypeStruct((clip_count, row_count, lanes), jnp.float32)]
    if peers:
        out_shape.append(jax.ShapeDtypeStruct((peers, 1, clip_count * row_count), jnp.float32))
    return pl.pallas_call(
        kernel,
        in_specs=[pl.BlockSpec(memory_space=pltpu.SMEM)] + in_specs,
        out_specs=[pl.BlockSpec(memory_space=pltpu.VMEM)] * len(out_shape),
        out_shape=out_shape,
        scratch_shapes=[
            pltpu.VMEM((shard_total, clip_count * row_count, depth), jnp.bfloat16),
            pltpu.VMEM((shard_total, lanes, depth), jnp.bfloat16),
            pltpu.SemaphoreType.DMA((shard_total, clip_count, stream_count)),
            pltpu.SemaphoreType.DMA((shard_total,)),
        ],
        input_output_aliases=aliases,
        compiler_params=pltpu.CompilerParams(vmem_limit_bytes=(8 + 4 * shard_total) * 1024 * 1024),
        cost_estimate=pl.CostEstimate(
            flops=2 * clip_count * row_count * depth * columns * shard_total,
            bytes_accessed=shard_total * depth * (clip_count * row_count + columns) * 2,
            transcendentals=0,
        ),
        name="project",
    )(where, *operands)


def finish(total, squares, gain, columns, model_width, devices):
    clip_count, row_count, lanes = total.shape
    near_rows = row_count // 2

    def kernel(total_ref, squares_ref, gain_ref, features_ref, row_ref):
        clip = pl.program_id(0)
        diagonal = on_diagonal()
        scales = []
        for first in range(0, row_count, LANES):
            at = pl.ds(pl.multiple_of(clip * row_count + first, LANES), LANES)
            mean = jnp.sum(squares_ref[:, :, at], axis=0) / model_width
            scale = jnp.broadcast_to(lax.rsqrt(mean + epsilon), (LANES, LANES))
            scales.append(jnp.sum(jnp.where(diagonal, scale, 0.0), axis=1, keepdims=True))
        scale = jnp.concatenate(scales, axis=0)
        clean = total_ref[0, :near_rows] * scale[:near_rows]
        features_ref[0] = (clean * gain_ref[...]).astype(jnp.bfloat16)
        difference = total_ref[0, near_rows:] * scale[near_rows:] - clean
        sums = jnp.sum(difference * difference, axis=0, keepdims=True)
        penalty = jnp.sum(sums * gain_ref[...] * gain_ref[...], axis=1, keepdims=True)
        lane = lax.broadcasted_iota(jnp.int32, (1, lanes), 1)
        sums = sums + jnp.where(lane == columns + clip, penalty, 0.0)
        sums = jnp.broadcast_to(sums[None], row_ref.shape)

        @pl.when(clip == 0)
        def _():
            row_ref[...] = sums

        @pl.when(clip > 0)
        def _():
            row_ref[...] += sums

    return pl.pallas_call(
        kernel,
        grid=(clip_count,),
        in_specs=[
            pl.BlockSpec((1, row_count, lanes), lambda c: (c, 0, 0)),
            pl.BlockSpec(squares.shape, lambda c: (0, 0, 0)),
            pl.BlockSpec((1, lanes), lambda c: (0, 0)),
        ],
        out_specs=[
            pl.BlockSpec((1, near_rows, lanes), lambda c: (c, 0, 0)),
            pl.BlockSpec((devices, 1, lanes), lambda c: (0, 0, 0)),
        ],
        out_shape=[
            jax.ShapeDtypeStruct((clip_count, near_rows, lanes), jnp.bfloat16),
            jax.ShapeDtypeStruct((devices, 1, lanes), jnp.float32),
        ],
        compiler_params=pltpu.CompilerParams(vmem_limit_bytes=16 * 1024 * 1024),
        name="finish",
    )(total, squares, gain)


def conclude(rows, where, gain, model_count, clip_count, tokens):
    devices, _, lanes = rows.shape
    columns = gain.shape[1] // clip_count
    model_width = gain.shape[1] * model_count

    def kernel(where_ref, rows_ref, gain_ref, penalty_ref, grad_ref):
        row = lax.broadcasted_iota(jnp.int32, (devices, 1, lanes), 0)
        model = (row // clip_count) % model_count
        sums = []
        for clip in range(clip_count):
            mine = (model == where_ref[1]) & (row % clip_count == clip)
            sums.append(jnp.sum(jnp.where(mine, rows_ref[...], 0.0), axis=0)[:, :columns])
        sums = jnp.concatenate(sums, axis=1)
        grad = gain_ref[...] * sums / (sigma_noise * sigma_noise * tokens)
        grad_ref[...] = grad.reshape(grad_ref.shape)
        lane = lax.broadcasted_iota(jnp.int32, (devices, 1, lanes), 2)
        own = jnp.where(lane == columns + where_ref[2], rows_ref[...], 0.0)
        penalty_ref[0] = jnp.sum(own) / (sigma_noise * sigma_noise * tokens * model_width)

    return pl.pallas_call(
        kernel,
        in_specs=[pl.BlockSpec(memory_space=pltpu.SMEM)]
        + [pl.BlockSpec(memory_space=pltpu.VMEM)] * 2,
        out_specs=[
            pl.BlockSpec(memory_space=pltpu.SMEM),
            pl.BlockSpec(memory_space=pltpu.VMEM),
        ],
        out_shape=[
            jax.ShapeDtypeStruct((1,), jnp.float32),
            jax.ShapeDtypeStruct((gain.shape[1],), jnp.float32),
        ],
        name="conclude",
    )(where, rows, gain)


def swap(array, axis, distance):
    count = lax.axis_size(axis)
    return lax.ppermute(array, axis, [(i, i ^ distance) for i in range(count)])


def distances(axis):
    count = lax.axis_size(axis)
    return [(axis, 1 << bit) for bit in reversed(range(count.bit_length() - 1))]


def spread(block, order, before_step):
    stacks = [([(0, 0)], block[None])]
    for step, (axis, distance) in enumerate(order):
        if step < len(order) - 1 and len(stacks) > 1:
            keys = [key for some, _ in stacks for key in some]
            stacks = [(keys, jnp.concatenate([array for _, array in stacks]))]
        received = []
        for part, (keys, array) in enumerate(stacks):
            keys = [(m ^ distance, c) if axis == "mp" else (m, c ^ distance) for m, c in keys]
            received.append((keys, swap(before_step(step, part, array), axis, distance)))
        stacks = stacks + received
    return stacks


def collect(rows, axes):
    return lax.all_to_all(rows, axes, split_axis=0, concat_axis=0, tiled=True)


def pick(options, index):
    return lax.select_n(index, *options) if len(options) > 1 else options[0]


def local(projections, perturbation, out_weight, norm_gain, live_counts):
    tile_len = projections.shape[2]
    local_width = projections.shape[4]
    slots = projections.shape[1]
    slab_count = lax.axis_size("frames")
    slab_index = lax.axis_index("frames")
    model_count = lax.axis_size("mp")
    model_index = lax.axis_index("mp")
    clip_count = lax.axis_size("dp")
    clip_index = lax.axis_index("dp")
    model_width = local_width * model_count
    token_total = slots * slab_count * tile_len
    half = local_width // clip_count
    near_rows = slots * tile_len

    def own_columns(array):
        return pick(
            [array[..., n * half : (n + 1) * half] for n in range(clip_count)], clip_index
        )

    clean = projections[0].transpose(0, 2, 1, 3)
    noise = perturbation[0].transpose(0, 2, 1, 3)
    up = [(i, i + 1) for i in range(slab_count - 1)]
    down = [(i + 1, i) for i in range(slab_count - 1)]

    halo = []
    edges = (slots - 1, 0)
    for noisy in (False, True):
        sent = [
            perturb(clean[slot, 1:], noise[slot, 1:]) if noisy else clean[slot, 1:]
            for slot in edges
        ]
        sent, clean, noise, out_weight = lax.optimization_barrier((sent, clean, noise, out_weight))
        halo.append(
            (lax.ppermute(sent[0], "frames", up), lax.ppermute(sent[1], "frames", down))
        )
    streams = (clean, perturb(clean, noise))
    counts = jnp.pad(live_counts[0], (1, 1))
    nearby = lax.dynamic_slice_in_dim(counts, slots * slab_index, slots + 2)
    where = jnp.concatenate(
        [jnp.stack([slab_index, model_index, clip_index]).astype(jnp.int32), nearby]
    )
    gain_row = jnp.pad(own_columns(norm_gain), (0, whole_lanes(half) - half))[None]
    gain_all = norm_gain[None]

    own_weight = own_columns(out_weight).T
    own_weight, halo[0] = lax.optimization_barrier((own_weight, halo[0]))
    line = slab_count == model_count and slab_count == 4
    last = slab_count - 1
    near, passed, across = [], [], None

    if line:
        near = [lax.ppermute(own_weight, "frames", up), lax.ppermute(own_weight, "frames", down)]
        across = lax.ppermute(own_weight, "frames", [(0, last), (last, 0)])

    def before_step(stream, step, part, value):
        nonlocal near, passed, gain_row, gain_all
        if line and stream == 0 and step == 1:
            value, near, gain_row, gain_all = lax.optimization_barrier(
                (value, near, gain_row, gain_all)
            )
            passed = [
                lax.ppermute(near[0], "frames", up[1:]),
                lax.ppermute(near[1], "frames", down[:2]),
            ]
        if line and stream == 1 and step == 2 and part == 1:
            value, passed = lax.optimization_barrier((value, passed))
        return value

    gathered = []
    orders = (
        distances("dp") + distances("mp"),
        distances("mp")[:1] + distances("dp") + distances("mp")[1:],
    )
    for n, order in enumerate(orders):
        attended = attention(where, streams[n], *halo[n]).reshape(near_rows, local_width)
        gathered.append(
            spread(attended, order, lambda *at, n=n: before_step(n, *at))
        )

    peers = model_count * clip_count
    if line:
        shards = [
            (0, own_weight, lambda slab: slab, lambda slab: slab >= 0),
            (0, near[0], lambda slab: jnp.maximum(slab - 1, 0), lambda slab: slab > 0),
            (0, near[1], lambda slab: jnp.minimum(slab + 1, last), lambda slab: slab < last),
            (0, passed[0], lambda slab: jnp.maximum(slab - 2, 0), lambda slab: slab >= 2),
            (0, passed[1], lambda slab: jnp.minimum(slab + 2, last), lambda slab: slab < 2),
            (0, across, lambda slab: last - slab, lambda slab: (slab == 0) | (slab == last)),
        ]
        (total,) = project(where, gathered, shards[:-1], None, half, 0)
        total, squares = project(where, gathered, shards[-1:], total, half, peers)
    else:
        weight = lax.all_gather(own_weight, "frames", axis=1, tiled=True)
        shards = [
            (
                0,
                lax.dynamic_slice_in_dim(weight, m * local_width, local_width, axis=1),
                lambda slab, m=m: m,
                lambda slab: slab >= 0,
            )
            for m in range(model_count)
        ]
        total, squares = project(where, gathered, shards, None, half, peers)

    squares = collect(squares, ("mp", "dp"))
    features, sums = finish(
        total, squares, gain_row, half, model_width, slab_count * model_count * clip_count
    )
    sums = collect(sums, ("frames", "mp", "dp"))

    features = features[..., :half].reshape(clip_count, slots, tile_len, half)
    columns = [pick([features[d] for d in range(clip_count)], clip_index)]
    for distance in range(1, clip_count):
        sent = pick([features[d ^ distance] for d in range(clip_count)], clip_index)
        columns.append(swap(sent, "dp", distance))
    features = jnp.concatenate(
        [
            pick([columns[n ^ d] for d in range(clip_count)], clip_index)
            for n in range(clip_count)
        ],
        axis=-1,
    )[None]
    sums, features = lax.optimization_barrier((sums, features))
    penalty, gain_grad = conclude(
        sums, where, gain_all, model_count, clip_count, token_total
    )
    return (features, penalty, gain_grad)


def solution(mesh):
    placed = (
        P("dp", "frames", None, None, "mp"),
        P("dp", "frames", None, None, "mp"),
        P("frames", "mp"),
        P("mp"),
        P("dp", None),
    )
    return jax.shard_map(
        local,
        mesh=mesh,
        in_specs=placed,
        out_specs=(P("dp", "frames", None, "mp"), P("dp"), P("mp")),
        check_vma=False,
    )
```

```python
import math

import jax
import jax.numpy as jnp
from jax import lax
from jax.experimental import pallas as pl
from jax.experimental.pallas import tpu as pltpu
from jax.sharding import PartitionSpec as P

HEAD_DIM = 128
HEADS_AT_ONCE = 1
LANES = 128


sigma_noise = 0.25
epsilon = 1e-06


def perturb(clean, noise):
    return (clean.astype(jnp.float32) + sigma_noise * noise.astype(jnp.float32)).astype(jnp.bfloat16)


def prepare_halo(clean, noise, slots):
    _, _, tile_len, width = clean.shape

    def kernel(clean_ref, noise_ref, *refs):
        out_refs, (keep, add, sems) = refs[: len(slots)], refs[len(slots) :]
        copies = []
        for n, slot in enumerate(slots):
            for m, (source, target) in enumerate(((clean_ref, keep), (noise_ref, add))):
                copies.append(
                    pltpu.make_async_copy(
                        source.at[slot, pl.ds(1, 2)], target.at[n], sems.at[n, m]
                    )
                )
                copies[-1].start()
        for n in range(len(slots)):
            copies[2 * n].wait()
            copies[2 * n + 1].wait()
            out_refs[n][0] = keep[n]
            out_refs[n][1] = perturb(keep[n], add[n])

    block = (2, 2, tile_len, width)
    return pl.pallas_call(
        kernel,
        in_specs=[pl.BlockSpec(memory_space=pl.ANY)] * 2,
        out_specs=[pl.BlockSpec(memory_space=pltpu.VMEM)] * len(slots),
        out_shape=[jax.ShapeDtypeStruct(block, jnp.bfloat16)] * len(slots),
        scratch_shapes=[
            pltpu.VMEM((len(slots), 2, tile_len, width), jnp.bfloat16),
            pltpu.VMEM((len(slots), 2, tile_len, width), jnp.bfloat16),
            pltpu.SemaphoreType.DMA((len(slots), 2)),
        ],
        compiler_params=pltpu.CompilerParams(vmem_limit_bytes=16 * 1024 * 1024),
        name="prepare_halo",
    )(clean, noise)


def prepare_weight(where, weight, clip_count):
    depth, width = weight.shape
    half = width // clip_count

    def kernel(where_ref, weight_ref, out_ref):
        for clip in range(clip_count):

            @pl.when(where_ref[2] == clip)
            def _():
                begin, end = clip * half, (clip + 1) * half
                for first in range(begin // LANES * LANES, end, LANES):
                    low, high = max(first, begin), min(first + LANES, end)
                    turned = weight_ref[:, pl.ds(first, LANES)].T
                    out_ref[pl.ds(low - begin, high - low)] = turned[low - first : high - first]

    return pl.pallas_call(
        kernel,
        in_specs=[
            pl.BlockSpec(memory_space=pltpu.SMEM),
            pl.BlockSpec(memory_space=pltpu.VMEM),
        ],
        out_specs=pl.BlockSpec(memory_space=pltpu.VMEM),
        out_shape=jax.ShapeDtypeStruct((half, depth), weight.dtype),
        compiler_params=pltpu.CompilerParams(vmem_limit_bytes=16 * 1024 * 1024),
        name="prepare_weight",
    )(where, weight)


def attend_kernel(where_ref, own_ref, right_ref, left_ref, out_ref):
    slots, _, tile_len, width = own_ref.shape
    key_pos = lax.broadcasted_iota(jnp.int32, (1, 2 * tile_len), 1)
    live = []
    for slot in range(slots):
        own_count = where_ref[4 + slot]
        far_count = where_ref[3 if slot == 0 else slots + 4]
        live.append((key_pos < own_count) | ((key_pos >= tile_len) & (key_pos < tile_len + far_count)))
    row_pos = lax.broadcasted_iota(jnp.int32, (tile_len, 1), 0)
    units = [(slot, head) for head in range(width // HEAD_DIM) for slot in range(slots)]

    scores = []
    for slot, head in units:
        cols = pl.ds(head * HEAD_DIM, HEAD_DIM)
        halo_ref = left_ref if slot == 0 else right_ref
        keys = jnp.concatenate([own_ref[slot, 1, :, cols], halo_ref[0, :, cols]], axis=0)
        raw = lax.dot_general(
            own_ref[slot, 0, :, cols],
            keys,
            (((1,), (1,)), ((), ())),
            preferred_element_type=jnp.float32,
        )
        scores.append(jnp.where(live[slot], raw * (1.0 / math.sqrt(HEAD_DIM)), jnp.float32(-1e30)))
    largest = [jnp.max(s, axis=-1, keepdims=True) for s in scores]
    weights = [jnp.exp(s - top) for s, top in zip(scores, largest)]
    totals = [jnp.sum(w, axis=-1, keepdims=True) for w in weights]
    for (slot, head), weight, total in zip(units, weights, totals):
        cols = pl.ds(head * HEAD_DIM, HEAD_DIM)
        halo_ref = left_ref if slot == 0 else right_ref
        values = jnp.concatenate([own_ref[slot, 2, :, cols], halo_ref[1, :, cols]], axis=0)
        probabilities = (weight * (1.0 / total)).astype(jnp.bfloat16)
        mixed = jnp.dot(probabilities, values, preferred_element_type=jnp.float32)
        out_ref[slot, :, cols] = jnp.where(row_pos < where_ref[4 + slot], mixed, 0.0).astype(
            jnp.bfloat16
        )


def attention(where, own, left, right, stream):
    slots, _, tile_len, width = own.shape
    block = HEADS_AT_ONCE * HEAD_DIM
    own_spec = pl.BlockSpec((slots, 3, tile_len, block), lambda h, c: (0, 0, 0, h))
    halo_spec = pl.BlockSpec((None, 2, tile_len, block), lambda h, c: (stream, 0, 0, h))
    return pl.pallas_call(
        attend_kernel,
        grid_spec=pltpu.PrefetchScalarGridSpec(
            num_scalar_prefetch=1,
            grid=(width // block,),
            in_specs=[own_spec, halo_spec, halo_spec],
            out_specs=pl.BlockSpec((slots, tile_len, block), lambda h, c: (0, 0, h)),
        ),
        out_shape=jax.ShapeDtypeStruct((slots, tile_len, width), jnp.bfloat16),
        compiler_params=pltpu.CompilerParams(vmem_limit_bytes=48 * 1024 * 1024),
        cost_estimate=pl.CostEstimate(
            flops=0,
            bytes_accessed=0,
            transcendentals=0,
        ),
        name="attention",
    )(where, own, right, left)


def whole_lanes(columns):
    return -(-columns // LANES) * LANES


def on_diagonal():
    row = lax.broadcasted_iota(jnp.int32, (LANES, LANES), 0)
    return row == lax.broadcasted_iota(jnp.int32, (LANES, LANES), 1)


def project(where, gathered, shards, total, columns, peers):
    stream_count = len(gathered)
    home = [
        {key: (n, at) for n, (keys, _) in enumerate(stacks) for at, key in enumerate(keys)}
        for stacks in gathered
    ]
    clip_count = 1 + max(clip for _, clip in home[0])
    place_count = 1 + max(place for place, _ in home[0])
    _, block_rows, depth = gathered[0][0][1].shape
    lanes = whole_lanes(columns)
    row_count = stream_count * block_rows
    shard_total = len(shards)
    flat = [array for stacks in gathered for _, array in stacks]
    base = [sum(len(stacks) for stacks in gathered[:n]) for n in range(stream_count)]

    def kernel(where_ref, *refs):
        slab, model, own_clip = where_ref[0], where_ref[1], where_ref[2]
        block_refs = refs[: len(flat)]
        weight_refs = refs[len(flat) : len(flat) + shard_total]
        total_ref = refs[len(flat) + shard_total] if total is not None else None
        rows, held, row_sem, weight_sem = refs[-4:]
        out_ref = refs[len(operands)]
        squares_ref = refs[len(operands) + 1]

        def weight_copy(shard):
            size = shards[shard][1].shape[0]
            return pltpu.make_async_copy(
                weight_refs[shard], held.at[shard, pl.ds(0, size)], weight_sem.at[shard]
            )

        def row_copy(place, shard, clip, stream):
            stack, at = home[stream][place, clip]
            source = block_refs[base[stream] + stack].at[at]
            first = pl.multiple_of(
                (clip ^ own_clip) * row_count + stream * block_rows, 16
            )
            return pltpu.make_async_copy(
                source,
                rows.at[shard, pl.ds(first, block_rows)],
                row_sem.at[shard, clip, stream],
            )

        for shard in range(shard_total):

            @pl.when(shards[shard][3](slab))
            def _():
                weight_copy(shard).start()
                for place in range(place_count):

                    @pl.when((shards[shard][2](slab) ^ model) == place)
                    def _():
                        for clip in range(clip_count):
                            for stream in range(stream_count):
                                row_copy(place, shard, clip, stream).start()

        if total is None:
            out_ref[...] = jnp.zeros_like(out_ref)
        else:
            out_ref[...] = total_ref[...]

        for shard in range(shard_total):

            @pl.when(shards[shard][3](slab))
            def _():
                weight_copy(shard).wait()
                for clip in range(clip_count):
                    for stream in range(stream_count):
                        row_copy(0, shard, clip, stream).wait()
                first, array = shards[shard][:2]
                size = array.shape[0]
                wide = whole_lanes(size)
                if wide > size:
                    held[shard, size:wide] = jnp.zeros((wide - size, depth), held.dtype)
                for clip in range(clip_count):
                    out_ref[clip, :, pl.ds(first, wide)] += lax.dot_general(
                        rows[shard, pl.ds(clip * row_count, row_count)],
                        held[shard, pl.ds(0, wide)],
                        (((1,), (1,)), ((), ())),
                        preferred_element_type=jnp.float32,
                    )

        if peers:
            diagonal = on_diagonal()
            for clip in range(clip_count):
                for first in range(0, row_count, LANES):
                    piece = out_ref[clip, pl.ds(first, LANES)]
                    sums = jnp.sum(piece * piece, axis=1, keepdims=True)
                    sums = jnp.sum(jnp.where(diagonal, sums, 0.0), axis=0, keepdims=True)
                    squares_ref[:, :, pl.ds(clip * row_count + first, LANES)] = jnp.broadcast_to(
                        sums[None], (peers, 1, LANES)
                    )

    operands = [*flat, *(array for _, array, _, _ in shards)]
    in_specs = [pl.BlockSpec(memory_space=pl.ANY) for _ in operands]
    aliases = {}
    if total is not None:
        operands.append(total)
        in_specs.append(pl.BlockSpec(memory_space=pltpu.VMEM))
        aliases = {len(operands): 0}
    out_shape = [jax.ShapeDtypeStruct((clip_count, row_count, lanes), jnp.float32)]
    if peers:
        out_shape.append(jax.ShapeDtypeStruct((peers, 1, clip_count * row_count), jnp.float32))
    return pl.pallas_call(
        kernel,
        in_specs=[pl.BlockSpec(memory_space=pltpu.SMEM)] + in_specs,
        out_specs=[pl.BlockSpec(memory_space=pltpu.VMEM)] * len(out_shape),
        out_shape=out_shape,
        scratch_shapes=[
            pltpu.VMEM((shard_total, clip_count * row_count, depth), jnp.bfloat16),
            pltpu.VMEM((shard_total, lanes, depth), jnp.bfloat16),
            pltpu.SemaphoreType.DMA((shard_total, clip_count, stream_count)),
            pltpu.SemaphoreType.DMA((shard_total,)),
        ],
        input_output_aliases=aliases,
        compiler_params=pltpu.CompilerParams(vmem_limit_bytes=(8 + 4 * shard_total) * 1024 * 1024),
        cost_estimate=pl.CostEstimate(
            flops=0,
            bytes_accessed=0,
            transcendentals=0,
        ),
        name="project",
    )(where, *operands)


def finish(total, squares, gain, columns, model_width, devices):
    clip_count, row_count, lanes = total.shape
    near_rows = row_count // 2

    def kernel(total_ref, squares_ref, gain_ref, features_ref, row_ref):
        clip = pl.program_id(0)
        diagonal = on_diagonal()
        scales = []
        for first in range(0, row_count, LANES):
            at = pl.ds(pl.multiple_of(clip * row_count + first, LANES), LANES)
            mean = jnp.sum(squares_ref[:, :, at], axis=0) / model_width
            scale = jnp.broadcast_to(lax.rsqrt(mean + epsilon), (LANES, LANES))
            scales.append(jnp.sum(jnp.where(diagonal, scale, 0.0), axis=1, keepdims=True))
        scale = jnp.concatenate(scales, axis=0)
        clean = total_ref[0, :near_rows] * scale[:near_rows]
        features_ref[0] = (clean * gain_ref[...]).astype(jnp.bfloat16)
        difference = total_ref[0, near_rows:] * scale[near_rows:] - clean
        sums = jnp.sum(difference * difference, axis=0, keepdims=True)
        penalty = jnp.sum(sums * gain_ref[...] * gain_ref[...], axis=1, keepdims=True)
        lane = lax.broadcasted_iota(jnp.int32, (1, lanes), 1)
        sums = sums + jnp.where(lane == columns + clip, penalty, 0.0)
        sums = jnp.broadcast_to(sums[None], row_ref.shape)

        @pl.when(clip == 0)
        def _():
            row_ref[...] = sums

        @pl.when(clip > 0)
        def _():
            row_ref[...] += sums

    return pl.pallas_call(
        kernel,
        grid=(clip_count,),
        in_specs=[
            pl.BlockSpec((1, row_count, lanes), lambda c: (c, 0, 0)),
            pl.BlockSpec(squares.shape, lambda c: (0, 0, 0)),
            pl.BlockSpec((1, lanes), lambda c: (0, 0)),
        ],
        out_specs=[
            pl.BlockSpec((1, near_rows, lanes), lambda c: (c, 0, 0)),
            pl.BlockSpec((devices, 1, lanes), lambda c: (0, 0, 0)),
        ],
        out_shape=[
            jax.ShapeDtypeStruct((clip_count, near_rows, lanes), jnp.bfloat16),
            jax.ShapeDtypeStruct((devices, 1, lanes), jnp.float32),
        ],
        compiler_params=pltpu.CompilerParams(vmem_limit_bytes=16 * 1024 * 1024),
        name="finish",
    )(total, squares, gain)


def conclude(rows, where, gain, model_count, clip_count, tokens):
    devices, _, lanes = rows.shape
    columns = gain.shape[1] // clip_count
    model_width = gain.shape[1] * model_count

    def kernel(where_ref, rows_ref, gain_ref, penalty_ref, grad_ref):
        row = lax.broadcasted_iota(jnp.int32, (devices, 1, lanes), 0)
        model = (row // clip_count) % model_count
        sums = []
        for clip in range(clip_count):
            mine = (model == where_ref[1]) & (row % clip_count == clip)
            sums.append(jnp.sum(jnp.where(mine, rows_ref[...], 0.0), axis=0)[:, :columns])
        sums = jnp.concatenate(sums, axis=1)
        grad = gain_ref[...] * sums / (sigma_noise * sigma_noise * tokens)
        grad_ref[...] = grad.reshape(grad_ref.shape)
        lane = lax.broadcasted_iota(jnp.int32, (devices, 1, lanes), 2)
        own = jnp.where(lane == columns + where_ref[2], rows_ref[...], 0.0)
        penalty_ref[0] = jnp.sum(own) / (sigma_noise * sigma_noise * tokens * model_width)

    return pl.pallas_call(
        kernel,
        in_specs=[pl.BlockSpec(memory_space=pltpu.SMEM)]
        + [pl.BlockSpec(memory_space=pltpu.VMEM)] * 2,
        out_specs=[
            pl.BlockSpec(memory_space=pltpu.SMEM),
            pl.BlockSpec(memory_space=pltpu.VMEM),
        ],
        out_shape=[
            jax.ShapeDtypeStruct((1,), jnp.float32),
            jax.ShapeDtypeStruct((gain.shape[1],), jnp.float32),
        ],
        name="conclude",
    )(where, rows, gain)


def swap(array, axis, distance):
    count = lax.axis_size(axis)
    return lax.ppermute(array, axis, [(i, i ^ distance) for i in range(count)])


def distances(axis):
    count = lax.axis_size(axis)
    return [(axis, 1 << bit) for bit in reversed(range(count.bit_length() - 1))]


def spread(block, order, before_step):
    stacks = [([(0, 0)], block[None])]
    for step, (axis, distance) in enumerate(order):
        if step < len(order) - 1 and len(stacks) > 1:
            keys = [key for some, _ in stacks for key in some]
            stacks = [(keys, jnp.concatenate([array for _, array in stacks]))]
        received = []
        for part, (keys, array) in enumerate(stacks):
            keys = [(m ^ distance, c) if axis == "mp" else (m, c ^ distance) for m, c in keys]
            received.append((keys, swap(before_step(step, part, array), axis, distance)))
        stacks = stacks + received
    return stacks


def collect(rows, axes):
    return lax.all_to_all(rows, axes, split_axis=0, concat_axis=0, tiled=True)


def pick(options, index):
    return lax.select_n(index, *options) if len(options) > 1 else options[0]


def local(projections, perturbation, out_weight, norm_gain, live_counts):
    tile_len = projections.shape[2]
    local_width = projections.shape[4]
    slots = projections.shape[1]
    slab_count = lax.axis_size("frames")
    slab_index = lax.axis_index("frames")
    model_count = lax.axis_size("mp")
    model_index = lax.axis_index("mp")
    clip_count = lax.axis_size("dp")
    clip_index = lax.axis_index("dp")
    model_width = local_width * model_count
    token_total = slots * slab_count * tile_len
    half = local_width // clip_count
    near_rows = slots * tile_len

    def own_columns(array):
        return pick(
            [array[..., n * half : (n + 1) * half] for n in range(clip_count)], clip_index
        )

    clean = projections[0].transpose(0, 2, 1, 3)
    noise = perturbation[0].transpose(0, 2, 1, 3)
    up = [(i, i + 1) for i in range(slab_count - 1)]
    down = [(i + 1, i) for i in range(slab_count - 1)]

    tail, head = prepare_halo(clean, noise, (slots - 1, 0))
    tail, head, clean, noise, out_weight = lax.optimization_barrier(
        (tail, head, clean, noise, out_weight)
    )
    right = lax.ppermute(head, "frames", down)
    left = lax.ppermute(tail, "frames", up)
    streams = (clean, perturb(clean, noise))
    counts = jnp.pad(live_counts[0], (1, 1))
    nearby = lax.dynamic_slice_in_dim(counts, slots * slab_index, slots + 2)
    where = jnp.concatenate(
        [jnp.stack([slab_index, model_index, clip_index]).astype(jnp.int32), nearby]
    )
    gain_row = jnp.pad(own_columns(norm_gain), (0, whole_lanes(half) - half))[None]
    gain_all = norm_gain[None]

    own_weight = prepare_weight(where, out_weight, clip_count)
    line = slab_count == model_count and slab_count == 4
    last = slab_count - 1
    cut = min(LANES, half)
    near, passed, across = [], [], []

    if line:
        near = [lax.ppermute(own_weight, "frames", pairs) for pairs in (down, up)]
        across = [
            lax.ppermute(block, "frames", [(0, last), (last, 0)])
            for block in (own_weight[:cut], own_weight[cut:])
        ]

    def before_step(stream, step, part, value):
        nonlocal near, passed, gain_row, gain_all
        if line and stream == 0 and step == 1:
            value, near, gain_row, gain_all = lax.optimization_barrier(
                (value, near, gain_row, gain_all)
            )
            passed = [
                lax.ppermute(near[0], "frames", down[:2]),
                lax.ppermute(near[1], "frames", up[1:]),
            ]
        if line and stream == 1 and step == 1:
            value, across[0] = lax.optimization_barrier((value, across[0]))
        if line and stream == 1 and step == 2 and part == 1:
            value, passed = lax.optimization_barrier((value, passed))
        return value

    gathered = []
    orders = (
        distances("dp") + distances("mp"),
        distances("mp")[:1] + distances("dp") + distances("mp")[1:],
    )
    for n, order in enumerate(orders):
        attended = attention(where, streams[n], left, right, n).reshape(near_rows, local_width)
        gathered.append(
            spread(attended, order, lambda *at, n=n: before_step(n, *at))
        )

    peers = model_count * clip_count
    if line:
        shards = [
            (0, own_weight, lambda slab: slab, lambda slab: slab >= 0),
            (0, near[0], lambda slab: jnp.minimum(slab + 1, last), lambda slab: slab < last),
            (0, near[1], lambda slab: jnp.maximum(slab - 1, 0), lambda slab: slab > 0),
            (0, passed[0], lambda slab: jnp.minimum(slab + 2, last), lambda slab: slab < 2),
            (0, passed[1], lambda slab: jnp.maximum(slab - 2, 0), lambda slab: slab >= 2),
        ]
        for first, block in zip((0, cut), across):
            shards.append(
                (first, block, lambda slab: last - slab, lambda slab: (slab == 0) | (slab == last))
            )
        (total,) = project(where, gathered, shards[:-1], None, half, 0)
        total, squares = project(where, gathered, shards[-1:], total, half, peers)
    else:
        weight = lax.all_gather(own_weight, "frames", axis=1, tiled=True)
        shards = [
            (
                0,
                lax.dynamic_slice_in_dim(weight, m * local_width, local_width, axis=1),
                lambda slab, m=m: m,
                lambda slab: slab >= 0,
            )
            for m in range(model_count)
        ]
        total, squares = project(where, gathered, shards, None, half, peers)

    squares = collect(squares, ("mp", "dp"))
    features, sums = finish(
        total, squares, gain_row, half, model_width, slab_count * model_count * clip_count
    )
    sums = collect(sums, ("frames", "mp", "dp"))

    features = features[..., :half].reshape(clip_count, slots, tile_len, half)
    columns = [pick([features[d] for d in range(clip_count)], clip_index)]
    for distance in range(1, clip_count):
        sent = pick([features[d ^ distance] for d in range(clip_count)], clip_index)
        columns.append(swap(sent, "dp", distance))
    features = jnp.concatenate(
        [
            pick([columns[n ^ d] for d in range(clip_count)], clip_index)
            for n in range(clip_count)
        ],
        axis=-1,
    )[None]
    sums, features = lax.optimization_barrier((sums, features))
    penalty, gain_grad = conclude(
        sums, where, gain_all, model_count, clip_count, token_total
    )
    return (features, penalty, gain_grad)


def solution(mesh):
    placed = (
        P("dp", "frames", None, None, "mp"),
        P("dp", "frames", None, None, "mp"),
        P("frames", "mp"),
        P("mp"),
        P("dp", None),
    )
    return jax.shard_map(
        local,
        mesh=mesh,
        in_specs=placed,
        out_specs=(P("dp", "frames", None, "mp"), P("dp"), P("mp")),
        check_vma=False,
    )
```

```python
import math

import jax
import jax.numpy as jnp
from jax import lax
from jax.experimental import pallas as pl
from jax.experimental.pallas import tpu as pltpu
from jax.sharding import PartitionSpec as P

HEAD_DIM = 128
HEADS_AT_ONCE = 1
LANES = 128


sigma_noise = 0.25
epsilon = 1e-06


def perturb(clean, noise):
    return (clean.astype(jnp.float32) + sigma_noise * noise.astype(jnp.float32)).astype(jnp.bfloat16)


def prepare_halo(clean, noise, slots):
    _, _, tile_len, width = clean.shape

    def kernel(clean_ref, noise_ref, *refs):
        out_refs, (keep, add, sems) = refs[: len(slots)], refs[len(slots) :]
        copies = []
        for n, slot in enumerate(slots):
            for m, (source, target) in enumerate(((clean_ref, keep), (noise_ref, add))):
                copies.append(
                    pltpu.make_async_copy(
                        source.at[slot, pl.ds(1, 2)], target.at[n], sems.at[n, m]
                    )
                )
                copies[-1].start()
        for n in range(len(slots)):
            copies[2 * n].wait()
            copies[2 * n + 1].wait()
            out_refs[n][0] = keep[n]
            out_refs[n][1] = perturb(keep[n], add[n])

    block = (2, 2, tile_len, width)
    return pl.pallas_call(
        kernel,
        in_specs=[pl.BlockSpec(memory_space=pl.ANY)] * 2,
        out_specs=[pl.BlockSpec(memory_space=pltpu.VMEM)] * len(slots),
        out_shape=[jax.ShapeDtypeStruct(block, jnp.bfloat16)] * len(slots),
        scratch_shapes=[
            pltpu.VMEM((len(slots), 2, tile_len, width), jnp.bfloat16),
            pltpu.VMEM((len(slots), 2, tile_len, width), jnp.bfloat16),
            pltpu.SemaphoreType.DMA((len(slots), 2)),
        ],
        compiler_params=pltpu.CompilerParams(vmem_limit_bytes=60 * 1024 * 1024),
        name="prepare_halo",
    )(clean, noise)


def prepare_weight(where, weight, clip_count):
    depth, width = weight.shape
    half = width // clip_count

    def kernel(where_ref, weight_ref, out_ref):
        for clip in range(clip_count):

            @pl.when(where_ref[2] == clip)
            def _():
                begin, end = clip * half, (clip + 1) * half
                for first in range(begin // LANES * LANES, end, LANES):
                    low, high = max(first, begin), min(first + LANES, end)
                    turned = weight_ref[:, pl.ds(first, LANES)].T
                    out_ref[pl.ds(low - begin, high - low)] = turned[low - first : high - first]

    return pl.pallas_call(
        kernel,
        in_specs=[
            pl.BlockSpec(memory_space=pltpu.SMEM),
            pl.BlockSpec(memory_space=pltpu.VMEM),
        ],
        out_specs=pl.BlockSpec(memory_space=pltpu.VMEM),
        out_shape=jax.ShapeDtypeStruct((half, depth), weight.dtype),
        compiler_params=pltpu.CompilerParams(vmem_limit_bytes=60 * 1024 * 1024),
        name="prepare_weight",
    )(where, weight)


def attend_kernel(where_ref, own_ref, right_ref, left_ref, out_ref):
    slots, _, tile_len, width = own_ref.shape
    key_pos = lax.broadcasted_iota(jnp.int32, (1, 2 * tile_len), 1)
    live = []
    for slot in range(slots):
        own_count = where_ref[4 + slot]
        far_count = where_ref[3 if slot == 0 else slots + 4]
        live.append((key_pos < own_count) | ((key_pos >= tile_len) & (key_pos < tile_len + far_count)))
    row_pos = lax.broadcasted_iota(jnp.int32, (tile_len, 1), 0)
    units = [(slot, head) for head in range(width // HEAD_DIM) for slot in range(slots)]

    scores = []
    for slot, head in units:
        cols = pl.ds(head * HEAD_DIM, HEAD_DIM)
        halo_ref = left_ref if slot == 0 else right_ref
        keys = jnp.concatenate([own_ref[slot, 1, :, cols], halo_ref[0, :, cols]], axis=0)
        raw = lax.dot_general(
            own_ref[slot, 0, :, cols],
            keys,
            (((1,), (1,)), ((), ())),
            preferred_element_type=jnp.float32,
        )
        scores.append(jnp.where(live[slot], raw * (1.0 / math.sqrt(HEAD_DIM)), jnp.float32(-1e30)))
    largest = [jnp.max(s, axis=-1, keepdims=True) for s in scores]
    weights = [jnp.exp(s - top) for s, top in zip(scores, largest)]
    totals = [jnp.sum(w, axis=-1, keepdims=True) for w in weights]
    for (slot, head), weight, total in zip(units, weights, totals):
        cols = pl.ds(head * HEAD_DIM, HEAD_DIM)
        halo_ref = left_ref if slot == 0 else right_ref
        values = jnp.concatenate([own_ref[slot, 2, :, cols], halo_ref[1, :, cols]], axis=0)
        probabilities = (weight * (1.0 / total)).astype(jnp.bfloat16)
        mixed = jnp.dot(probabilities, values, preferred_element_type=jnp.float32)
        out_ref[slot, :, cols] = jnp.where(row_pos < where_ref[4 + slot], mixed, 0.0).astype(
            jnp.bfloat16
        )


def attention(where, own, left, right, stream):
    slots, _, tile_len, width = own.shape
    block = HEADS_AT_ONCE * HEAD_DIM
    own_spec = pl.BlockSpec((slots, 3, tile_len, block), lambda h, c: (0, 0, 0, h))
    halo_spec = pl.BlockSpec((None, 2, tile_len, block), lambda h, c: (stream, 0, 0, h))
    return pl.pallas_call(
        attend_kernel,
        grid_spec=pltpu.PrefetchScalarGridSpec(
            num_scalar_prefetch=1,
            grid=(width // block,),
            in_specs=[own_spec, halo_spec, halo_spec],
            out_specs=pl.BlockSpec((slots, tile_len, block), lambda h, c: (0, 0, h)),
        ),
        out_shape=jax.ShapeDtypeStruct((slots, tile_len, width), jnp.bfloat16),
        compiler_params=pltpu.CompilerParams(vmem_limit_bytes=48 * 1024 * 1024),
        cost_estimate=pl.CostEstimate(
            flops=0,
            bytes_accessed=0,
            transcendentals=0,
        ),
        name="attention",
    )(where, own, right, left)


def whole_lanes(columns):
    return -(-columns // LANES) * LANES


def on_diagonal():
    row = lax.broadcasted_iota(jnp.int32, (LANES, LANES), 0)
    return row == lax.broadcasted_iota(jnp.int32, (LANES, LANES), 1)


def project(where, gathered, shards, total, columns, peers):
    stream_count = len(gathered)
    home = [
        {key: (n, at) for n, (keys, _) in enumerate(stacks) for at, key in enumerate(keys)}
        for stacks in gathered
    ]
    clip_count = 1 + max(clip for _, clip in home[0])
    place_count = 1 + max(place for place, _ in home[0])
    _, block_rows, depth = gathered[0][0][1].shape
    lanes = whole_lanes(columns)
    row_count = stream_count * block_rows
    shard_total = len(shards)
    flat = [array for stacks in gathered for _, array in stacks]
    base = [sum(len(stacks) for stacks in gathered[:n]) for n in range(stream_count)]

    def kernel(where_ref, *refs):
        slab, model, own_clip = where_ref[0], where_ref[1], where_ref[2]
        block_refs = refs[: len(flat)]
        weight_refs = refs[len(flat) : len(flat) + shard_total]
        total_ref = refs[len(flat) + shard_total] if total is not None else None
        rows, held, row_sem, weight_sem = refs[-4:]
        out_ref = refs[len(operands)]
        squares_ref = refs[len(operands) + 1]

        def weight_copy(shard):
            size = shards[shard][1].shape[0]
            return pltpu.make_async_copy(
                weight_refs[shard], held.at[shard, pl.ds(0, size)], weight_sem.at[shard]
            )

        def row_copy(place, shard, clip, stream):
            stack, at = home[stream][place, clip]
            source = block_refs[base[stream] + stack].at[at]
            first = pl.multiple_of(
                (clip ^ own_clip) * row_count + stream * block_rows, 16
            )
            return pltpu.make_async_copy(
                source,
                rows.at[shard, pl.ds(first, block_rows)],
                row_sem.at[shard, clip, stream],
            )

        for shard in range(shard_total):

            @pl.when(shards[shard][3](slab))
            def _():
                weight_copy(shard).start()
                for place in range(place_count):

                    @pl.when((shards[shard][2](slab) ^ model) == place)
                    def _():
                        for clip in range(clip_count):
                            for stream in range(stream_count):
                                row_copy(place, shard, clip, stream).start()

        if total is None:
            out_ref[...] = jnp.zeros_like(out_ref)
        else:
            out_ref[...] = total_ref[...]

        for shard in range(shard_total):

            @pl.when(shards[shard][3](slab))
            def _():
                weight_copy(shard).wait()
                for clip in range(clip_count):
                    for stream in range(stream_count):
                        row_copy(0, shard, clip, stream).wait()
                first, array = shards[shard][:2]
                size = array.shape[0]
                wide = whole_lanes(size)
                if wide > size:
                    held[shard, size:wide] = jnp.zeros((wide - size, depth), held.dtype)
                for clip in range(clip_count):
                    out_ref[clip, :, pl.ds(first, wide)] += lax.dot_general(
                        rows[shard, pl.ds(clip * row_count, row_count)],
                        held[shard, pl.ds(0, wide)],
                        (((1,), (1,)), ((), ())),
                        preferred_element_type=jnp.float32,
                    )

        if peers:
            diagonal = on_diagonal()
            for clip in range(clip_count):
                for first in range(0, row_count, LANES):
                    piece = out_ref[clip, pl.ds(first, LANES)]
                    sums = jnp.sum(piece * piece, axis=1, keepdims=True)
                    sums = jnp.sum(jnp.where(diagonal, sums, 0.0), axis=0, keepdims=True)
                    squares_ref[:, :, pl.ds(clip * row_count + first, LANES)] = jnp.broadcast_to(
                        sums[None], (peers, 1, LANES)
                    )

    operands = [*flat, *(array for _, array, _, _ in shards)]
    in_specs = [pl.BlockSpec(memory_space=pl.ANY) for _ in operands]
    aliases = {}
    if total is not None:
        operands.append(total)
        in_specs.append(pl.BlockSpec(memory_space=pltpu.VMEM))
        aliases = {len(operands): 0}
    out_shape = [jax.ShapeDtypeStruct((clip_count, row_count, lanes), jnp.float32)]
    if peers:
        out_shape.append(jax.ShapeDtypeStruct((peers, 1, clip_count * row_count), jnp.float32))
    return pl.pallas_call(
        kernel,
        in_specs=[pl.BlockSpec(memory_space=pltpu.SMEM)] + in_specs,
        out_specs=[pl.BlockSpec(memory_space=pltpu.VMEM)] * len(out_shape),
        out_shape=out_shape,
        scratch_shapes=[
            pltpu.VMEM((shard_total, clip_count * row_count, depth), jnp.bfloat16),
            pltpu.VMEM((shard_total, lanes, depth), jnp.bfloat16),
            pltpu.SemaphoreType.DMA((shard_total, clip_count, stream_count)),
            pltpu.SemaphoreType.DMA((shard_total,)),
        ],
        input_output_aliases=aliases,
        compiler_params=pltpu.CompilerParams(vmem_limit_bytes=(8 + 4 * shard_total) * 1024 * 1024),
        cost_estimate=pl.CostEstimate(
            flops=0,
            bytes_accessed=0,
            transcendentals=0,
        ),
        name="project",
    )(where, *operands)


def finish(total, squares, gain, columns, model_width, devices):
    clip_count, row_count, lanes = total.shape
    near_rows = row_count // 2

    def kernel(total_ref, squares_ref, gain_ref, features_ref, row_ref):
        clip = pl.program_id(0)
        diagonal = on_diagonal()
        scales = []
        for first in range(0, row_count, LANES):
            at = pl.ds(pl.multiple_of(clip * row_count + first, LANES), LANES)
            mean = jnp.sum(squares_ref[:, :, at], axis=0) / model_width
            scale = jnp.broadcast_to(lax.rsqrt(mean + epsilon), (LANES, LANES))
            scales.append(jnp.sum(jnp.where(diagonal, scale, 0.0), axis=1, keepdims=True))
        scale = jnp.concatenate(scales, axis=0)
        clean = total_ref[0, :near_rows] * scale[:near_rows]
        features_ref[0] = (clean * gain_ref[...]).astype(jnp.bfloat16)
        difference = total_ref[0, near_rows:] * scale[near_rows:] - clean
        sums = jnp.sum(difference * difference, axis=0, keepdims=True)
        penalty = jnp.sum(sums * gain_ref[...] * gain_ref[...], axis=1, keepdims=True)
        lane = lax.broadcasted_iota(jnp.int32, (1, lanes), 1)
        sums = sums + jnp.where(lane == columns + clip, penalty, 0.0)
        sums = jnp.broadcast_to(sums[None], row_ref.shape)

        @pl.when(clip == 0)
        def _():
            row_ref[...] = sums

        @pl.when(clip > 0)
        def _():
            row_ref[...] += sums

    return pl.pallas_call(
        kernel,
        grid=(clip_count,),
        in_specs=[
            pl.BlockSpec((1, row_count, lanes), lambda c: (c, 0, 0)),
            pl.BlockSpec(squares.shape, lambda c: (0, 0, 0)),
            pl.BlockSpec((1, lanes), lambda c: (0, 0)),
        ],
        out_specs=[
            pl.BlockSpec((1, near_rows, lanes), lambda c: (c, 0, 0)),
            pl.BlockSpec((devices, 1, lanes), lambda c: (0, 0, 0)),
        ],
        out_shape=[
            jax.ShapeDtypeStruct((clip_count, near_rows, lanes), jnp.bfloat16),
            jax.ShapeDtypeStruct((devices, 1, lanes), jnp.float32),
        ],
        compiler_params=pltpu.CompilerParams(vmem_limit_bytes=16 * 1024 * 1024),
        name="finish",
    )(total, squares, gain)


def conclude(rows, where, gain, model_count, clip_count, tokens):
    devices, _, lanes = rows.shape
    columns = gain.shape[0] // clip_count
    model_width = gain.shape[0] * model_count
    lane = lax.broadcasted_iota(jnp.int32, rows.shape, 2)
    penalty = jnp.sum(jnp.where(lane == columns + where[2], rows, 0.0))
    penalty = penalty.reshape(1) / (sigma_noise * sigma_noise * tokens * model_width)
    sums = rows.reshape(-1, model_count, clip_count, lanes)[..., :columns]
    model = lax.broadcasted_iota(jnp.int32, sums.shape, 1)
    sums = jnp.sum(jnp.where(model == where[1], sums, 0.0), axis=(0, 1)).reshape(-1)
    return penalty, gain * sums / (sigma_noise * sigma_noise * tokens)


def swap(array, axis, distance):
    count = lax.axis_size(axis)
    return lax.ppermute(array, axis, [(i, i ^ distance) for i in range(count)])


def distances(axis):
    count = lax.axis_size(axis)
    return [(axis, 1 << bit) for bit in reversed(range(count.bit_length() - 1))]


def spread(block, order, before_step):
    stacks = [([(0, 0)], block[None])]
    for step, (axis, distance) in enumerate(order):
        if step < len(order) - 1 and len(stacks) > 1:
            keys = [key for some, _ in stacks for key in some]
            stacks = [(keys, jnp.concatenate([array for _, array in stacks]))]
        received = []
        for part, (keys, array) in enumerate(stacks):
            keys = [(m ^ distance, c) if axis == "mp" else (m, c ^ distance) for m, c in keys]
            received.append((keys, swap(before_step(step, part, array), axis, distance)))
        stacks = stacks + received
    return stacks


def collect(rows, axes):
    return lax.all_to_all(rows, axes, split_axis=0, concat_axis=0, tiled=True)


def pick(options, index):
    return lax.select_n(index, *options) if len(options) > 1 else options[0]


def local(projections, perturbation, out_weight, norm_gain, live_counts):
    tile_len = projections.shape[2]
    local_width = projections.shape[4]
    slots = projections.shape[1]
    slab_count = lax.axis_size("frames")
    slab_index = lax.axis_index("frames")
    model_count = lax.axis_size("mp")
    model_index = lax.axis_index("mp")
    clip_count = lax.axis_size("dp")
    clip_index = lax.axis_index("dp")
    model_width = local_width * model_count
    token_total = slots * slab_count * tile_len
    half = local_width // clip_count
    near_rows = slots * tile_len

    def own_columns(array):
        return pick(
            [array[..., n * half : (n + 1) * half] for n in range(clip_count)], clip_index
        )

    clean = projections[0].transpose(0, 2, 1, 3)
    noise = perturbation[0].transpose(0, 2, 1, 3)
    up = [(i, i + 1) for i in range(slab_count - 1)]
    down = [(i + 1, i) for i in range(slab_count - 1)]

    tail, head = prepare_halo(clean, noise, (slots - 1, 0))
    tail, head, clean, noise, out_weight = lax.optimization_barrier(
        (tail, head, clean, noise, out_weight)
    )
    right = lax.ppermute(head, "frames", down)
    left = lax.ppermute(tail, "frames", up)
    streams = (clean, perturb(clean, noise))
    counts = jnp.pad(live_counts[0], (1, 1))
    nearby = lax.dynamic_slice_in_dim(counts, slots * slab_index, slots + 2)
    where = jnp.concatenate(
        [jnp.stack([slab_index, model_index, clip_index]).astype(jnp.int32), nearby]
    )
    gain_row = jnp.pad(own_columns(norm_gain), (0, whole_lanes(half) - half))[None]

    own_weight = prepare_weight(where, out_weight, clip_count)
    line = slab_count == model_count and slab_count == 4
    last = slab_count - 1
    cut = whole_lanes(half) // 2
    near, passed, across = [], [], []

    if line:
        near = [lax.ppermute(own_weight, "frames", pairs) for pairs in (down, up)]
        across = [
            lax.ppermute(block, "frames", [(0, last), (last, 0)])
            for block in (own_weight[:cut], own_weight[cut:])
        ]

    def before_step(stream, step, part, value):
        nonlocal near, passed, gain_row
        if line and stream == 0 and step == 1:
            value, near, gain_row = lax.optimization_barrier((value, near, gain_row))
            passed = [
                lax.ppermute(near[0], "frames", down[:2]),
                lax.ppermute(near[1], "frames", up[1:]),
            ]
        if line and stream == 1 and step == 1:
            value, across[0] = lax.optimization_barrier((value, across[0]))
        if line and stream == 1 and step == 2 and part == 1:
            value, passed = lax.optimization_barrier((value, passed))
        return value

    gathered = []
    orders = (
        distances("dp") + distances("mp"),
        distances("mp")[:1] + distances("dp") + distances("mp")[1:],
    )
    for n, order in enumerate(orders):
        attended = attention(where, streams[n], left, right, n).reshape(near_rows, local_width)
        gathered.append(
            spread(attended, order, lambda *at, n=n: before_step(n, *at))
        )

    peers = model_count * clip_count
    if line:
        shards = [
            (0, own_weight, lambda slab: slab, lambda slab: slab >= 0),
            (0, near[0], lambda slab: jnp.minimum(slab + 1, last), lambda slab: slab < last),
            (0, near[1], lambda slab: jnp.maximum(slab - 1, 0), lambda slab: slab > 0),
            (0, passed[0], lambda slab: jnp.minimum(slab + 2, last), lambda slab: slab < 2),
            (0, passed[1], lambda slab: jnp.maximum(slab - 2, 0), lambda slab: slab >= 2),
        ]
        for first, block in zip((0, cut), across):
            shards.append(
                (first, block, lambda slab: last - slab, lambda slab: (slab == 0) | (slab == last))
            )
        (total,) = project(where, gathered, shards[:-1], None, half, 0)
        total, squares = project(where, gathered, shards[-1:], total, half, peers)
    else:
        weight = lax.all_gather(own_weight, "frames", axis=1, tiled=True)
        shards = [
            (
                0,
                lax.dynamic_slice_in_dim(weight, m * local_width, local_width, axis=1),
                lambda slab, m=m: m,
                lambda slab: slab >= 0,
            )
            for m in range(model_count)
        ]
        total, squares = project(where, gathered, shards, None, half, peers)

    squares = collect(squares, ("mp", "dp"))
    features, sums = finish(
        total, squares, gain_row, half, model_width, slab_count * model_count * clip_count
    )
    sums = collect(sums, ("frames", "mp", "dp"))

    features = features[..., :half].reshape(clip_count, slots, tile_len, half)
    columns = [pick([features[d] for d in range(clip_count)], clip_index)]
    for distance in range(1, clip_count):
        sent = pick([features[d ^ distance] for d in range(clip_count)], clip_index)
        columns.append(swap(sent, "dp", distance))
    features = jnp.concatenate(
        [
            pick([columns[n ^ d] for d in range(clip_count)], clip_index)
            for n in range(clip_count)
        ],
        axis=-1,
    )[None]
    sums, features = lax.optimization_barrier((sums, features))
    penalty, gain_grad = conclude(
        sums, where, norm_gain, model_count, clip_count, token_total
    )
    return (features, penalty, gain_grad)


def solution(mesh):
    placed = (
        P("dp", "frames", None, None, "mp"),
        P("dp", "frames", None, None, "mp"),
        P("frames", "mp"),
        P("mp"),
        P("dp", None),
    )
    return jax.shard_map(
        local,
        mesh=mesh,
        in_specs=placed,
        out_specs=(P("dp", "frames", None, "mp"), P("dp"), P("mp")),
        check_vma=False,
    )
```

```python
import math

import jax
import jax.numpy as jnp
from jax import lax
from jax.experimental import pallas as pl
from jax.experimental.pallas import tpu as pltpu
from jax.sharding import PartitionSpec as P

HEAD_DIM = 128
HEADS_AT_ONCE = 1
LANES = 128


sigma_noise = 0.25
epsilon = 1e-06


def perturb(clean, noise):
    return (clean.astype(jnp.float32) + sigma_noise * noise.astype(jnp.float32)).astype(jnp.bfloat16)


def prepare_halo(clean, noise, slots):
    _, _, tile_len, width = clean.shape

    def kernel(clean_ref, noise_ref, *refs):
        out_refs, (keep, add, in_sems, out_sems) = refs[: len(slots)], refs[len(slots) :]
        pieces = [(n, slot, part) for n, slot in enumerate(slots) for part in range(2)]
        loads, stores = [], []
        for n, slot, part in pieces:
            for m, (source, target) in enumerate(((clean_ref, keep), (noise_ref, add))):
                loads.append(
                    pltpu.make_async_copy(
                        source.at[slot, 1 + part], target.at[n, part], in_sems.at[n, part, m]
                    )
                )
                loads[-1].start()
        for at, (n, slot, part) in enumerate(pieces):
            loads[2 * at].wait()
            loads[2 * at + 1].wait()
            add[n, part] = perturb(keep[n, part], add[n, part])
            for m, source in enumerate((keep, add)):
                stores.append(
                    pltpu.make_async_copy(
                        source.at[n, part], out_refs[n].at[m, part], out_sems.at[n, part, m]
                    )
                )
                stores[-1].start()
        for store in stores:
            store.wait()

    scratch = pltpu.VMEM((len(slots), 2, tile_len, width), jnp.bfloat16)
    return pl.pallas_call(
        kernel,
        in_specs=[pl.BlockSpec(memory_space=pl.ANY)] * 2,
        out_specs=[pl.BlockSpec(memory_space=pl.ANY)] * len(slots),
        out_shape=[jax.ShapeDtypeStruct((2, 2, tile_len, width), jnp.bfloat16)] * len(slots),
        scratch_shapes=[
            scratch,
            scratch,
            pltpu.SemaphoreType.DMA((len(slots), 2, 2)),
            pltpu.SemaphoreType.DMA((len(slots), 2, 2)),
        ],
        compiler_params=pltpu.CompilerParams(vmem_limit_bytes=60 * 1024 * 1024),
        name="prepare_halo",
    )(clean, noise)


def prepare_weight(where, weight, clip_count, cut):
    depth, width = weight.shape
    half = width // clip_count

    def kernel(where_ref, weight_ref, whole_ref, early_ref, late_ref):
        for clip in range(clip_count):

            @pl.when(where_ref[2] == clip)
            def _():
                begin, end = clip * half, (clip + 1) * half
                for first in range(begin // LANES * LANES, end, LANES):
                    low, high = max(first, begin), min(first + LANES, end)
                    turned = weight_ref[:, pl.ds(first, LANES)].T
                    whole_ref[pl.ds(low - begin, high - low)] = turned[low - first : high - first]

        early_ref[...] = whole_ref[:cut]
        late_ref[...] = whole_ref[cut:]

    return pl.pallas_call(
        kernel,
        in_specs=[
            pl.BlockSpec(memory_space=pltpu.SMEM),
            pl.BlockSpec(memory_space=pltpu.VMEM),
        ],
        out_specs=[pl.BlockSpec(memory_space=pltpu.VMEM)] * 3,
        out_shape=[
            jax.ShapeDtypeStruct((rows, depth), weight.dtype) for rows in (half, cut, half - cut)
        ],
        compiler_params=pltpu.CompilerParams(vmem_limit_bytes=60 * 1024 * 1024),
        name="prepare_weight",
    )(where, weight)


def attend_kernel(where_ref, own_ref, right_ref, left_ref, out_ref):
    slots, _, tile_len, width = own_ref.shape
    key_pos = lax.broadcasted_iota(jnp.int32, (1, 2 * tile_len), 1)
    live = []
    for slot in range(slots):
        own_count = where_ref[4 + slot]
        far_count = where_ref[3 if slot == 0 else slots + 4]
        live.append((key_pos < own_count) | ((key_pos >= tile_len) & (key_pos < tile_len + far_count)))
    row_pos = lax.broadcasted_iota(jnp.int32, (tile_len, 1), 0)
    units = [(slot, head) for head in range(width // HEAD_DIM) for slot in range(slots)]

    scores = []
    for slot, head in units:
        cols = pl.ds(head * HEAD_DIM, HEAD_DIM)
        halo_ref = left_ref if slot == 0 else right_ref
        keys = jnp.concatenate([own_ref[slot, 1, :, cols], halo_ref[0, :, cols]], axis=0)
        raw = lax.dot_general(
            own_ref[slot, 0, :, cols],
            keys,
            (((1,), (1,)), ((), ())),
            preferred_element_type=jnp.float32,
        )
        scores.append(jnp.where(live[slot], raw * (1.0 / math.sqrt(HEAD_DIM)), jnp.float32(-1e30)))
    largest = [jnp.max(s, axis=-1, keepdims=True) for s in scores]
    weights = [jnp.exp(s - top) for s, top in zip(scores, largest)]
    totals = [jnp.sum(w, axis=-1, keepdims=True) for w in weights]
    for (slot, head), weight, total in zip(units, weights, totals):
        cols = pl.ds(head * HEAD_DIM, HEAD_DIM)
        halo_ref = left_ref if slot == 0 else right_ref
        values = jnp.concatenate([own_ref[slot, 2, :, cols], halo_ref[1, :, cols]], axis=0)
        probabilities = (weight * (1.0 / total)).astype(jnp.bfloat16)
        mixed = jnp.dot(probabilities, values, preferred_element_type=jnp.float32)
        out_ref[slot, :, cols] = jnp.where(row_pos < where_ref[4 + slot], mixed, 0.0).astype(
            jnp.bfloat16
        )


def attention(where, own, left, right, stream):
    slots, _, tile_len, width = own.shape
    block = HEADS_AT_ONCE * HEAD_DIM
    own_spec = pl.BlockSpec((slots, 3, tile_len, block), lambda h, c: (0, 0, 0, h))
    halo_spec = pl.BlockSpec((None, 2, tile_len, block), lambda h, c: (stream, 0, 0, h))
    return pl.pallas_call(
        attend_kernel,
        grid_spec=pltpu.PrefetchScalarGridSpec(
            num_scalar_prefetch=1,
            grid=(width // block,),
            in_specs=[own_spec, halo_spec, halo_spec],
            out_specs=pl.BlockSpec((slots, tile_len, block), lambda h, c: (0, 0, h)),
        ),
        out_shape=jax.ShapeDtypeStruct((slots, tile_len, width), jnp.bfloat16),
        compiler_params=pltpu.CompilerParams(vmem_limit_bytes=48 * 1024 * 1024),
        cost_estimate=pl.CostEstimate(
            flops=0,
            bytes_accessed=0,
            transcendentals=0,
        ),
        name="attention",
    )(where, own, right, left)


def whole_lanes(columns):
    return -(-columns // LANES) * LANES


def on_diagonal():
    row = lax.broadcasted_iota(jnp.int32, (LANES, LANES), 0)
    return row == lax.broadcasted_iota(jnp.int32, (LANES, LANES), 1)


def project(where, gathered, shards, total, columns, peers):
    stream_count = len(gathered)
    home = [
        {key: (n, at) for n, (keys, _) in enumerate(stacks) for at, key in enumerate(keys)}
        for stacks in gathered
    ]
    clip_count = 1 + max(clip for _, clip in home[0])
    place_count = 1 + max(place for place, _ in home[0])
    _, block_rows, depth = gathered[0][0][1].shape
    lanes = whole_lanes(columns)
    row_count = stream_count * block_rows
    shard_total = len(shards)
    flat = [array for stacks in gathered for _, array in stacks]
    base = [sum(len(stacks) for stacks in gathered[:n]) for n in range(stream_count)]

    def kernel(where_ref, *refs):
        slab, model, own_clip = where_ref[0], where_ref[1], where_ref[2]
        block_refs = refs[: len(flat)]
        weight_refs = refs[len(flat) : len(flat) + shard_total]
        total_ref = refs[len(flat) + shard_total] if total is not None else None
        rows, held, row_sem, weight_sem = refs[-4:]
        out_ref = refs[len(operands)]
        squares_ref = refs[len(operands) + 1]

        def weight_copy(shard):
            size = shards[shard][1].shape[0]
            return pltpu.make_async_copy(
                weight_refs[shard], held.at[shard, pl.ds(0, size)], weight_sem.at[shard]
            )

        def row_copy(place, shard, clip, stream):
            stack, at = home[stream][place, clip]
            source = block_refs[base[stream] + stack].at[at]
            first = pl.multiple_of(
                (clip ^ own_clip) * row_count + stream * block_rows, 16
            )
            return pltpu.make_async_copy(
                source,
                rows.at[shard, pl.ds(first, block_rows)],
                row_sem.at[shard, clip, stream],
            )

        for shard in range(shard_total):

            @pl.when(shards[shard][3](slab))
            def _():
                weight_copy(shard).start()
                for place in range(place_count):

                    @pl.when((shards[shard][2](slab) ^ model) == place)
                    def _():
                        for clip in range(clip_count):
                            for stream in range(stream_count):
                                row_copy(place, shard, clip, stream).start()

        if total is None:
            out_ref[...] = jnp.zeros_like(out_ref)
        else:
            out_ref[...] = total_ref[...]

        for shard in range(shard_total):

            @pl.when(shards[shard][3](slab))
            def _():
                weight_copy(shard).wait()
                for clip in range(clip_count):
                    for stream in range(stream_count):
                        row_copy(0, shard, clip, stream).wait()
                first, array = shards[shard][:2]
                size = array.shape[0]
                wide = whole_lanes(size)
                if wide > size:
                    held[shard, size:wide] = jnp.zeros((wide - size, depth), held.dtype)
                for clip in range(clip_count):
                    out_ref[clip, :, pl.ds(first, wide)] += lax.dot_general(
                        rows[shard, pl.ds(clip * row_count, row_count)],
                        held[shard, pl.ds(0, wide)],
                        (((1,), (1,)), ((), ())),
                        preferred_element_type=jnp.float32,
                    )

        if peers:
            diagonal = on_diagonal()
            for clip in range(clip_count):
                for first in range(0, row_count, LANES):
                    piece = out_ref[clip, pl.ds(first, LANES)]
                    sums = jnp.sum(piece * piece, axis=1, keepdims=True)
                    sums = jnp.sum(jnp.where(diagonal, sums, 0.0), axis=0, keepdims=True)
                    squares_ref[:, :, pl.ds(clip * row_count + first, LANES)] = jnp.broadcast_to(
                        sums[None], (peers, 1, LANES)
                    )

    operands = [*flat, *(array for _, array, _, _ in shards)]
    in_specs = [pl.BlockSpec(memory_space=pl.ANY) for _ in operands]
    aliases = {}
    if total is not None:
        operands.append(total)
        in_specs.append(pl.BlockSpec(memory_space=pltpu.VMEM))
        aliases = {len(operands): 0}
    out_shape = [jax.ShapeDtypeStruct((clip_count, row_count, lanes), jnp.float32)]
    if peers:
        out_shape.append(jax.ShapeDtypeStruct((peers, 1, clip_count * row_count), jnp.float32))
    return pl.pallas_call(
        kernel,
        in_specs=[pl.BlockSpec(memory_space=pltpu.SMEM)] + in_specs,
        out_specs=[pl.BlockSpec(memory_space=pltpu.VMEM)] * len(out_shape),
        out_shape=out_shape,
        scratch_shapes=[
            pltpu.VMEM((shard_total, clip_count * row_count, depth), jnp.bfloat16),
            pltpu.VMEM((shard_total, lanes, depth), jnp.bfloat16),
            pltpu.SemaphoreType.DMA((shard_total, clip_count, stream_count)),
            pltpu.SemaphoreType.DMA((shard_total,)),
        ],
        input_output_aliases=aliases,
        compiler_params=pltpu.CompilerParams(vmem_limit_bytes=(8 + 4 * shard_total) * 1024 * 1024),
        cost_estimate=pl.CostEstimate(
            flops=0,
            bytes_accessed=0,
            transcendentals=0,
        ),
        name="project",
    )(where, *operands)


def row_scales(squares_ref, clip, row_count, model_width):
    diagonal = on_diagonal()
    scales = []
    for first in range(0, row_count, LANES):
        at = pl.ds(pl.multiple_of(clip * row_count + first, LANES), LANES)
        mean = jnp.sum(squares_ref[:, :, at], axis=0) / model_width
        scale = jnp.broadcast_to(lax.rsqrt(mean + epsilon), (LANES, LANES))
        scales.append(jnp.sum(jnp.where(diagonal, scale, 0.0), axis=1, keepdims=True))
    return jnp.concatenate(scales, axis=0)


def finish(total, squares, gain, columns, model_width, devices):
    clip_count, row_count, lanes = total.shape
    near_rows = row_count // 2

    def kernel(total_ref, squares_ref, gain_ref, row_ref):
        lane = lax.broadcasted_iota(jnp.int32, (1, lanes), 1)
        row = jnp.zeros((1, lanes), jnp.float32)
        for clip in range(clip_count):
            scale = row_scales(squares_ref, clip, row_count, model_width)
            clean = total_ref[clip, :near_rows] * scale[:near_rows]
            difference = total_ref[clip, near_rows:] * scale[near_rows:] - clean
            sums = jnp.sum(difference * difference, axis=0, keepdims=True)
            penalty = jnp.sum(sums * gain_ref[...] * gain_ref[...], axis=1, keepdims=True)
            row = row + sums + jnp.where(lane == columns + clip, penalty, 0.0)
        row_ref[...] = jnp.broadcast_to(row[None], row_ref.shape)

    return pl.pallas_call(
        kernel,
        out_shape=jax.ShapeDtypeStruct((devices, 1, lanes), jnp.float32),
        compiler_params=pltpu.CompilerParams(vmem_limit_bytes=16 * 1024 * 1024),
        name="finish",
    )(total, squares, gain)


def make_features(total, squares, gain, model_width):
    clip_count, row_count, lanes = total.shape
    near_rows = row_count // 2

    def kernel(total_ref, squares_ref, gain_ref, features_ref):
        for clip in range(clip_count):
            scale = row_scales(squares_ref, clip, row_count, model_width)
            clean = total_ref[clip, :near_rows] * scale[:near_rows]
            features_ref[clip] = (clean * gain_ref[...]).astype(jnp.bfloat16)

    return pl.pallas_call(
        kernel,
        out_shape=jax.ShapeDtypeStruct((clip_count, near_rows, lanes), jnp.bfloat16),
        compiler_params=pltpu.CompilerParams(vmem_limit_bytes=16 * 1024 * 1024),
        cost_estimate=pl.CostEstimate(
            flops=10**10, bytes_accessed=0, transcendentals=0
        ),
        name="make_features",
    )(total, squares, gain)


def conclude(rows, where, gain, model_count, clip_count, tokens):
    devices, _, lanes = rows.shape
    columns = gain.shape[1] // clip_count
    model_width = gain.shape[1] * model_count

    def kernel(where_ref, rows_ref, gain_ref, penalty_ref, grad_ref):
        row = lax.broadcasted_iota(jnp.int32, (devices, 1, lanes), 0)
        model = (row // clip_count) % model_count
        sums = []
        for clip in range(clip_count):
            mine = (model == where_ref[1]) & (row % clip_count == clip)
            sums.append(jnp.sum(jnp.where(mine, rows_ref[...], 0.0), axis=0)[:, :columns])
        sums = jnp.concatenate(sums, axis=1)
        grad = gain_ref[...] * sums / (sigma_noise * sigma_noise * tokens)
        grad_ref[...] = grad.reshape(grad_ref.shape)
        lane = lax.broadcasted_iota(jnp.int32, (devices, 1, lanes), 2)
        own = jnp.where(lane == columns + where_ref[2], rows_ref[...], 0.0)
        penalty_ref[0] = jnp.sum(own) / (sigma_noise * sigma_noise * tokens * model_width)

    return pl.pallas_call(
        kernel,
        in_specs=[pl.BlockSpec(memory_space=pltpu.SMEM)]
        + [pl.BlockSpec(memory_space=pltpu.VMEM)] * 2,
        out_specs=[
            pl.BlockSpec(memory_space=pltpu.SMEM),
            pl.BlockSpec(memory_space=pltpu.VMEM),
        ],
        out_shape=[
            jax.ShapeDtypeStruct((1,), jnp.float32),
            jax.ShapeDtypeStruct((gain.shape[1],), jnp.float32),
        ],
        compiler_params=pltpu.CompilerParams(vmem_limit_bytes=60 * 1024 * 1024),
        name="conclude",
    )(where, rows, gain)


def swap(array, axis, distance):
    count = lax.axis_size(axis)
    return lax.ppermute(array, axis, [(i, i ^ distance) for i in range(count)])


def distances(axis):
    count = lax.axis_size(axis)
    return [(axis, 1 << bit) for bit in reversed(range(count.bit_length() - 1))]


def spread(block, order, before_step):
    stacks = [([(0, 0)], block[None])]
    for step, (axis, distance) in enumerate(order):
        if step < len(order) - 1 and len(stacks) > 1:
            keys = [key for some, _ in stacks for key in some]
            stacks = [(keys, jnp.concatenate([array for _, array in stacks]))]
        received = []
        for part, (keys, array) in enumerate(stacks):
            keys = [(m ^ distance, c) if axis == "mp" else (m, c ^ distance) for m, c in keys]
            received.append((keys, swap(before_step(step, part, array), axis, distance)))
        stacks = stacks + received
    return stacks


def collect(rows, axes):
    return lax.all_to_all(rows, axes, split_axis=0, concat_axis=0, tiled=True)


def pick(options, index):
    return lax.select_n(index, *options) if len(options) > 1 else options[0]


def local(projections, perturbation, out_weight, norm_gain, live_counts):
    tile_len = projections.shape[2]
    local_width = projections.shape[4]
    slots = projections.shape[1]
    slab_count = lax.axis_size("frames")
    slab_index = lax.axis_index("frames")
    model_count = lax.axis_size("mp")
    model_index = lax.axis_index("mp")
    clip_count = lax.axis_size("dp")
    clip_index = lax.axis_index("dp")
    model_width = local_width * model_count
    token_total = slots * slab_count * tile_len
    half = local_width // clip_count
    near_rows = slots * tile_len

    def own_columns(array):
        return pick(
            [array[..., n * half : (n + 1) * half] for n in range(clip_count)], clip_index
        )

    clean = projections[0].transpose(0, 2, 1, 3)
    noise = perturbation[0].transpose(0, 2, 1, 3)
    up = [(i, i + 1) for i in range(slab_count - 1)]
    down = [(i + 1, i) for i in range(slab_count - 1)]

    tail, head = prepare_halo(clean, noise, (slots - 1, 0))
    tail, head, clean, noise, out_weight = lax.optimization_barrier(
        (tail, head, clean, noise, out_weight)
    )
    right = lax.ppermute(head, "frames", down)
    left = lax.ppermute(tail, "frames", up)
    streams = (clean, perturb(clean, noise))
    counts = jnp.pad(live_counts[0], (1, 1))
    nearby = lax.dynamic_slice_in_dim(counts, slots * slab_index, slots + 2)
    where = jnp.concatenate(
        [jnp.stack([slab_index, model_index, clip_index]).astype(jnp.int32), nearby]
    )
    gain_row = jnp.pad(own_columns(norm_gain), (0, whole_lanes(half) - half))[None]
    gain_all = norm_gain[None]

    cut = min(LANES, half // 2)
    own_weight, *parts = prepare_weight(where, out_weight, clip_count, cut)
    line = slab_count == model_count and slab_count == 4
    last = slab_count - 1
    near, passed, across = [], [], []

    if line:
        near = [lax.ppermute(own_weight, "frames", pairs) for pairs in (down, up)]
        across = [
            lax.ppermute(block, "frames", [(0, last), (last, 0)]) for block in parts
        ]

    def before_step(stream, step, part, value):
        nonlocal near, passed, gain_row, gain_all
        if line and stream == 0 and step == 1:
            value, near, gain_row, gain_all = lax.optimization_barrier(
                (value, near, gain_row, gain_all)
            )
            passed = [
                lax.ppermute(near[0], "frames", down[:2]),
                lax.ppermute(near[1], "frames", up[1:]),
            ]
        if line and stream == 1 and step == 1:
            value, across[0] = lax.optimization_barrier((value, across[0]))
        if line and stream == 1 and step == 2 and part == 1:
            value, passed = lax.optimization_barrier((value, passed))
        return value

    gathered = []
    orders = (
        distances("dp") + distances("mp"),
        distances("mp")[:1] + distances("dp") + distances("mp")[1:],
    )
    for n, order in enumerate(orders):
        attended = attention(where, streams[n], left, right, n).reshape(near_rows, local_width)
        gathered.append(
            spread(attended, order, lambda *at, n=n: before_step(n, *at))
        )

    peers = model_count * clip_count
    if line:
        shards = [
            (0, own_weight, lambda slab: slab, lambda slab: slab >= 0),
            (0, near[0], lambda slab: jnp.minimum(slab + 1, last), lambda slab: slab < last),
            (0, near[1], lambda slab: jnp.maximum(slab - 1, 0), lambda slab: slab > 0),
            (0, passed[0], lambda slab: jnp.minimum(slab + 2, last), lambda slab: slab < 2),
            (0, passed[1], lambda slab: jnp.maximum(slab - 2, 0), lambda slab: slab >= 2),
        ]
        for first, block in zip((0, cut), across):
            shards.append(
                (first, block, lambda slab: last - slab, lambda slab: (slab == 0) | (slab == last))
            )
        (total,) = project(where, gathered, shards[:-1], None, half, 0)
        total, squares = project(where, gathered, shards[-1:], total, half, peers)
    else:
        weight = lax.all_gather(own_weight, "frames", axis=1, tiled=True)
        shards = [
            (
                0,
                lax.dynamic_slice_in_dim(weight, m * local_width, local_width, axis=1),
                lambda slab, m=m: m,
                lambda slab: slab >= 0,
            )
            for m in range(model_count)
        ]
        total, squares = project(where, gathered, shards, None, half, peers)

    squares = collect(squares, ("mp", "dp"))
    sums = finish(
        total, squares, gain_row, half, model_width, slab_count * model_count * clip_count
    )
    features = make_features(total, squares, gain_row, model_width)
    sums = collect(sums, ("frames", "mp", "dp"))

    features = features[..., :half].reshape(clip_count, slots, tile_len, half)
    columns = [pick([features[d] for d in range(clip_count)], clip_index)]
    for distance in range(1, clip_count):
        sent = pick([features[d ^ distance] for d in range(clip_count)], clip_index)
        columns.append(swap(sent, "dp", distance))
    features = jnp.concatenate(
        [
            pick([columns[n ^ d] for d in range(clip_count)], clip_index)
            for n in range(clip_count)
        ],
        axis=-1,
    )[None]
    sums, features = lax.optimization_barrier((sums, features))
    penalty, gain_grad = conclude(
        sums, where, gain_all, model_count, clip_count, token_total
    )
    return (features, penalty, gain_grad)


def solution(mesh):
    placed = (
        P("dp", "frames", None, None, "mp"),
        P("dp", "frames", None, None, "mp"),
        P("frames", "mp"),
        P("mp"),
        P("dp", None),
    )
    return jax.shard_map(
        local,
        mesh=mesh,
        in_specs=placed,
        out_specs=(P("dp", "frames", None, "mp"), P("dp"), P("mp")),
        check_vma=False,
    )
```

```python
import math

import jax
import jax.numpy as jnp
from jax import lax
from jax.experimental import pallas as pl
from jax.experimental.pallas import tpu as pltpu
from jax.sharding import PartitionSpec as P

HEAD_DIM = 128
HEADS_AT_ONCE = 1
LANES = 128


sigma_noise = 0.25
epsilon = 1e-06


def perturb(clean, noise):
    return (clean.astype(jnp.float32) + sigma_noise * noise.astype(jnp.float32)).astype(jnp.bfloat16)


def prepare_halo(clean, noise, slots):
    _, _, tile_len, width = clean.shape

    def kernel(clean_ref, noise_ref, *refs):
        out_refs, (keep, add, in_sems, out_sems) = refs[: len(slots)], refs[len(slots) :]
        pieces = [(n, slot, part) for n, slot in enumerate(slots) for part in range(2)]
        loads, stores = [], []
        for n, slot, part in pieces:
            for m, (source, target) in enumerate(((clean_ref, keep), (noise_ref, add))):
                loads.append(
                    pltpu.make_async_copy(
                        source.at[slot, 1 + part], target.at[n, part], in_sems.at[n, part, m]
                    )
                )
                loads[-1].start()
        for at, (n, slot, part) in enumerate(pieces):
            loads[2 * at].wait()
            loads[2 * at + 1].wait()
            add[n, part] = perturb(keep[n, part], add[n, part])
            for m, source in enumerate((keep, add)):
                stores.append(
                    pltpu.make_async_copy(
                        source.at[n, part], out_refs[n].at[m, part], out_sems.at[n, part, m]
                    )
                )
                stores[-1].start()
        for store in stores:
            store.wait()

    scratch = pltpu.VMEM((len(slots), 2, tile_len, width), jnp.bfloat16)
    return pl.pallas_call(
        kernel,
        in_specs=[pl.BlockSpec(memory_space=pl.ANY)] * 2,
        out_specs=[pl.BlockSpec(memory_space=pl.ANY)] * len(slots),
        out_shape=[jax.ShapeDtypeStruct((2, 2, tile_len, width), jnp.bfloat16)] * len(slots),
        scratch_shapes=[
            scratch,
            scratch,
            pltpu.SemaphoreType.DMA((len(slots), 2, 2)),
            pltpu.SemaphoreType.DMA((len(slots), 2, 2)),
        ],
        compiler_params=pltpu.CompilerParams(vmem_limit_bytes=60 * 1024 * 1024),
        name="prepare_halo",
    )(clean, noise)


def prepare_weight(where, weight, clip_count, cut):
    depth, width = weight.shape
    half = width // clip_count

    def kernel(where_ref, weight_ref, whole_ref, early_ref, late_ref):
        for clip in range(clip_count):

            @pl.when(where_ref[2] == clip)
            def _():
                begin, end = clip * half, (clip + 1) * half
                for first in range(begin // LANES * LANES, end, LANES):
                    low, high = max(first, begin), min(first + LANES, end)
                    turned = weight_ref[:, pl.ds(first, LANES)].T
                    whole_ref[pl.ds(low - begin, high - low)] = turned[low - first : high - first]

        early_ref[...] = whole_ref[:cut]
        late_ref[...] = whole_ref[cut:]

    return pl.pallas_call(
        kernel,
        in_specs=[
            pl.BlockSpec(memory_space=pltpu.SMEM),
            pl.BlockSpec(memory_space=pltpu.VMEM),
        ],
        out_specs=[pl.BlockSpec(memory_space=pltpu.VMEM)] * 3,
        out_shape=[
            jax.ShapeDtypeStruct((rows, depth), weight.dtype) for rows in (half, cut, half - cut)
        ],
        compiler_params=pltpu.CompilerParams(vmem_limit_bytes=60 * 1024 * 1024),
        name="prepare_weight",
    )(where, weight)


def attend_kernel(where_ref, own_ref, right_ref, left_ref, out_ref):
    slots, _, tile_len, width = own_ref.shape
    key_pos = lax.broadcasted_iota(jnp.int32, (1, 2 * tile_len), 1)
    live = []
    for slot in range(slots):
        own_count = where_ref[4 + slot]
        far_count = where_ref[3 if slot == 0 else slots + 4]
        live.append((key_pos < own_count) | ((key_pos >= tile_len) & (key_pos < tile_len + far_count)))
    row_pos = lax.broadcasted_iota(jnp.int32, (tile_len, 1), 0)
    units = [(slot, head) for head in range(width // HEAD_DIM) for slot in range(slots)]

    scores = []
    for slot, head in units:
        cols = pl.ds(head * HEAD_DIM, HEAD_DIM)
        halo_ref = left_ref if slot == 0 else right_ref
        keys = jnp.concatenate([own_ref[slot, 1, :, cols], halo_ref[0, :, cols]], axis=0)
        raw = lax.dot_general(
            own_ref[slot, 0, :, cols],
            keys,
            (((1,), (1,)), ((), ())),
            preferred_element_type=jnp.float32,
        )
        scores.append(jnp.where(live[slot], raw * (1.0 / math.sqrt(HEAD_DIM)), jnp.float32(-1e30)))
    largest = [jnp.max(s, axis=-1, keepdims=True) for s in scores]
    weights = [jnp.exp(s - top) for s, top in zip(scores, largest)]
    totals = [jnp.sum(w, axis=-1, keepdims=True) for w in weights]
    for (slot, head), weight, total in zip(units, weights, totals):
        cols = pl.ds(head * HEAD_DIM, HEAD_DIM)
        halo_ref = left_ref if slot == 0 else right_ref
        values = jnp.concatenate([own_ref[slot, 2, :, cols], halo_ref[1, :, cols]], axis=0)
        probabilities = (weight * (1.0 / total)).astype(jnp.bfloat16)
        mixed = jnp.dot(probabilities, values, preferred_element_type=jnp.float32)
        out_ref[slot, :, cols] = jnp.where(row_pos < where_ref[4 + slot], mixed, 0.0).astype(
            jnp.bfloat16
        )


def attention(where, own, left, right, stream):
    slots, _, tile_len, width = own.shape
    block = HEADS_AT_ONCE * HEAD_DIM
    own_spec = pl.BlockSpec((slots, 3, tile_len, block), lambda h, c: (0, 0, 0, h))
    halo_spec = pl.BlockSpec((None, 2, tile_len, block), lambda h, c: (stream, 0, 0, h))
    return pl.pallas_call(
        attend_kernel,
        grid_spec=pltpu.PrefetchScalarGridSpec(
            num_scalar_prefetch=1,
            grid=(width // block,),
            in_specs=[own_spec, halo_spec, halo_spec],
            out_specs=pl.BlockSpec((slots, tile_len, block), lambda h, c: (0, 0, h)),
        ),
        out_shape=jax.ShapeDtypeStruct((slots, tile_len, width), jnp.bfloat16),
        compiler_params=pltpu.CompilerParams(vmem_limit_bytes=48 * 1024 * 1024),
        cost_estimate=pl.CostEstimate(
            flops=0,
            bytes_accessed=0,
            transcendentals=0,
        ),
        name="attention",
    )(where, own, right, left)


def whole_lanes(columns):
    return -(-columns // LANES) * LANES


def on_diagonal():
    row = lax.broadcasted_iota(jnp.int32, (LANES, LANES), 0)
    return row == lax.broadcasted_iota(jnp.int32, (LANES, LANES), 1)


def project(where, gathered, shards, total, columns, peers):
    stream_count = len(gathered)
    home = [
        {key: (n, at) for n, (keys, _) in enumerate(stacks) for at, key in enumerate(keys)}
        for stacks in gathered
    ]
    clip_count = 1 + max(clip for _, clip in home[0])
    place_count = 1 + max(place for place, _ in home[0])
    _, block_rows, depth = gathered[0][0][1].shape
    lanes = whole_lanes(columns)
    row_count = stream_count * block_rows
    shard_total = len(shards)
    flat = [array for stacks in gathered for _, array in stacks]
    base = [sum(len(stacks) for stacks in gathered[:n]) for n in range(stream_count)]

    def kernel(where_ref, *refs):
        slab, model, own_clip = where_ref[0], where_ref[1], where_ref[2]
        block_refs = refs[: len(flat)]
        weight_refs = refs[len(flat) : len(flat) + shard_total]
        total_ref = refs[len(flat) + shard_total] if total is not None else None
        rows, held, row_sem, weight_sem = refs[-4:]
        out_ref = refs[len(operands)]
        squares_ref = refs[len(operands) + 1]

        def weight_copy(shard):
            size = shards[shard][1].shape[0]
            return pltpu.make_async_copy(
                weight_refs[shard], held.at[shard, pl.ds(0, size)], weight_sem.at[shard]
            )

        def row_copy(place, shard, clip, stream):
            stack, at = home[stream][place, clip]
            source = block_refs[base[stream] + stack].at[at]
            first = pl.multiple_of(
                (clip ^ own_clip) * row_count + stream * block_rows, 16
            )
            return pltpu.make_async_copy(
                source,
                rows.at[shard, pl.ds(first, block_rows)],
                row_sem.at[shard, clip, stream],
            )

        for shard in range(shard_total):

            @pl.when(shards[shard][3](slab))
            def _():
                weight_copy(shard).start()
                for place in range(place_count):

                    @pl.when((shards[shard][2](slab) ^ model) == place)
                    def _():
                        for clip in range(clip_count):
                            for stream in range(stream_count):
                                row_copy(place, shard, clip, stream).start()

        if total is None:
            out_ref[...] = jnp.zeros_like(out_ref)
        else:
            out_ref[...] = total_ref[...]

        for shard in range(shard_total):

            @pl.when(shards[shard][3](slab))
            def _():
                weight_copy(shard).wait()
                for clip in range(clip_count):
                    for stream in range(stream_count):
                        row_copy(0, shard, clip, stream).wait()
                first, array = shards[shard][:2]
                size = array.shape[0]
                wide = whole_lanes(size)
                if wide > size:
                    held[shard, size:wide] = jnp.zeros((wide - size, depth), held.dtype)
                for clip in range(clip_count):
                    out_ref[clip, :, pl.ds(first, wide)] += lax.dot_general(
                        rows[shard, pl.ds(clip * row_count, row_count)],
                        held[shard, pl.ds(0, wide)],
                        (((1,), (1,)), ((), ())),
                        preferred_element_type=jnp.float32,
                    )

        if peers:
            diagonal = on_diagonal()
            for clip in range(clip_count):
                for first in range(0, row_count, LANES):
                    piece = out_ref[clip, pl.ds(first, LANES)]
                    sums = jnp.sum(piece * piece, axis=1, keepdims=True)
                    sums = jnp.sum(jnp.where(diagonal, sums, 0.0), axis=0, keepdims=True)
                    squares_ref[:, :, pl.ds(clip * row_count + first, LANES)] = jnp.broadcast_to(
                        sums[None], (peers, 1, LANES)
                    )

    operands = [*flat, *(array for _, array, _, _ in shards)]
    in_specs = [pl.BlockSpec(memory_space=pl.ANY) for _ in operands]
    aliases = {}
    if total is not None:
        operands.append(total)
        in_specs.append(pl.BlockSpec(memory_space=pltpu.VMEM))
        aliases = {len(operands): 0}
    out_shape = [jax.ShapeDtypeStruct((clip_count, row_count, lanes), jnp.float32)]
    if peers:
        out_shape.append(jax.ShapeDtypeStruct((peers, 1, clip_count * row_count), jnp.float32))
    return pl.pallas_call(
        kernel,
        in_specs=[pl.BlockSpec(memory_space=pltpu.SMEM)] + in_specs,
        out_specs=[pl.BlockSpec(memory_space=pltpu.VMEM)] * len(out_shape),
        out_shape=out_shape,
        scratch_shapes=[
            pltpu.VMEM((shard_total, clip_count * row_count, depth), jnp.bfloat16),
            pltpu.VMEM((shard_total, lanes, depth), jnp.bfloat16),
            pltpu.SemaphoreType.DMA((shard_total, clip_count, stream_count)),
            pltpu.SemaphoreType.DMA((shard_total,)),
        ],
        input_output_aliases=aliases,
        compiler_params=pltpu.CompilerParams(vmem_limit_bytes=(8 + 4 * shard_total) * 1024 * 1024),
        cost_estimate=pl.CostEstimate(
            flops=0,
            bytes_accessed=0,
            transcendentals=0,
        ),
        name="project",
    )(where, *operands)


def row_scales(squares_ref, clip, row_count, model_width):
    diagonal = on_diagonal()
    scales = []
    for first in range(0, row_count, LANES):
        at = pl.ds(pl.multiple_of(clip * row_count + first, LANES), LANES)
        mean = jnp.sum(squares_ref[:, :, at], axis=0) / model_width
        scale = jnp.broadcast_to(lax.rsqrt(mean + epsilon), (LANES, LANES))
        scales.append(jnp.sum(jnp.where(diagonal, scale, 0.0), axis=1, keepdims=True))
    return jnp.concatenate(scales, axis=0)


def finish(total, squares, gain, columns, model_width, devices):
    clip_count, row_count, lanes = total.shape
    near_rows = row_count // 2

    def kernel(total_ref, squares_ref, gain_ref, row_ref):
        lane = lax.broadcasted_iota(jnp.int32, (1, lanes), 1)
        row = jnp.zeros((1, lanes), jnp.float32)
        for clip in range(clip_count):
            scale = row_scales(squares_ref, clip, row_count, model_width)
            clean = total_ref[clip, :near_rows] * scale[:near_rows]
            difference = total_ref[clip, near_rows:] * scale[near_rows:] - clean
            sums = jnp.sum(difference * difference, axis=0, keepdims=True)
            penalty = jnp.sum(sums * gain_ref[...] * gain_ref[...], axis=1, keepdims=True)
            row = row + sums + jnp.where(lane == columns + clip, penalty, 0.0)
        row_ref[...] = jnp.broadcast_to(row[None], row_ref.shape)

    return pl.pallas_call(
        kernel,
        out_shape=jax.ShapeDtypeStruct((devices, 1, lanes), jnp.float32),
        compiler_params=pltpu.CompilerParams(vmem_limit_bytes=16 * 1024 * 1024),
        name="finish",
    )(total, squares, gain)


def make_features(total, squares, gain, model_width):
    clip_count, row_count, lanes = total.shape
    near_rows = row_count // 2

    def kernel(total_ref, squares_ref, gain_ref, features_ref):
        for clip in range(clip_count):
            scale = row_scales(squares_ref, clip, row_count, model_width)
            clean = total_ref[clip, :near_rows] * scale[:near_rows]
            features_ref[clip] = (clean * gain_ref[...]).astype(jnp.bfloat16)

    return pl.pallas_call(
        kernel,
        out_shape=jax.ShapeDtypeStruct((clip_count, near_rows, lanes), jnp.bfloat16),
        compiler_params=pltpu.CompilerParams(vmem_limit_bytes=16 * 1024 * 1024),
        cost_estimate=pl.CostEstimate(
            flops=10**10, bytes_accessed=0, transcendentals=0
        ),
        name="make_features",
    )(total, squares, gain)


def conclude(rows, where, gain, model_count, clip_count, tokens):
    devices, _, lanes = rows.shape
    columns = gain.shape[1] // clip_count
    model_width = gain.shape[1] * model_count

    def kernel(where_ref, rows_ref, gain_ref, penalty_ref, grad_ref):
        row = lax.broadcasted_iota(jnp.int32, (devices, 1, lanes), 0)
        model = (row // clip_count) % model_count
        sums = []
        for clip in range(clip_count):
            mine = (model == where_ref[1]) & (row % clip_count == clip)
            sums.append(jnp.sum(jnp.where(mine, rows_ref[...], 0.0), axis=0)[:, :columns])
        sums = jnp.concatenate(sums, axis=1)
        grad = gain_ref[...] * sums / (sigma_noise * sigma_noise * tokens)
        grad_ref[...] = grad.reshape(grad_ref.shape)
        lane = lax.broadcasted_iota(jnp.int32, (devices, 1, lanes), 2)
        own = jnp.where(lane == columns + where_ref[2], rows_ref[...], 0.0)
        penalty_ref[0] = jnp.sum(own) / (sigma_noise * sigma_noise * tokens * model_width)

    return pl.pallas_call(
        kernel,
        in_specs=[pl.BlockSpec(memory_space=pltpu.SMEM)]
        + [pl.BlockSpec(memory_space=pltpu.VMEM)] * 2,
        out_specs=[
            pl.BlockSpec(memory_space=pltpu.SMEM),
            pl.BlockSpec(memory_space=pltpu.VMEM),
        ],
        out_shape=[
            jax.ShapeDtypeStruct((1,), jnp.float32),
            jax.ShapeDtypeStruct((gain.shape[1],), jnp.float32),
        ],
        compiler_params=pltpu.CompilerParams(vmem_limit_bytes=60 * 1024 * 1024),
        name="conclude",
    )(where, rows, gain)


def swap(array, axis, distance):
    count = lax.axis_size(axis)
    return lax.ppermute(array, axis, [(i, i ^ distance) for i in range(count)])


def distances(axis):
    count = lax.axis_size(axis)
    return [(axis, 1 << bit) for bit in reversed(range(count.bit_length() - 1))]


def spread(block, order, before_step):
    stacks = [([(0, 0)], block[None])]
    for step, (axis, distance) in enumerate(order):
        if step < len(order) - 1 and len(stacks) > 1:
            keys = [key for some, _ in stacks for key in some]
            stacks = [(keys, jnp.concatenate([array for _, array in stacks]))]
        received = []
        for part, (keys, array) in enumerate(stacks):
            keys = [(m ^ distance, c) if axis == "mp" else (m, c ^ distance) for m, c in keys]
            received.append((keys, swap(before_step(step, part, array), axis, distance)))
        stacks = stacks + received
    return stacks


def collect(rows, axes):
    return lax.all_to_all(rows, axes, split_axis=0, concat_axis=0, tiled=True)


def pick(options, index):
    return lax.select_n(index, *options) if len(options) > 1 else options[0]


def local(projections, perturbation, out_weight, norm_gain, live_counts):
    tile_len = projections.shape[2]
    local_width = projections.shape[4]
    slots = projections.shape[1]
    slab_count = lax.axis_size("frames")
    slab_index = lax.axis_index("frames")
    model_count = lax.axis_size("mp")
    model_index = lax.axis_index("mp")
    clip_count = lax.axis_size("dp")
    clip_index = lax.axis_index("dp")
    model_width = local_width * model_count
    token_total = slots * slab_count * tile_len
    half = local_width // clip_count
    near_rows = slots * tile_len

    def own_columns(array):
        return pick(
            [array[..., n * half : (n + 1) * half] for n in range(clip_count)], clip_index
        )

    clean = projections[0].transpose(0, 2, 1, 3)
    noise = perturbation[0].transpose(0, 2, 1, 3)
    up = [(i, i + 1) for i in range(slab_count - 1)]
    down = [(i + 1, i) for i in range(slab_count - 1)]

    tail, head = prepare_halo(clean, noise, (slots - 1, 0))
    tail, head, clean, noise, out_weight = lax.optimization_barrier(
        (tail, head, clean, noise, out_weight)
    )
    right = lax.ppermute(head, "frames", down)
    left = lax.ppermute(tail, "frames", up)
    streams = (clean, perturb(clean, noise))
    counts = jnp.pad(live_counts[0], (1, 1))
    nearby = lax.dynamic_slice_in_dim(counts, slots * slab_index, slots + 2)
    where = jnp.concatenate(
        [jnp.stack([slab_index, model_index, clip_index]).astype(jnp.int32), nearby]
    )
    gain_row = jnp.pad(own_columns(norm_gain), (0, whole_lanes(half) - half))[None]
    gain_all = norm_gain[None]

    cut = whole_lanes(half) // 2
    own_weight, *parts = prepare_weight(where, out_weight, clip_count, cut)
    line = slab_count == model_count and slab_count == 4
    last = slab_count - 1
    near, passed, across = [], [], []

    if line:
        near = [lax.ppermute(own_weight, "frames", pairs) for pairs in (down, up)]
        across = [
            lax.ppermute(block, "frames", [(0, last), (last, 0)]) for block in parts
        ]

    def before_step(stream, step, part, value):
        nonlocal near, passed, gain_row, gain_all
        if line and stream == 0 and step == 1:
            value, near, gain_row, gain_all = lax.optimization_barrier(
                (value, near, gain_row, gain_all)
            )
            passed = [
                lax.ppermute(near[0], "frames", down[:2]),
                lax.ppermute(near[1], "frames", up[1:]),
            ]
        if line and stream == 1 and step == 1:
            value, across[0] = lax.optimization_barrier((value, across[0]))
        if line and step == 2:
            value, across[1] = lax.optimization_barrier((value, across[1]))
        return value

    gathered = []
    orders = (
        distances("dp") + distances("mp"),
        distances("mp")[:1] + distances("dp") + distances("mp")[1:],
    )
    for n, order in enumerate(orders):
        attended = attention(where, streams[n], left, right, n).reshape(near_rows, local_width)
        gathered.append(
            spread(attended, order, lambda *at, n=n: before_step(n, *at))
        )

    peers = model_count * clip_count
    if line:
        shards = [
            (0, own_weight, lambda slab: slab, lambda slab: slab >= 0),
            (0, near[0], lambda slab: jnp.minimum(slab + 1, last), lambda slab: slab < last),
            (0, near[1], lambda slab: jnp.maximum(slab - 1, 0), lambda slab: slab > 0),
        ]
        for first, block in zip((0, cut), across):
            shards.append(
                (first, block, lambda slab: last - slab, lambda slab: (slab == 0) | (slab == last))
            )
        shards += [
            (0, passed[0], lambda slab: jnp.minimum(slab + 2, last), lambda slab: slab < 2),
            (0, passed[1], lambda slab: jnp.maximum(slab - 2, 0), lambda slab: slab >= 2),
        ]
        (total,) = project(where, gathered, shards[:-2], None, half, 0)
        total, squares = project(where, gathered, shards[-2:], total, half, peers)
    else:
        weight = lax.all_gather(own_weight, "frames", axis=1, tiled=True)
        shards = [
            (
                0,
                lax.dynamic_slice_in_dim(weight, m * local_width, local_width, axis=1),
                lambda slab, m=m: m,
                lambda slab: slab >= 0,
            )
            for m in range(model_count)
        ]
        total, squares = project(where, gathered, shards, None, half, peers)

    squares = collect(squares, ("mp", "dp"))
    sums = finish(
        total, squares, gain_row, half, model_width, slab_count * model_count * clip_count
    )
    features = make_features(total, squares, gain_row, model_width)
    sums = collect(sums, ("frames", "mp", "dp"))

    features = features[..., :half].reshape(clip_count, slots, tile_len, half)
    columns = [pick([features[d] for d in range(clip_count)], clip_index)]
    for distance in range(1, clip_count):
        sent = pick([features[d ^ distance] for d in range(clip_count)], clip_index)
        columns.append(swap(sent, "dp", distance))
    features = jnp.concatenate(
        [
            pick([columns[n ^ d] for d in range(clip_count)], clip_index)
            for n in range(clip_count)
        ],
        axis=-1,
    )[None]
    sums, features = lax.optimization_barrier((sums, features))
    penalty, gain_grad = conclude(
        sums, where, gain_all, model_count, clip_count, token_total
    )
    return (features, penalty, gain_grad)


def solution(mesh):
    placed = (
        P("dp", "frames", None, None, "mp"),
        P("dp", "frames", None, None, "mp"),
        P("frames", "mp"),
        P("mp"),
        P("dp", None),
    )
    return jax.shard_map(
        local,
        mesh=mesh,
        in_specs=placed,
        out_specs=(P("dp", "frames", None, "mp"), P("dp"), P("mp")),
        check_vma=False,
    )
```

```python
import math

import jax
import jax.numpy as jnp
from jax import lax
from jax.experimental import pallas as pl
from jax.experimental.pallas import tpu as pltpu
from jax.sharding import PartitionSpec as P

HEAD_DIM = 128
HEADS_AT_ONCE = 1
LANES = 128


sigma_noise = 0.25
epsilon = 1e-06


def perturb(clean, noise):
    return (clean.astype(jnp.float32) + sigma_noise * noise.astype(jnp.float32)).astype(jnp.bfloat16)


def prepare_halo(clean, noise, slots):
    _, _, tile_len, width = clean.shape

    def kernel(clean_ref, noise_ref, *refs):
        out_refs, (keep, add, in_sems, out_sems) = refs[: len(slots)], refs[len(slots) :]
        pieces = [(n, slot, part) for n, slot in enumerate(slots) for part in range(2)]
        loads, stores = [], []
        for n, slot, part in pieces:
            for m, (source, target) in enumerate(((clean_ref, keep), (noise_ref, add))):
                loads.append(
                    pltpu.make_async_copy(
                        source.at[slot, 1 + part], target.at[n, part], in_sems.at[n, part, m]
                    )
                )
                loads[-1].start()
        for at, (n, slot, part) in enumerate(pieces):
            loads[2 * at].wait()
            loads[2 * at + 1].wait()
            add[n, part] = perturb(keep[n, part], add[n, part])
            for m, source in enumerate((keep, add)):
                stores.append(
                    pltpu.make_async_copy(
                        source.at[n, part], out_refs[n].at[m, part], out_sems.at[n, part, m]
                    )
                )
                stores[-1].start()
        for store in stores:
            store.wait()

    scratch = pltpu.VMEM((len(slots), 2, tile_len, width), jnp.bfloat16)
    return pl.pallas_call(
        kernel,
        in_specs=[pl.BlockSpec(memory_space=pl.ANY)] * 2,
        out_specs=[pl.BlockSpec(memory_space=pl.ANY)] * len(slots),
        out_shape=[jax.ShapeDtypeStruct((2, 2, tile_len, width), jnp.bfloat16)] * len(slots),
        scratch_shapes=[
            scratch,
            scratch,
            pltpu.SemaphoreType.DMA((len(slots), 2, 2)),
            pltpu.SemaphoreType.DMA((len(slots), 2, 2)),
        ],
        compiler_params=pltpu.CompilerParams(vmem_limit_bytes=60 * 1024 * 1024),
        name="prepare_halo",
    )(clean, noise)


def prepare_weight(where, weight, clip_count, cut):
    depth, width = weight.shape
    half = width // clip_count

    def kernel(where_ref, weight_ref, whole_ref, early_ref, late_ref):
        for clip in range(clip_count):

            @pl.when(where_ref[2] == clip)
            def _():
                begin, end = clip * half, (clip + 1) * half
                for first in range(begin // LANES * LANES, end, LANES):
                    low, high = max(first, begin), min(first + LANES, end)
                    turned = weight_ref[:, pl.ds(first, LANES)].T
                    whole_ref[pl.ds(low - begin, high - low)] = turned[low - first : high - first]

        early_ref[...] = whole_ref[:cut]
        late_ref[...] = whole_ref[cut:]

    return pl.pallas_call(
        kernel,
        in_specs=[
            pl.BlockSpec(memory_space=pltpu.SMEM),
            pl.BlockSpec(memory_space=pltpu.VMEM),
        ],
        out_specs=[pl.BlockSpec(memory_space=pltpu.VMEM)] * 3,
        out_shape=[
            jax.ShapeDtypeStruct((rows, depth), weight.dtype) for rows in (half, cut, half - cut)
        ],
        compiler_params=pltpu.CompilerParams(vmem_limit_bytes=60 * 1024 * 1024),
        name="prepare_weight",
    )(where, weight)


def attend_kernel(where_ref, own_ref, right_ref, left_ref, out_ref):
    slots, _, tile_len, width = own_ref.shape
    key_pos = lax.broadcasted_iota(jnp.int32, (1, 2 * tile_len), 1)
    live = []
    for slot in range(slots):
        own_count = where_ref[4 + slot]
        far_count = where_ref[3 if slot == 0 else slots + 4]
        live.append((key_pos < own_count) | ((key_pos >= tile_len) & (key_pos < tile_len + far_count)))
    row_pos = lax.broadcasted_iota(jnp.int32, (tile_len, 1), 0)
    units = [(slot, head) for head in range(width // HEAD_DIM) for slot in range(slots)]

    scores = []
    for slot, head in units:
        cols = pl.ds(head * HEAD_DIM, HEAD_DIM)
        halo_ref = left_ref if slot == 0 else right_ref
        keys = jnp.concatenate([own_ref[slot, 1, :, cols], halo_ref[0, :, cols]], axis=0)
        raw = lax.dot_general(
            own_ref[slot, 0, :, cols],
            keys,
            (((1,), (1,)), ((), ())),
            preferred_element_type=jnp.float32,
        )
        scores.append(jnp.where(live[slot], raw * (1.0 / math.sqrt(HEAD_DIM)), jnp.float32(-1e30)))
    largest = [jnp.max(s, axis=-1, keepdims=True) for s in scores]
    weights = [jnp.exp(s - top) for s, top in zip(scores, largest)]
    totals = [jnp.sum(w, axis=-1, keepdims=True) for w in weights]
    for (slot, head), weight, total in zip(units, weights, totals):
        cols = pl.ds(head * HEAD_DIM, HEAD_DIM)
        halo_ref = left_ref if slot == 0 else right_ref
        values = jnp.concatenate([own_ref[slot, 2, :, cols], halo_ref[1, :, cols]], axis=0)
        probabilities = (weight * (1.0 / total)).astype(jnp.bfloat16)
        mixed = jnp.dot(probabilities, values, preferred_element_type=jnp.float32)
        out_ref[slot, :, cols] = jnp.where(row_pos < where_ref[4 + slot], mixed, 0.0).astype(
            jnp.bfloat16
        )


def attention(where, own, left, right, stream):
    slots, _, tile_len, width = own.shape
    block = HEADS_AT_ONCE * HEAD_DIM
    own_spec = pl.BlockSpec((slots, 3, tile_len, block), lambda h, c: (0, 0, 0, h))
    halo_spec = pl.BlockSpec((None, 2, tile_len, block), lambda h, c: (stream, 0, 0, h))
    return pl.pallas_call(
        attend_kernel,
        grid_spec=pltpu.PrefetchScalarGridSpec(
            num_scalar_prefetch=1,
            grid=(width // block,),
            in_specs=[own_spec, halo_spec, halo_spec],
            out_specs=pl.BlockSpec((slots, tile_len, block), lambda h, c: (0, 0, h)),
        ),
        out_shape=jax.ShapeDtypeStruct((slots, tile_len, width), jnp.bfloat16),
        compiler_params=pltpu.CompilerParams(vmem_limit_bytes=48 * 1024 * 1024),
        cost_estimate=pl.CostEstimate(
            flops=0,
            bytes_accessed=0,
            transcendentals=0,
        ),
        name="attention",
    )(where, own, right, left)


def whole_lanes(columns):
    return -(-columns // LANES) * LANES


def on_diagonal():
    row = lax.broadcasted_iota(jnp.int32, (LANES, LANES), 0)
    return row == lax.broadcasted_iota(jnp.int32, (LANES, LANES), 1)


def project(where, gathered, shards, total, columns, peers):
    stream_count = len(gathered)
    home = [
        {key: (n, at) for n, (keys, _) in enumerate(stacks) for at, key in enumerate(keys)}
        for stacks in gathered
    ]
    clip_count = 1 + max(clip for _, clip in home[0])
    place_count = 1 + max(place for place, _ in home[0])
    _, block_rows, depth = gathered[0][0][1].shape
    lanes = whole_lanes(columns)
    row_count = stream_count * block_rows
    shard_total = len(shards)
    flat = [array for stacks in gathered for _, array in stacks]
    base = [sum(len(stacks) for stacks in gathered[:n]) for n in range(stream_count)]

    def kernel(where_ref, *refs):
        slab, model, own_clip = where_ref[0], where_ref[1], where_ref[2]
        block_refs = refs[: len(flat)]
        weight_refs = refs[len(flat) : len(flat) + shard_total]
        total_ref = refs[len(flat) + shard_total] if total is not None else None
        rows, held, row_sem, weight_sem = refs[-4:]
        out_ref = refs[len(operands)]
        squares_ref = refs[len(operands) + 1]

        def weight_copy(shard):
            size = shards[shard][1].shape[0]
            return pltpu.make_async_copy(
                weight_refs[shard], held.at[shard, pl.ds(0, size)], weight_sem.at[shard]
            )

        def row_copy(place, shard, clip, stream):
            stack, at = home[stream][place, clip]
            source = block_refs[base[stream] + stack].at[at]
            first = pl.multiple_of(
                (clip ^ own_clip) * row_count + stream * block_rows, 16
            )
            return pltpu.make_async_copy(
                source,
                rows.at[shard, pl.ds(first, block_rows)],
                row_sem.at[shard, clip, stream],
            )

        for shard in range(shard_total):

            @pl.when(shards[shard][3](slab))
            def _():
                weight_copy(shard).start()
                for place in range(place_count):

                    @pl.when((shards[shard][2](slab) ^ model) == place)
                    def _():
                        for clip in range(clip_count):
                            for stream in range(stream_count):
                                row_copy(place, shard, clip, stream).start()

        if total is None:
            out_ref[...] = jnp.zeros_like(out_ref)
        else:
            out_ref[...] = total_ref[...]

        for shard in range(shard_total):

            @pl.when(shards[shard][3](slab))
            def _():
                weight_copy(shard).wait()
                for clip in range(clip_count):
                    for stream in range(stream_count):
                        row_copy(0, shard, clip, stream).wait()
                first, array = shards[shard][:2]
                size = array.shape[0]
                wide = whole_lanes(size)
                if wide > size:
                    held[shard, size:wide] = jnp.zeros((wide - size, depth), held.dtype)
                for clip in range(clip_count):
                    out_ref[clip, :, pl.ds(first, wide)] += lax.dot_general(
                        rows[shard, pl.ds(clip * row_count, row_count)],
                        held[shard, pl.ds(0, wide)],
                        (((1,), (1,)), ((), ())),
                        preferred_element_type=jnp.float32,
                    )

        if peers:
            diagonal = on_diagonal()
            for clip in range(clip_count):
                for first in range(0, row_count, LANES):
                    piece = out_ref[clip, pl.ds(first, LANES)]
                    sums = jnp.sum(piece * piece, axis=1, keepdims=True)
                    sums = jnp.sum(jnp.where(diagonal, sums, 0.0), axis=0, keepdims=True)
                    squares_ref[:, :, pl.ds(clip * row_count + first, LANES)] = jnp.broadcast_to(
                        sums[None], (peers, 1, LANES)
                    )

    operands = [*flat, *(array for _, array, _, _ in shards)]
    in_specs = [pl.BlockSpec(memory_space=pl.ANY) for _ in operands]
    aliases = {}
    if total is not None:
        operands.append(total)
        in_specs.append(pl.BlockSpec(memory_space=pltpu.VMEM))
        aliases = {len(operands): 0}
    out_shape = [jax.ShapeDtypeStruct((clip_count, row_count, lanes), jnp.float32)]
    if peers:
        out_shape.append(jax.ShapeDtypeStruct((peers, 1, clip_count * row_count), jnp.float32))
    return pl.pallas_call(
        kernel,
        in_specs=[pl.BlockSpec(memory_space=pltpu.SMEM)] + in_specs,
        out_specs=[pl.BlockSpec(memory_space=pltpu.VMEM)] * len(out_shape),
        out_shape=out_shape,
        scratch_shapes=[
            pltpu.VMEM((shard_total, clip_count * row_count, depth), jnp.bfloat16),
            pltpu.VMEM((shard_total, lanes, depth), jnp.bfloat16),
            pltpu.SemaphoreType.DMA((shard_total, clip_count, stream_count)),
            pltpu.SemaphoreType.DMA((shard_total,)),
        ],
        input_output_aliases=aliases,
        compiler_params=pltpu.CompilerParams(vmem_limit_bytes=(8 + 4 * shard_total) * 1024 * 1024),
        cost_estimate=pl.CostEstimate(
            flops=0,
            bytes_accessed=0,
            transcendentals=0,
        ),
        name="project",
    )(where, *operands)


def row_scales(squares_ref, clip, row_count, model_width):
    diagonal = on_diagonal()
    scales = []
    for first in range(0, row_count, LANES):
        at = pl.ds(pl.multiple_of(clip * row_count + first, LANES), LANES)
        mean = jnp.sum(squares_ref[:, :, at], axis=0) / model_width
        scale = jnp.broadcast_to(lax.rsqrt(mean + epsilon), (LANES, LANES))
        scales.append(jnp.sum(jnp.where(diagonal, scale, 0.0), axis=1, keepdims=True))
    return jnp.concatenate(scales, axis=0)


def finish(total, squares, gain, columns, model_width, devices):
    clip_count, row_count, lanes = total.shape
    near_rows = row_count // 2

    def kernel(total_ref, squares_ref, gain_ref, row_ref):
        lane = lax.broadcasted_iota(jnp.int32, (1, lanes), 1)
        row = jnp.zeros((1, lanes), jnp.float32)
        for clip in range(clip_count):
            scale = row_scales(squares_ref, clip, row_count, model_width)
            clean = total_ref[clip, :near_rows] * scale[:near_rows]
            difference = total_ref[clip, near_rows:] * scale[near_rows:] - clean
            sums = jnp.sum(difference * difference, axis=0, keepdims=True)
            penalty = jnp.sum(sums * gain_ref[...] * gain_ref[...], axis=1, keepdims=True)
            row = row + sums + jnp.where(lane == columns + clip, penalty, 0.0)
        row_ref[...] = jnp.broadcast_to(row[None], row_ref.shape)

    return pl.pallas_call(
        kernel,
        out_shape=jax.ShapeDtypeStruct((devices, 1, lanes), jnp.float32),
        compiler_params=pltpu.CompilerParams(vmem_limit_bytes=16 * 1024 * 1024),
        name="finish",
    )(total, squares, gain)


def make_features(total, squares, gain, model_width):
    clip_count, row_count, lanes = total.shape
    near_rows = row_count // 2

    def kernel(total_ref, squares_ref, gain_ref, features_ref):
        for clip in range(clip_count):
            scale = row_scales(squares_ref, clip, row_count, model_width)
            clean = total_ref[clip, :near_rows] * scale[:near_rows]
            features_ref[clip] = (clean * gain_ref[...]).astype(jnp.bfloat16)

    return pl.pallas_call(
        kernel,
        out_shape=jax.ShapeDtypeStruct((clip_count, near_rows, lanes), jnp.bfloat16),
        compiler_params=pltpu.CompilerParams(vmem_limit_bytes=16 * 1024 * 1024),
        cost_estimate=pl.CostEstimate(
            flops=10**10, bytes_accessed=0, transcendentals=0
        ),
        name="make_features",
    )(total, squares, gain)


def conclude(rows, where, gain, model_count, clip_count, tokens):
    devices, _, lanes = rows.shape
    columns = gain.shape[1] // clip_count
    model_width = gain.shape[1] * model_count

    def kernel(where_ref, rows_ref, gain_ref, penalty_ref, grad_ref):
        row = lax.broadcasted_iota(jnp.int32, (devices, 1, lanes), 0)
        model = (row // clip_count) % model_count
        sums = []
        for clip in range(clip_count):
            mine = (model == where_ref[1]) & (row % clip_count == clip)
            sums.append(jnp.sum(jnp.where(mine, rows_ref[...], 0.0), axis=0)[:, :columns])
        sums = jnp.concatenate(sums, axis=1)
        grad = gain_ref[...] * sums / (sigma_noise * sigma_noise * tokens)
        grad_ref[...] = grad.reshape(grad_ref.shape)
        lane = lax.broadcasted_iota(jnp.int32, (devices, 1, lanes), 2)
        own = jnp.where(lane == columns + where_ref[2], rows_ref[...], 0.0)
        penalty_ref[0] = jnp.sum(own) / (sigma_noise * sigma_noise * tokens * model_width)

    return pl.pallas_call(
        kernel,
        in_specs=[pl.BlockSpec(memory_space=pltpu.SMEM)]
        + [pl.BlockSpec(memory_space=pltpu.VMEM)] * 2,
        out_specs=[
            pl.BlockSpec(memory_space=pltpu.SMEM),
            pl.BlockSpec(memory_space=pltpu.VMEM),
        ],
        out_shape=[
            jax.ShapeDtypeStruct((1,), jnp.float32),
            jax.ShapeDtypeStruct((gain.shape[1],), jnp.float32),
        ],
        compiler_params=pltpu.CompilerParams(vmem_limit_bytes=60 * 1024 * 1024),
        name="conclude",
    )(where, rows, gain)


def swap(array, axis, distance):
    count = lax.axis_size(axis)
    return lax.ppermute(array, axis, [(i, i ^ distance) for i in range(count)])


def distances(axis):
    count = lax.axis_size(axis)
    return [(axis, 1 << bit) for bit in reversed(range(count.bit_length() - 1))]


def spread(block, order, before_step):
    stacks = [([(0, 0)], block[None])]
    for step, (axis, distance) in enumerate(order):
        if step < len(order) - 1 and len(stacks) > 1:
            keys = [key for some, _ in stacks for key in some]
            stacks = [(keys, jnp.concatenate([array for _, array in stacks]))]
        received = []
        for part, (keys, array) in enumerate(stacks):
            keys = [(m ^ distance, c) if axis == "mp" else (m, c ^ distance) for m, c in keys]
            received.append((keys, swap(before_step(step, part, array), axis, distance)))
        stacks = stacks + received
    return stacks


def collect(rows, axes):
    return lax.all_to_all(rows, axes, split_axis=0, concat_axis=0, tiled=True)


def pick(options, index):
    return lax.select_n(index, *options) if len(options) > 1 else options[0]


def local(projections, perturbation, out_weight, norm_gain, live_counts):
    tile_len = projections.shape[2]
    local_width = projections.shape[4]
    slots = projections.shape[1]
    slab_count = lax.axis_size("frames")
    slab_index = lax.axis_index("frames")
    model_count = lax.axis_size("mp")
    model_index = lax.axis_index("mp")
    clip_count = lax.axis_size("dp")
    clip_index = lax.axis_index("dp")
    model_width = local_width * model_count
    token_total = slots * slab_count * tile_len
    half = local_width // clip_count
    near_rows = slots * tile_len

    def own_columns(array):
        return pick(
            [array[..., n * half : (n + 1) * half] for n in range(clip_count)], clip_index
        )

    clean = projections[0].transpose(0, 2, 1, 3)
    noise = perturbation[0].transpose(0, 2, 1, 3)
    up = [(i, i + 1) for i in range(slab_count - 1)]
    down = [(i + 1, i) for i in range(slab_count - 1)]

    tail, head = prepare_halo(clean, noise, (slots - 1, 0))
    tail, head, clean, noise, out_weight = lax.optimization_barrier(
        (tail, head, clean, noise, out_weight)
    )
    right = lax.ppermute(head, "frames", down)
    left = lax.ppermute(tail, "frames", up)
    streams = (clean, perturb(clean, noise))
    counts = jnp.pad(live_counts[0], (1, 1))
    nearby = lax.dynamic_slice_in_dim(counts, slots * slab_index, slots + 2)
    where = jnp.concatenate(
        [jnp.stack([slab_index, model_index, clip_index]).astype(jnp.int32), nearby]
    )
    gain_row = jnp.pad(own_columns(norm_gain), (0, whole_lanes(half) - half))[None]
    gain_all = norm_gain[None]

    cut = whole_lanes(half) // 2
    own_weight, *parts = prepare_weight(where, out_weight, clip_count, cut)
    line = slab_count == model_count and slab_count == 4
    last = slab_count - 1
    near, passed, across = [], None, []

    if line:
        near = [lax.ppermute(own_weight, "frames", pairs) for pairs in (down, up)]
        across = [
            lax.ppermute(block, "frames", [(0, last), (last, 0)]) for block in parts
        ]

    def before_step(stream, step, part, value):
        nonlocal near, passed, gain_row, gain_all
        if line and stream == 0 and step == 1:
            value, near, gain_row, gain_all = lax.optimization_barrier(
                (value, near, gain_row, gain_all)
            )
            options = [own_weight, near[0], near[1], own_weight]
            sent = lax.select_n(slab_index, *options)
            passed = lax.ppermute(sent, "frames", [(0, 2), (1, 0), (2, last), (last, 1)])
        if line and stream == 1 and step == 1:
            value, across[0] = lax.optimization_barrier((value, across[0]))
        return value

    gathered = []
    orders = (
        distances("dp") + distances("mp"),
        distances("mp")[:1] + distances("dp") + distances("mp")[1:],
    )
    for n, order in enumerate(orders):
        attended = attention(where, streams[n], left, right, n).reshape(near_rows, local_width)
        gathered.append(
            spread(attended, order, lambda *at, n=n: before_step(n, *at))
        )

    peers = model_count * clip_count
    if line:
        shards = [
            (0, own_weight, lambda slab: slab, lambda slab: slab >= 0),
            (0, near[0], lambda slab: jnp.minimum(slab + 1, last), lambda slab: slab < last),
            (0, near[1], lambda slab: jnp.maximum(slab - 1, 0), lambda slab: slab > 0),
        ]
        for first, block in zip((0, cut), across):
            shards.append(
                (first, block, lambda slab: last - slab, lambda slab: (slab == 0) | (slab == last))
            )
        shards.append((0, passed, lambda slab: (slab + 2) % slab_count, lambda slab: slab >= 0))
        (total,) = project(where, gathered, shards[:4], None, half, 0)
        (total,) = project(where, gathered, shards[5:], total, half, 0)
        total, squares = project(where, gathered, shards[4:5], total, half, peers)
    else:
        weight = lax.all_gather(own_weight, "frames", axis=1, tiled=True)
        shards = [
            (
                0,
                lax.dynamic_slice_in_dim(weight, m * local_width, local_width, axis=1),
                lambda slab, m=m: m,
                lambda slab: slab >= 0,
            )
            for m in range(model_count)
        ]
        total, squares = project(where, gathered, shards, None, half, peers)

    squares = collect(squares, ("mp", "dp"))
    sums = finish(
        total, squares, gain_row, half, model_width, slab_count * model_count * clip_count
    )
    features = make_features(total, squares, gain_row, model_width)
    sums = collect(sums, ("frames", "mp", "dp"))

    features = features[..., :half].reshape(clip_count, slots, tile_len, half)
    columns = [pick([features[d] for d in range(clip_count)], clip_index)]
    for distance in range(1, clip_count):
        sent = pick([features[d ^ distance] for d in range(clip_count)], clip_index)
        columns.append(swap(sent, "dp", distance))
    features = jnp.concatenate(
        [
            pick([columns[n ^ d] for d in range(clip_count)], clip_index)
            for n in range(clip_count)
        ],
        axis=-1,
    )[None]
    sums, features = lax.optimization_barrier((sums, features))
    penalty, gain_grad = conclude(
        sums, where, gain_all, model_count, clip_count, token_total
    )
    return (features, penalty, gain_grad)


def solution(mesh):
    placed = (
        P("dp", "frames", None, None, "mp"),
        P("dp", "frames", None, None, "mp"),
        P("frames", "mp"),
        P("mp"),
        P("dp", None),
    )
    return jax.shard_map(
        local,
        mesh=mesh,
        in_specs=placed,
        out_specs=(P("dp", "frames", None, "mp"), P("dp"), P("mp")),
        check_vma=False,
    )
```

```python
import math

import jax
import jax.numpy as jnp
from jax import lax
from jax.experimental import pallas as pl
from jax.experimental.pallas import tpu as pltpu
from jax.sharding import PartitionSpec as P

HEAD_DIM = 128
HEADS_AT_ONCE = 1
LANES = 128


sigma_noise = 0.25
epsilon = 1e-06


def perturb(clean, noise):
    return (clean.astype(jnp.float32) + sigma_noise * noise.astype(jnp.float32)).astype(jnp.bfloat16)


def prepare_halo(clean, noise, slots):
    _, _, tile_len, width = clean.shape

    def kernel(clean_ref, noise_ref, *refs):
        out_refs, (keep, add, in_sems, out_sems) = refs[: len(slots)], refs[len(slots) :]
        pieces = [(n, slot, part) for n, slot in enumerate(slots) for part in range(2)]
        loads, stores = [], []
        for n, slot, part in pieces:
            for m, (source, target) in enumerate(((clean_ref, keep), (noise_ref, add))):
                loads.append(
                    pltpu.make_async_copy(
                        source.at[slot, 1 + part], target.at[n, part], in_sems.at[n, part, m]
                    )
                )
                loads[-1].start()
        for at, (n, slot, part) in enumerate(pieces):
            loads[2 * at].wait()
            loads[2 * at + 1].wait()
            add[n, part] = perturb(keep[n, part], add[n, part])
            for m, source in enumerate((keep, add)):
                stores.append(
                    pltpu.make_async_copy(
                        source.at[n, part], out_refs[n].at[m, part], out_sems.at[n, part, m]
                    )
                )
                stores[-1].start()
        for store in stores:
            store.wait()

    scratch = pltpu.VMEM((len(slots), 2, tile_len, width), jnp.bfloat16)
    return pl.pallas_call(
        kernel,
        in_specs=[pl.BlockSpec(memory_space=pl.ANY)] * 2,
        out_specs=[pl.BlockSpec(memory_space=pl.ANY)] * len(slots),
        out_shape=[jax.ShapeDtypeStruct((2, 2, tile_len, width), jnp.bfloat16)] * len(slots),
        scratch_shapes=[
            scratch,
            scratch,
            pltpu.SemaphoreType.DMA((len(slots), 2, 2)),
            pltpu.SemaphoreType.DMA((len(slots), 2, 2)),
        ],
        compiler_params=pltpu.CompilerParams(vmem_limit_bytes=60 * 1024 * 1024),
        name="prepare_halo",
    )(clean, noise)


def prepare_weight(where, weight, clip_count, cut):
    depth, width = weight.shape
    half = width // clip_count

    def kernel(where_ref, weight_ref, whole_ref, early_ref, late_ref):
        for clip in range(clip_count):

            @pl.when(where_ref[2] == clip)
            def _():
                begin, end = clip * half, (clip + 1) * half
                for first in range(begin // LANES * LANES, end, LANES):
                    low, high = max(first, begin), min(first + LANES, end)
                    turned = weight_ref[:, pl.ds(first, LANES)].T
                    whole_ref[pl.ds(low - begin, high - low)] = turned[low - first : high - first]

        early_ref[...] = whole_ref[:cut]
        late_ref[...] = whole_ref[cut:]

    return pl.pallas_call(
        kernel,
        in_specs=[
            pl.BlockSpec(memory_space=pltpu.SMEM),
            pl.BlockSpec(memory_space=pltpu.VMEM),
        ],
        out_specs=[pl.BlockSpec(memory_space=pltpu.VMEM)] * 3,
        out_shape=[
            jax.ShapeDtypeStruct((rows, depth), weight.dtype) for rows in (half, cut, half - cut)
        ],
        compiler_params=pltpu.CompilerParams(vmem_limit_bytes=60 * 1024 * 1024),
        name="prepare_weight",
    )(where, weight)


def attend_kernel(where_ref, own_ref, right_ref, left_ref, out_ref):
    slots, _, tile_len, width = own_ref.shape
    key_pos = lax.broadcasted_iota(jnp.int32, (1, 2 * tile_len), 1)
    live = []
    for slot in range(slots):
        own_count = where_ref[4 + slot]
        far_count = where_ref[3 if slot == 0 else slots + 4]
        live.append((key_pos < own_count) | ((key_pos >= tile_len) & (key_pos < tile_len + far_count)))
    row_pos = lax.broadcasted_iota(jnp.int32, (tile_len, 1), 0)
    units = [(slot, head) for head in range(width // HEAD_DIM) for slot in range(slots)]

    scores = []
    for slot, head in units:
        cols = pl.ds(head * HEAD_DIM, HEAD_DIM)
        halo_ref = left_ref if slot == 0 else right_ref
        keys = jnp.concatenate([own_ref[slot, 1, :, cols], halo_ref[0, :, cols]], axis=0)
        raw = lax.dot_general(
            own_ref[slot, 0, :, cols],
            keys,
            (((1,), (1,)), ((), ())),
            preferred_element_type=jnp.float32,
        )
        scores.append(jnp.where(live[slot], raw * (1.0 / math.sqrt(HEAD_DIM)), jnp.float32(-1e30)))
    largest = [jnp.max(s, axis=-1, keepdims=True) for s in scores]
    weights = [jnp.exp(s - top) for s, top in zip(scores, largest)]
    totals = [jnp.sum(w, axis=-1, keepdims=True) for w in weights]
    for (slot, head), weight, total in zip(units, weights, totals):
        cols = pl.ds(head * HEAD_DIM, HEAD_DIM)
        halo_ref = left_ref if slot == 0 else right_ref
        values = jnp.concatenate([own_ref[slot, 2, :, cols], halo_ref[1, :, cols]], axis=0)
        probabilities = (weight * (1.0 / total)).astype(jnp.bfloat16)
        mixed = jnp.dot(probabilities, values, preferred_element_type=jnp.float32)
        out_ref[slot, :, cols] = jnp.where(row_pos < where_ref[4 + slot], mixed, 0.0).astype(
            jnp.bfloat16
        )


def attention(where, own, left, right, stream):
    slots, _, tile_len, width = own.shape
    block = HEADS_AT_ONCE * HEAD_DIM
    own_spec = pl.BlockSpec((slots, 3, tile_len, block), lambda h, c: (0, 0, 0, h))
    halo_spec = pl.BlockSpec((None, 2, tile_len, block), lambda h, c: (stream, 0, 0, h))
    return pl.pallas_call(
        attend_kernel,
        grid_spec=pltpu.PrefetchScalarGridSpec(
            num_scalar_prefetch=1,
            grid=(width // block,),
            in_specs=[own_spec, halo_spec, halo_spec],
            out_specs=pl.BlockSpec((slots, tile_len, block), lambda h, c: (0, 0, h)),
        ),
        out_shape=jax.ShapeDtypeStruct((slots, tile_len, width), jnp.bfloat16),
        compiler_params=pltpu.CompilerParams(vmem_limit_bytes=48 * 1024 * 1024),
        cost_estimate=pl.CostEstimate(
            flops=0,
            bytes_accessed=0,
            transcendentals=0,
        ),
        name="attention",
    )(where, own, right, left)


def whole_lanes(columns):
    return -(-columns // LANES) * LANES


def on_diagonal():
    row = lax.broadcasted_iota(jnp.int32, (LANES, LANES), 0)
    return row == lax.broadcasted_iota(jnp.int32, (LANES, LANES), 1)


def project(where, gathered, shards, total, columns, peers):
    stream_count = len(gathered)
    home = [
        {key: (n, at) for n, (keys, _) in enumerate(stacks) for at, key in enumerate(keys)}
        for stacks in gathered
    ]
    clip_count = 1 + max(clip for _, clip in home[0])
    place_count = 1 + max(place for place, _ in home[0])
    _, block_rows, depth = gathered[0][0][1].shape
    lanes = whole_lanes(columns)
    row_count = stream_count * block_rows
    shard_total = len(shards)
    flat = [array for stacks in gathered for _, array in stacks]
    base = [sum(len(stacks) for stacks in gathered[:n]) for n in range(stream_count)]

    def kernel(where_ref, *refs):
        slab, model, own_clip = where_ref[0], where_ref[1], where_ref[2]
        block_refs = refs[: len(flat)]
        weight_refs = refs[len(flat) : len(flat) + shard_total]
        total_ref = refs[len(flat) + shard_total] if total is not None else None
        rows, held, row_sem, weight_sem = refs[-4:]
        out_ref = refs[len(operands)]
        squares_ref = refs[len(operands) + 1]

        def weight_copy(shard):
            size = shards[shard][1].shape[0]
            return pltpu.make_async_copy(
                weight_refs[shard], held.at[shard, pl.ds(0, size)], weight_sem.at[shard]
            )

        def row_copy(place, shard, clip, stream):
            stack, at = home[stream][place, clip]
            source = block_refs[base[stream] + stack].at[at]
            first = pl.multiple_of(
                (clip ^ own_clip) * row_count + stream * block_rows, 16
            )
            return pltpu.make_async_copy(
                source,
                rows.at[shard, pl.ds(first, block_rows)],
                row_sem.at[shard, clip, stream],
            )

        for shard in range(shard_total):

            @pl.when(shards[shard][3](slab))
            def _():
                weight_copy(shard).start()
                for place in range(place_count):

                    @pl.when((shards[shard][2](slab) ^ model) == place)
                    def _():
                        for clip in range(clip_count):
                            for stream in range(stream_count):
                                row_copy(place, shard, clip, stream).start()

        if total is None:
            out_ref[...] = jnp.zeros_like(out_ref)
        else:
            out_ref[...] = total_ref[...]

        for shard in range(shard_total):

            @pl.when(shards[shard][3](slab))
            def _():
                weight_copy(shard).wait()
                for clip in range(clip_count):
                    for stream in range(stream_count):
                        row_copy(0, shard, clip, stream).wait()
                first, array = shards[shard][:2]
                size = array.shape[0]
                wide = whole_lanes(size)
                if wide > size:
                    held[shard, size:wide] = jnp.zeros((wide - size, depth), held.dtype)
                out_ref[:, pl.ds(first, wide)] += lax.dot_general(
                    rows[shard],
                    held[shard, pl.ds(0, wide)],
                    (((1,), (1,)), ((), ())),
                    preferred_element_type=jnp.float32,
                )

        if peers:
            diagonal = on_diagonal()
            for first in range(0, clip_count * row_count, LANES):
                piece = out_ref[pl.ds(first, LANES)]
                sums = jnp.sum(piece * piece, axis=1, keepdims=True)
                sums = jnp.sum(jnp.where(diagonal, sums, 0.0), axis=0, keepdims=True)
                squares_ref[:, :, pl.ds(first, LANES)] = jnp.broadcast_to(
                    sums[None], (peers, 1, LANES)
                )

    operands = [*flat, *(array for _, array, _, _ in shards)]
    in_specs = [pl.BlockSpec(memory_space=pl.ANY) for _ in operands]
    aliases = {}
    if total is not None:
        operands.append(total)
        in_specs.append(pl.BlockSpec(memory_space=pltpu.VMEM))
        aliases = {len(operands): 0}
    out_shape = [jax.ShapeDtypeStruct((clip_count * row_count, lanes), jnp.float32)]
    if peers:
        out_shape.append(jax.ShapeDtypeStruct((peers, 1, clip_count * row_count), jnp.float32))
    return pl.pallas_call(
        kernel,
        in_specs=[pl.BlockSpec(memory_space=pltpu.SMEM)] + in_specs,
        out_specs=[pl.BlockSpec(memory_space=pltpu.VMEM)] * len(out_shape),
        out_shape=out_shape,
        scratch_shapes=[
            pltpu.VMEM((shard_total, clip_count * row_count, depth), jnp.bfloat16),
            pltpu.VMEM((shard_total, lanes, depth), jnp.bfloat16),
            pltpu.SemaphoreType.DMA((shard_total, clip_count, stream_count)),
            pltpu.SemaphoreType.DMA((shard_total,)),
        ],
        input_output_aliases=aliases,
        compiler_params=pltpu.CompilerParams(vmem_limit_bytes=(8 + 4 * shard_total) * 1024 * 1024),
        cost_estimate=pl.CostEstimate(
            flops=0,
            bytes_accessed=0,
            transcendentals=0,
        ),
        name="project",
    )(where, *operands)


def row_scales(squares_ref, clip, row_count, model_width):
    diagonal = on_diagonal()
    scales = []
    for first in range(0, row_count, LANES):
        at = pl.ds(clip * row_count + first, LANES)
        mean = jnp.sum(squares_ref[:, :, at], axis=0) / model_width
        scale = jnp.broadcast_to(lax.rsqrt(mean + epsilon), (LANES, LANES))
        scales.append(jnp.sum(jnp.where(diagonal, scale, 0.0), axis=1, keepdims=True))
    return jnp.concatenate(scales, axis=0)


def finish(total, squares, gain, clip_count, columns, model_width, devices):
    rows, lanes = total.shape
    row_count = rows // clip_count
    near_rows = row_count // 2

    def kernel(total_ref, squares_ref, gain_ref, row_ref):
        lane = lax.broadcasted_iota(jnp.int32, (1, lanes), 1)
        row = jnp.zeros((1, lanes), jnp.float32)
        for clip in range(clip_count):
            scale = row_scales(squares_ref, clip, row_count, model_width)
            clean = total_ref[pl.ds(clip * row_count, near_rows)] * scale[:near_rows]
            difference = total_ref[pl.ds(clip * row_count + near_rows, near_rows)] * scale[near_rows:] - clean
            sums = jnp.sum(difference * difference, axis=0, keepdims=True)
            penalty = jnp.sum(sums * gain_ref[...] * gain_ref[...], axis=1, keepdims=True)
            row = row + sums + jnp.where(lane == columns + clip, penalty, 0.0)
        row_ref[...] = jnp.broadcast_to(row[None], row_ref.shape)

    return pl.pallas_call(
        kernel,
        out_shape=jax.ShapeDtypeStruct((devices, 1, lanes), jnp.float32),
        compiler_params=pltpu.CompilerParams(vmem_limit_bytes=16 * 1024 * 1024),
        name="finish",
    )(total, squares, gain)


def make_features(total, squares, gain, clip_count, model_width):
    rows, lanes = total.shape
    row_count = rows // clip_count
    near_rows = row_count // 2

    def kernel(total_ref, squares_ref, gain_ref, features_ref):
        for clip in range(clip_count):
            scale = row_scales(squares_ref, clip, row_count, model_width)
            clean = total_ref[pl.ds(clip * row_count, near_rows)] * scale[:near_rows]
            features_ref[clip] = (clean * gain_ref[...]).astype(jnp.bfloat16)

    return pl.pallas_call(
        kernel,
        out_shape=jax.ShapeDtypeStruct((clip_count, near_rows, lanes), jnp.bfloat16),
        compiler_params=pltpu.CompilerParams(vmem_limit_bytes=16 * 1024 * 1024),
        cost_estimate=pl.CostEstimate(
            flops=10**10, bytes_accessed=0, transcendentals=0
        ),
        name="make_features",
    )(total, squares, gain)


def conclude(rows, where, gain, model_count, clip_count, tokens):
    devices, _, lanes = rows.shape
    columns = gain.shape[1] // clip_count
    model_width = gain.shape[1] * model_count

    def kernel(where_ref, rows_ref, gain_ref, penalty_ref, grad_ref):
        row = lax.broadcasted_iota(jnp.int32, (devices, 1, lanes), 0)
        model = (row // clip_count) % model_count
        sums = []
        for clip in range(clip_count):
            mine = (model == where_ref[1]) & (row % clip_count == clip)
            sums.append(jnp.sum(jnp.where(mine, rows_ref[...], 0.0), axis=0)[:, :columns])
        sums = jnp.concatenate(sums, axis=1)
        grad = gain_ref[...] * sums / (sigma_noise * sigma_noise * tokens)
        grad_ref[...] = grad.reshape(grad_ref.shape)
        lane = lax.broadcasted_iota(jnp.int32, (devices, 1, lanes), 2)
        own = jnp.where(lane == columns + where_ref[2], rows_ref[...], 0.0)
        penalty_ref[0] = jnp.sum(own) / (sigma_noise * sigma_noise * tokens * model_width)

    return pl.pallas_call(
        kernel,
        in_specs=[pl.BlockSpec(memory_space=pltpu.SMEM)]
        + [pl.BlockSpec(memory_space=pltpu.VMEM)] * 2,
        out_specs=[
            pl.BlockSpec(memory_space=pltpu.SMEM),
            pl.BlockSpec(memory_space=pltpu.VMEM),
        ],
        out_shape=[
            jax.ShapeDtypeStruct((1,), jnp.float32),
            jax.ShapeDtypeStruct((gain.shape[1],), jnp.float32),
        ],
        compiler_params=pltpu.CompilerParams(vmem_limit_bytes=4 * 1024 * 1024),
        name="conclude",
    )(where, rows, gain)


def swap(array, axis, distance):
    count = lax.axis_size(axis)
    return lax.ppermute(array, axis, [(i, i ^ distance) for i in range(count)])


def distances(axis):
    count = lax.axis_size(axis)
    return [(axis, 1 << bit) for bit in reversed(range(count.bit_length() - 1))]


def spread(block, order, before_step):
    stacks = [([(0, 0)], block[None])]
    for step, (axis, distance) in enumerate(order):
        if step < len(order) - 1 and len(stacks) > 1:
            keys = [key for some, _ in stacks for key in some]
            stacks = [(keys, jnp.concatenate([array for _, array in stacks]))]
        received = []
        for part, (keys, array) in enumerate(stacks):
            keys = [(m ^ distance, c) if axis == "mp" else (m, c ^ distance) for m, c in keys]
            received.append((keys, swap(before_step(step, part, array), axis, distance)))
        stacks = stacks + received
    return stacks


def collect(rows, axes):
    return lax.all_to_all(rows, axes, split_axis=0, concat_axis=0, tiled=True)


def pick(options, index):
    return lax.select_n(index, *options) if len(options) > 1 else options[0]


def local(projections, perturbation, out_weight, norm_gain, live_counts):
    tile_len = projections.shape[2]
    local_width = projections.shape[4]
    slots = projections.shape[1]
    slab_count = lax.axis_size("frames")
    slab_index = lax.axis_index("frames")
    model_count = lax.axis_size("mp")
    model_index = lax.axis_index("mp")
    clip_count = lax.axis_size("dp")
    clip_index = lax.axis_index("dp")
    model_width = local_width * model_count
    token_total = slots * slab_count * tile_len
    half = local_width // clip_count
    near_rows = slots * tile_len

    def own_columns(array):
        return pick(
            [array[..., n * half : (n + 1) * half] for n in range(clip_count)], clip_index
        )

    clean = projections[0].transpose(0, 2, 1, 3)
    noise = perturbation[0].transpose(0, 2, 1, 3)
    up = [(i, i + 1) for i in range(slab_count - 1)]
    down = [(i + 1, i) for i in range(slab_count - 1)]

    tail, head = prepare_halo(clean, noise, (slots - 1, 0))
    tail, head, clean, noise, out_weight = lax.optimization_barrier(
        (tail, head, clean, noise, out_weight)
    )
    right = lax.ppermute(head, "frames", down)
    left = lax.ppermute(tail, "frames", up)
    streams = (clean, perturb(clean, noise))
    counts = jnp.pad(live_counts[0], (1, 1))
    nearby = lax.dynamic_slice_in_dim(counts, slots * slab_index, slots + 2)
    where = jnp.concatenate(
        [jnp.stack([slab_index, model_index, clip_index]).astype(jnp.int32), nearby]
    )
    gain_row = jnp.pad(own_columns(norm_gain), (0, whole_lanes(half) - half))[None]
    gain_all = norm_gain[None]

    cut = min(LANES, half // 2)
    own_weight, *parts = prepare_weight(where, out_weight, clip_count, cut)
    line = slab_count == model_count and slab_count == 4
    last = slab_count - 1
    near, passed, across = [], [], []

    if line:
        near = [lax.ppermute(own_weight, "frames", pairs) for pairs in (down, up)]
        across = [
            lax.ppermute(block, "frames", [(0, last), (last, 0)]) for block in parts
        ]

    def before_step(stream, step, part, value):
        nonlocal near, passed, gain_row, gain_all
        if line and stream == 0 and step == 1:
            value, near, gain_row, gain_all = lax.optimization_barrier(
                (value, near, gain_row, gain_all)
            )
            passed = [
                lax.ppermute(near[0], "frames", down[:2]),
                lax.ppermute(near[1], "frames", up[1:]),
            ]
        if line and stream == 1 and step == 1:
            value, across[0] = lax.optimization_barrier((value, across[0]))
        if line and stream == 1 and step == 2 and part == 1:
            value, passed = lax.optimization_barrier((value, passed))
        return value

    gathered = []
    orders = (
        distances("dp") + distances("mp"),
        distances("mp")[:1] + distances("dp") + distances("mp")[1:],
    )
    for n, order in enumerate(orders):
        attended = attention(where, streams[n], left, right, n).reshape(near_rows, local_width)
        gathered.append(
            spread(attended, order, lambda *at, n=n: before_step(n, *at))
        )

    peers = model_count * clip_count
    if line:
        shards = [
            (0, own_weight, lambda slab: slab, lambda slab: slab >= 0),
            (0, near[0], lambda slab: jnp.minimum(slab + 1, last), lambda slab: slab < last),
            (0, near[1], lambda slab: jnp.maximum(slab - 1, 0), lambda slab: slab > 0),
            (0, passed[0], lambda slab: jnp.minimum(slab + 2, last), lambda slab: slab < 2),
            (0, passed[1], lambda slab: jnp.maximum(slab - 2, 0), lambda slab: slab >= 2),
        ]
        for first, block in zip((0, cut), across):
            shards.append(
                (first, block, lambda slab: last - slab, lambda slab: (slab == 0) | (slab == last))
            )
        (total,) = project(where, gathered, shards[:-1], None, half, 0)
        total, squares = project(where, gathered, shards[-1:], total, half, peers)
    else:
        weight = lax.all_gather(own_weight, "frames", axis=1, tiled=True)
        shards = [
            (
                0,
                lax.dynamic_slice_in_dim(weight, m * local_width, local_width, axis=1),
                lambda slab, m=m: m,
                lambda slab: slab >= 0,
            )
            for m in range(model_count)
        ]
        total, squares = project(where, gathered, shards, None, half, peers)

    squares = collect(squares, ("mp", "dp"))
    sums = finish(
        total,
        squares,
        gain_row,
        clip_count,
        half,
        model_width,
        slab_count * model_count * clip_count,
    )
    features = make_features(total, squares, gain_row, clip_count, model_width)
    sums = collect(sums, ("frames", "mp", "dp"))

    features = features[..., :half].reshape(clip_count, slots, tile_len, half)
    columns = [pick([features[d] for d in range(clip_count)], clip_index)]
    for distance in range(1, clip_count):
        sent = pick([features[d ^ distance] for d in range(clip_count)], clip_index)
        columns.append(swap(sent, "dp", distance))
    features = jnp.concatenate(
        [
            pick([columns[n ^ d] for d in range(clip_count)], clip_index)
            for n in range(clip_count)
        ],
        axis=-1,
    )[None]
    sums, features = lax.optimization_barrier((sums, features))
    penalty, gain_grad = conclude(
        sums, where, gain_all, model_count, clip_count, token_total
    )
    return (features, penalty, gain_grad)


def solution(mesh):
    placed = (
        P("dp", "frames", None, None, "mp"),
        P("dp", "frames", None, None, "mp"),
        P("frames", "mp"),
        P("mp"),
        P("dp", None),
    )
    return jax.shard_map(
        local,
        mesh=mesh,
        in_specs=placed,
        out_specs=(P("dp", "frames", None, "mp"), P("dp"), P("mp")),
        check_vma=False,
    )
```

```python
import math

import jax
import jax.numpy as jnp
from jax import lax
from jax.experimental import pallas as pl
from jax.experimental.pallas import tpu as pltpu
from jax.sharding import PartitionSpec as P

HEAD_DIM = 128
HEADS_AT_ONCE = 1
LANES = 128


sigma_noise = 0.25
epsilon = 1e-06


def perturb(clean, noise):
    return (clean.astype(jnp.float32) + sigma_noise * noise.astype(jnp.float32)).astype(jnp.bfloat16)


def prepare_halo(clean, noise, slots):
    _, _, tile_len, width = clean.shape

    def kernel(clean_ref, noise_ref, *refs):
        out_refs, (keep, add, in_sems, out_sems) = refs[: len(slots)], refs[len(slots) :]
        pieces = [(n, slot, part) for n, slot in enumerate(slots) for part in range(2)]
        loads, stores = [], []
        for n, slot, part in pieces:
            for m, (source, target) in enumerate(((clean_ref, keep), (noise_ref, add))):
                loads.append(
                    pltpu.make_async_copy(
                        source.at[slot, 1 + part], target.at[n, part], in_sems.at[n, part, m]
                    )
                )
                loads[-1].start()
        for at, (n, slot, part) in enumerate(pieces):
            loads[2 * at].wait()
            loads[2 * at + 1].wait()
            add[n, part] = perturb(keep[n, part], add[n, part])
            for m, source in enumerate((keep, add)):
                stores.append(
                    pltpu.make_async_copy(
                        source.at[n, part], out_refs[n].at[m, part], out_sems.at[n, part, m]
                    )
                )
                stores[-1].start()
        for store in stores:
            store.wait()

    scratch = pltpu.VMEM((len(slots), 2, tile_len, width), jnp.bfloat16)
    return pl.pallas_call(
        kernel,
        in_specs=[pl.BlockSpec(memory_space=pl.ANY)] * 2,
        out_specs=[pl.BlockSpec(memory_space=pl.ANY)] * len(slots),
        out_shape=[jax.ShapeDtypeStruct((2, 2, tile_len, width), jnp.bfloat16)] * len(slots),
        scratch_shapes=[
            scratch,
            scratch,
            pltpu.SemaphoreType.DMA((len(slots), 2, 2)),
            pltpu.SemaphoreType.DMA((len(slots), 2, 2)),
        ],
        compiler_params=pltpu.CompilerParams(vmem_limit_bytes=60 * 1024 * 1024),
        name="prepare_halo",
    )(clean, noise)


def prepare_weight(where, weight, clip_count, cut):
    depth, width = weight.shape
    half = width // clip_count

    def kernel(where_ref, weight_ref, whole_ref, early_ref, late_ref):
        for clip in range(clip_count):

            @pl.when(where_ref[2] == clip)
            def _():
                begin, end = clip * half, (clip + 1) * half
                for first in range(begin // LANES * LANES, end, LANES):
                    low, high = max(first, begin), min(first + LANES, end)
                    turned = weight_ref[:, pl.ds(first, LANES)].T
                    whole_ref[pl.ds(low - begin, high - low)] = turned[low - first : high - first]

        early_ref[...] = whole_ref[:cut]
        late_ref[...] = whole_ref[cut:]

    return pl.pallas_call(
        kernel,
        in_specs=[
            pl.BlockSpec(memory_space=pltpu.SMEM),
            pl.BlockSpec(memory_space=pltpu.VMEM),
        ],
        out_specs=[pl.BlockSpec(memory_space=pltpu.VMEM)] * 3,
        out_shape=[
            jax.ShapeDtypeStruct((rows, depth), weight.dtype) for rows in (half, cut, half - cut)
        ],
        compiler_params=pltpu.CompilerParams(vmem_limit_bytes=60 * 1024 * 1024),
        name="prepare_weight",
    )(where, weight)


def attend_kernel(where_ref, own_ref, right_ref, left_ref, out_ref):
    slots, _, tile_len, width = own_ref.shape
    key_pos = lax.broadcasted_iota(jnp.int32, (1, 2 * tile_len), 1)
    live = []
    for slot in range(slots):
        own_count = where_ref[4 + slot]
        far_count = where_ref[3 if slot == 0 else slots + 4]
        live.append((key_pos < own_count) | ((key_pos >= tile_len) & (key_pos < tile_len + far_count)))
    row_pos = lax.broadcasted_iota(jnp.int32, (tile_len, 1), 0)
    units = [(slot, head) for head in range(width // HEAD_DIM) for slot in range(slots)]

    scores = []
    for slot, head in units:
        cols = pl.ds(head * HEAD_DIM, HEAD_DIM)
        halo_ref = left_ref if slot == 0 else right_ref
        keys = jnp.concatenate([own_ref[slot, 1, :, cols], halo_ref[0, :, cols]], axis=0)
        raw = lax.dot_general(
            own_ref[slot, 0, :, cols],
            keys,
            (((1,), (1,)), ((), ())),
            preferred_element_type=jnp.float32,
        )
        scores.append(jnp.where(live[slot], raw * (1.0 / math.sqrt(HEAD_DIM)), jnp.float32(-1e30)))
    largest = [jnp.max(s, axis=-1, keepdims=True) for s in scores]
    weights = [jnp.exp(s - top) for s, top in zip(scores, largest)]
    totals = [jnp.sum(w, axis=-1, keepdims=True) for w in weights]
    for (slot, head), weight, total in zip(units, weights, totals):
        cols = pl.ds(head * HEAD_DIM, HEAD_DIM)
        halo_ref = left_ref if slot == 0 else right_ref
        values = jnp.concatenate([own_ref[slot, 2, :, cols], halo_ref[1, :, cols]], axis=0)
        probabilities = (weight * (1.0 / total)).astype(jnp.bfloat16)
        mixed = jnp.dot(probabilities, values, preferred_element_type=jnp.float32)
        out_ref[slot, :, cols] = jnp.where(row_pos < where_ref[4 + slot], mixed, 0.0).astype(
            jnp.bfloat16
        )


def attention(where, own, left, right, stream):
    slots, _, tile_len, width = own.shape
    block = HEADS_AT_ONCE * HEAD_DIM
    own_spec = pl.BlockSpec((slots, 3, tile_len, block), lambda h, c: (0, 0, 0, h))
    halo_spec = pl.BlockSpec((None, 2, tile_len, block), lambda h, c: (stream, 0, 0, h))
    return pl.pallas_call(
        attend_kernel,
        grid_spec=pltpu.PrefetchScalarGridSpec(
            num_scalar_prefetch=1,
            grid=(width // block,),
            in_specs=[own_spec, halo_spec, halo_spec],
            out_specs=pl.BlockSpec((slots, tile_len, block), lambda h, c: (0, 0, h)),
        ),
        out_shape=jax.ShapeDtypeStruct((slots, tile_len, width), jnp.bfloat16),
        compiler_params=pltpu.CompilerParams(vmem_limit_bytes=48 * 1024 * 1024),
        cost_estimate=pl.CostEstimate(
            flops=0,
            bytes_accessed=0,
            transcendentals=0,
        ),
        name="attention",
    )(where, own, right, left)


def whole_lanes(columns):
    return -(-columns // LANES) * LANES


def on_diagonal():
    row = lax.broadcasted_iota(jnp.int32, (LANES, LANES), 0)
    return row == lax.broadcasted_iota(jnp.int32, (LANES, LANES), 1)


def project(where, gathered, shards, total, columns, peers):
    stream_count = len(gathered)
    home = [
        {key: (n, at) for n, (keys, _) in enumerate(stacks) for at, key in enumerate(keys)}
        for stacks in gathered
    ]
    clip_count = 1 + max(clip for _, clip in home[0])
    place_count = 1 + max(place for place, _ in home[0])
    _, block_rows, depth = gathered[0][0][1].shape
    lanes = whole_lanes(columns)
    row_count = stream_count * block_rows
    shard_total = len(shards)
    flat = [array for stacks in gathered for _, array in stacks]
    base = [sum(len(stacks) for stacks in gathered[:n]) for n in range(stream_count)]

    def kernel(where_ref, *refs):
        slab, model, own_clip = where_ref[0], where_ref[1], where_ref[2]
        block_refs = refs[: len(flat)]
        weight_refs = refs[len(flat) : len(flat) + shard_total]
        total_ref = refs[len(flat) + shard_total] if total is not None else None
        rows = refs[-1]
        out_ref = refs[len(operands)]
        squares_ref = refs[len(operands) + 1]
        if total is None:
            out_ref[...] = jnp.zeros_like(out_ref)
        else:
            out_ref[...] = total_ref[...]

        for shard, (first, array, place_of, exists) in enumerate(shards):

            @pl.when(exists(slab))
            def _():
                held = rows.at[shard % 2]
                for place in range(place_count):

                    @pl.when((place_of(slab) ^ model) == place)
                    def _():
                        for clip in range(clip_count):
                            for stream in range(stream_count):
                                stack, at = home[stream][place, clip]
                                begin = (clip ^ own_clip) * row_count + stream * block_rows
                                held[pl.ds(pl.multiple_of(begin, 16), block_rows)] = block_refs[
                                    base[stream] + stack
                                ][at]

                out_ref[:, pl.ds(first, array.shape[0])] += lax.dot_general(
                    held[...],
                    weight_refs[shard][...],
                    (((1,), (1,)), ((), ())),
                    preferred_element_type=jnp.float32,
                )

        if peers:
            diagonal = on_diagonal()
            for first in range(0, clip_count * row_count, LANES):
                piece = out_ref[pl.ds(first, LANES)]
                sums = jnp.sum(piece * piece, axis=1, keepdims=True)
                sums = jnp.sum(jnp.where(diagonal, sums, 0.0), axis=0, keepdims=True)
                squares_ref[:, :, pl.ds(first, LANES)] = jnp.broadcast_to(
                    sums[None], (peers, 1, LANES)
                )

    operands = [*flat, *(array for _, array, _, _ in shards)]
    aliases = {}
    if total is not None:
        operands.append(total)
        aliases = {len(operands): 0}
    in_specs = [pl.BlockSpec(memory_space=pltpu.VMEM) for _ in operands]
    out_shape = [jax.ShapeDtypeStruct((clip_count * row_count, lanes), jnp.float32)]
    if peers:
        out_shape.append(jax.ShapeDtypeStruct((peers, 1, clip_count * row_count), jnp.float32))
    return pl.pallas_call(
        kernel,
        in_specs=[pl.BlockSpec(memory_space=pltpu.SMEM)] + in_specs,
        out_specs=[pl.BlockSpec(memory_space=pltpu.VMEM)] * len(out_shape),
        out_shape=out_shape,
        scratch_shapes=[pltpu.VMEM((2, clip_count * row_count, depth), jnp.bfloat16)],
        input_output_aliases=aliases,
        compiler_params=pltpu.CompilerParams(vmem_limit_bytes=(16 + shard_total) * 1024 * 1024),
        cost_estimate=pl.CostEstimate(
            flops=0,
            bytes_accessed=0,
            transcendentals=0,
        ),
        name="project",
    )(where, *operands)


def row_scales(squares_ref, clip, row_count, model_width):
    diagonal = on_diagonal()
    scales = []
    for first in range(0, row_count, LANES):
        at = pl.ds(clip * row_count + first, LANES)
        mean = jnp.sum(squares_ref[:, :, at], axis=0) / model_width
        scale = jnp.broadcast_to(lax.rsqrt(mean + epsilon), (LANES, LANES))
        scales.append(jnp.sum(jnp.where(diagonal, scale, 0.0), axis=1, keepdims=True))
    return jnp.concatenate(scales, axis=0)


def finish(total, squares, gain, clip_count, columns, model_width, devices):
    rows, lanes = total.shape
    row_count = rows // clip_count
    near_rows = row_count // 2

    def kernel(total_ref, squares_ref, gain_ref, row_ref):
        lane = lax.broadcasted_iota(jnp.int32, (1, lanes), 1)
        row = jnp.zeros((1, lanes), jnp.float32)
        for clip in range(clip_count):
            scale = row_scales(squares_ref, clip, row_count, model_width)
            clean = total_ref[pl.ds(clip * row_count, near_rows)] * scale[:near_rows]
            difference = total_ref[pl.ds(clip * row_count + near_rows, near_rows)] * scale[near_rows:] - clean
            sums = jnp.sum(difference * difference, axis=0, keepdims=True)
            penalty = jnp.sum(sums * gain_ref[...] * gain_ref[...], axis=1, keepdims=True)
            row = row + sums + jnp.where(lane == columns + clip, penalty, 0.0)
        row_ref[...] = jnp.broadcast_to(row[None], row_ref.shape)

    return pl.pallas_call(
        kernel,
        out_shape=jax.ShapeDtypeStruct((devices, 1, lanes), jnp.float32),
        compiler_params=pltpu.CompilerParams(vmem_limit_bytes=16 * 1024 * 1024),
        name="finish",
    )(total, squares, gain)


def make_features(total, squares, gain, clip_count, model_width):
    rows, lanes = total.shape
    row_count = rows // clip_count
    near_rows = row_count // 2

    def kernel(total_ref, squares_ref, gain_ref, features_ref):
        for clip in range(clip_count):
            scale = row_scales(squares_ref, clip, row_count, model_width)
            clean = total_ref[pl.ds(clip * row_count, near_rows)] * scale[:near_rows]
            features_ref[clip] = (clean * gain_ref[...]).astype(jnp.bfloat16)

    return pl.pallas_call(
        kernel,
        out_shape=jax.ShapeDtypeStruct((clip_count, near_rows, lanes), jnp.bfloat16),
        compiler_params=pltpu.CompilerParams(vmem_limit_bytes=16 * 1024 * 1024),
        cost_estimate=pl.CostEstimate(
            flops=10**10, bytes_accessed=0, transcendentals=0
        ),
        name="make_features",
    )(total, squares, gain)


def conclude(rows, where, gain, model_count, clip_count, tokens):
    devices, _, lanes = rows.shape
    columns = gain.shape[1] // clip_count
    model_width = gain.shape[1] * model_count

    def kernel(where_ref, rows_ref, gain_ref, penalty_ref, grad_ref):
        row = lax.broadcasted_iota(jnp.int32, (devices, 1, lanes), 0)
        model = (row // clip_count) % model_count
        sums = []
        for clip in range(clip_count):
            mine = (model == where_ref[1]) & (row % clip_count == clip)
            sums.append(jnp.sum(jnp.where(mine, rows_ref[...], 0.0), axis=0)[:, :columns])
        sums = jnp.concatenate(sums, axis=1)
        grad = gain_ref[...] * sums / (sigma_noise * sigma_noise * tokens)
        grad_ref[...] = grad.reshape(grad_ref.shape)
        lane = lax.broadcasted_iota(jnp.int32, (devices, 1, lanes), 2)
        own = jnp.where(lane == columns + where_ref[2], rows_ref[...], 0.0)
        penalty_ref[0] = jnp.sum(own) / (sigma_noise * sigma_noise * tokens * model_width)

    return pl.pallas_call(
        kernel,
        in_specs=[pl.BlockSpec(memory_space=pltpu.SMEM)]
        + [pl.BlockSpec(memory_space=pltpu.VMEM)] * 2,
        out_specs=[
            pl.BlockSpec(memory_space=pltpu.SMEM),
            pl.BlockSpec(memory_space=pltpu.VMEM),
        ],
        out_shape=[
            jax.ShapeDtypeStruct((1,), jnp.float32),
            jax.ShapeDtypeStruct((gain.shape[1],), jnp.float32),
        ],
        compiler_params=pltpu.CompilerParams(vmem_limit_bytes=4 * 1024 * 1024),
        name="conclude",
    )(where, rows, gain)


def swap(array, axis, distance):
    count = lax.axis_size(axis)
    return lax.ppermute(array, axis, [(i, i ^ distance) for i in range(count)])


def distances(axis):
    count = lax.axis_size(axis)
    return [(axis, 1 << bit) for bit in reversed(range(count.bit_length() - 1))]


def spread(block, order, before_step):
    stacks = [([(0, 0)], block[None])]
    for step, (axis, distance) in enumerate(order):
        if step < len(order) - 1 and len(stacks) > 1:
            keys = [key for some, _ in stacks for key in some]
            stacks = [(keys, jnp.concatenate([array for _, array in stacks]))]
        received = []
        for part, (keys, array) in enumerate(stacks):
            keys = [(m ^ distance, c) if axis == "mp" else (m, c ^ distance) for m, c in keys]
            received.append((keys, swap(before_step(step, part, array), axis, distance)))
        stacks = stacks + received
    return stacks


def collect(rows, axes):
    return lax.all_to_all(rows, axes, split_axis=0, concat_axis=0, tiled=True)


def pick(options, index):
    return lax.select_n(index, *options) if len(options) > 1 else options[0]


def local(projections, perturbation, out_weight, norm_gain, live_counts):
    tile_len = projections.shape[2]
    local_width = projections.shape[4]
    slots = projections.shape[1]
    slab_count = lax.axis_size("frames")
    slab_index = lax.axis_index("frames")
    model_count = lax.axis_size("mp")
    model_index = lax.axis_index("mp")
    clip_count = lax.axis_size("dp")
    clip_index = lax.axis_index("dp")
    model_width = local_width * model_count
    token_total = slots * slab_count * tile_len
    half = local_width // clip_count
    near_rows = slots * tile_len

    def own_columns(array):
        return pick(
            [array[..., n * half : (n + 1) * half] for n in range(clip_count)], clip_index
        )

    clean = projections[0].transpose(0, 2, 1, 3)
    noise = perturbation[0].transpose(0, 2, 1, 3)
    up = [(i, i + 1) for i in range(slab_count - 1)]
    down = [(i + 1, i) for i in range(slab_count - 1)]

    tail, head = prepare_halo(clean, noise, (slots - 1, 0))
    tail, head, clean, noise, out_weight = lax.optimization_barrier(
        (tail, head, clean, noise, out_weight)
    )
    right = lax.ppermute(head, "frames", down)
    left = lax.ppermute(tail, "frames", up)
    streams = (clean, perturb(clean, noise))
    counts = jnp.pad(live_counts[0], (1, 1))
    nearby = lax.dynamic_slice_in_dim(counts, slots * slab_index, slots + 2)
    where = jnp.concatenate(
        [jnp.stack([slab_index, model_index, clip_index]).astype(jnp.int32), nearby]
    )
    gain_row = jnp.pad(own_columns(norm_gain), (0, whole_lanes(half) - half))[None]
    gain_all = norm_gain[None]

    cut = min(LANES, half // 2)
    own_weight, *parts = prepare_weight(where, out_weight, clip_count, cut)
    line = slab_count == model_count and slab_count == 4
    last = slab_count - 1
    near, passed, across = [], [], []

    if line:
        near = [lax.ppermute(own_weight, "frames", pairs) for pairs in (down, up)]
        across = [
            lax.ppermute(block, "frames", [(0, last), (last, 0)]) for block in parts
        ]

    def before_step(stream, step, part, value):
        nonlocal near, passed, gain_row, gain_all
        if line and stream == 0 and step == 1:
            value, near, gain_row, gain_all = lax.optimization_barrier(
                (value, near, gain_row, gain_all)
            )
            passed = [
                lax.ppermute(near[0], "frames", down[:2]),
                lax.ppermute(near[1], "frames", up[1:]),
            ]
        if line and stream == 1 and step == 1:
            value, across[0] = lax.optimization_barrier((value, across[0]))
        if line and stream == 1 and step == 2 and part == 1:
            value, passed = lax.optimization_barrier((value, passed))
        return value

    gathered = []
    orders = (
        distances("dp") + distances("mp"),
        distances("mp")[:1] + distances("dp") + distances("mp")[1:],
    )
    for n, order in enumerate(orders):
        attended = attention(where, streams[n], left, right, n).reshape(near_rows, local_width)
        gathered.append(
            spread(attended, order, lambda *at, n=n: before_step(n, *at))
        )

    peers = model_count * clip_count
    if line:
        shards = [
            (0, own_weight, lambda slab: slab, lambda slab: slab >= 0),
            (0, near[0], lambda slab: jnp.minimum(slab + 1, last), lambda slab: slab < last),
            (0, near[1], lambda slab: jnp.maximum(slab - 1, 0), lambda slab: slab > 0),
            (0, passed[0], lambda slab: jnp.minimum(slab + 2, last), lambda slab: slab < 2),
            (0, passed[1], lambda slab: jnp.maximum(slab - 2, 0), lambda slab: slab >= 2),
        ]
        for first, block in zip((0, cut), across):
            shards.append(
                (first, block, lambda slab: last - slab, lambda slab: (slab == 0) | (slab == last))
            )
        (total,) = project(where, gathered, shards[:-1], None, half, 0)
        total, squares = project(where, gathered, shards[-1:], total, half, peers)
    else:
        weight = lax.all_gather(own_weight, "frames", axis=1, tiled=True)
        shards = [
            (
                0,
                lax.dynamic_slice_in_dim(weight, m * local_width, local_width, axis=1),
                lambda slab, m=m: m,
                lambda slab: slab >= 0,
            )
            for m in range(model_count)
        ]
        total, squares = project(where, gathered, shards, None, half, peers)

    squares = collect(squares, ("mp", "dp"))
    sums = finish(
        total,
        squares,
        gain_row,
        clip_count,
        half,
        model_width,
        slab_count * model_count * clip_count,
    )
    features = make_features(total, squares, gain_row, clip_count, model_width)
    sums = collect(sums, ("frames", "mp", "dp"))

    features = features[..., :half].reshape(clip_count, slots, tile_len, half)
    columns = [pick([features[d] for d in range(clip_count)], clip_index)]
    for distance in range(1, clip_count):
        sent = pick([features[d ^ distance] for d in range(clip_count)], clip_index)
        columns.append(swap(sent, "dp", distance))
    features = jnp.concatenate(
        [
            pick([columns[n ^ d] for d in range(clip_count)], clip_index)
            for n in range(clip_count)
        ],
        axis=-1,
    )[None]
    sums, features = lax.optimization_barrier((sums, features))
    penalty, gain_grad = conclude(
        sums, where, gain_all, model_count, clip_count, token_total
    )
    return (features, penalty, gain_grad)


def solution(mesh):
    placed = (
        P("dp", "frames", None, None, "mp"),
        P("dp", "frames", None, None, "mp"),
        P("frames", "mp"),
        P("mp"),
        P("dp", None),
    )
    return jax.shard_map(
        local,
        mesh=mesh,
        in_specs=placed,
        out_specs=(P("dp", "frames", None, "mp"), P("dp"), P("mp")),
        check_vma=False,
    )
```

```python
import math

import jax
import jax.numpy as jnp
from jax import lax
from jax.experimental import pallas as pl
from jax.experimental.pallas import tpu as pltpu
from jax.sharding import PartitionSpec as P

HEAD_DIM = 128
HEADS_AT_ONCE = 1
LANES = 128


sigma_noise = 0.25
epsilon = 1e-06


def perturb(clean, noise):
    return (clean.astype(jnp.float32) + sigma_noise * noise.astype(jnp.float32)).astype(jnp.bfloat16)


def prepare_halo(clean, noise, slots):
    _, _, tile_len, width = clean.shape

    def kernel(clean_ref, noise_ref, *refs):
        out_refs, (keep, add, in_sems, out_sems) = refs[: len(slots)], refs[len(slots) :]
        pieces = [(n, slot, part) for n, slot in enumerate(slots) for part in range(2)]
        loads, stores = [], []
        for n, slot, part in pieces:
            for m, (source, target) in enumerate(((clean_ref, keep), (noise_ref, add))):
                loads.append(
                    pltpu.make_async_copy(
                        source.at[slot, 1 + part], target.at[n, part], in_sems.at[n, part, m]
                    )
                )
                loads[-1].start()
        for at, (n, slot, part) in enumerate(pieces):
            loads[2 * at].wait()
            loads[2 * at + 1].wait()
            add[n, part] = perturb(keep[n, part], add[n, part])
            for m, source in enumerate((keep, add)):
                stores.append(
                    pltpu.make_async_copy(
                        source.at[n, part], out_refs[n].at[m, part], out_sems.at[n, part, m]
                    )
                )
                stores[-1].start()
        for store in stores:
            store.wait()

    scratch = pltpu.VMEM((len(slots), 2, tile_len, width), jnp.bfloat16)
    return pl.pallas_call(
        kernel,
        in_specs=[pl.BlockSpec(memory_space=pl.ANY)] * 2,
        out_specs=[pl.BlockSpec(memory_space=pl.ANY)] * len(slots),
        out_shape=[jax.ShapeDtypeStruct((2, 2, tile_len, width), jnp.bfloat16)] * len(slots),
        scratch_shapes=[
            scratch,
            scratch,
            pltpu.SemaphoreType.DMA((len(slots), 2, 2)),
            pltpu.SemaphoreType.DMA((len(slots), 2, 2)),
        ],
        compiler_params=pltpu.CompilerParams(vmem_limit_bytes=60 * 1024 * 1024),
        name="prepare_halo",
    )(clean, noise)


def prepare_weight(where, weight, clip_count):
    depth, width = weight.shape
    half = width // clip_count

    def kernel(where_ref, weight_ref, out_ref):
        for clip in range(clip_count):

            @pl.when(where_ref[2] == clip)
            def _():
                begin, end = clip * half, (clip + 1) * half
                for first in range(begin // LANES * LANES, end, LANES):
                    low, high = max(first, begin), min(first + LANES, end)
                    turned = weight_ref[:, pl.ds(first, LANES)].T
                    out_ref[pl.ds(low - begin, high - low)] = turned[low - first : high - first]

    return pl.pallas_call(
        kernel,
        in_specs=[
            pl.BlockSpec(memory_space=pltpu.SMEM),
            pl.BlockSpec(memory_space=pltpu.VMEM),
        ],
        out_specs=pl.BlockSpec(memory_space=pltpu.VMEM),
        out_shape=jax.ShapeDtypeStruct((half, depth), weight.dtype),
        compiler_params=pltpu.CompilerParams(vmem_limit_bytes=60 * 1024 * 1024),
        name="prepare_weight",
    )(where, weight)


def attend_kernel(where_ref, own_ref, right_ref, left_ref, out_ref):
    slots, _, tile_len, width = own_ref.shape
    key_pos = lax.broadcasted_iota(jnp.int32, (1, 2 * tile_len), 1)
    live = []
    for slot in range(slots):
        own_count = where_ref[4 + slot]
        far_count = where_ref[3 if slot == 0 else slots + 4]
        live.append((key_pos < own_count) | ((key_pos >= tile_len) & (key_pos < tile_len + far_count)))
    row_pos = lax.broadcasted_iota(jnp.int32, (tile_len, 1), 0)
    units = [(slot, head) for head in range(width // HEAD_DIM) for slot in range(slots)]

    scores = []
    for slot, head in units:
        cols = pl.ds(head * HEAD_DIM, HEAD_DIM)
        halo_ref = left_ref if slot == 0 else right_ref
        keys = jnp.concatenate([own_ref[slot, 1, :, cols], halo_ref[0, :, cols]], axis=0)
        raw = lax.dot_general(
            own_ref[slot, 0, :, cols],
            keys,
            (((1,), (1,)), ((), ())),
            preferred_element_type=jnp.float32,
        )
        scores.append(jnp.where(live[slot], raw * (1.0 / math.sqrt(HEAD_DIM)), jnp.float32(-1e30)))
    largest = [jnp.max(s, axis=-1, keepdims=True) for s in scores]
    weights = [jnp.exp(s - top) for s, top in zip(scores, largest)]
    totals = [jnp.sum(w, axis=-1, keepdims=True) for w in weights]
    for (slot, head), weight, total in zip(units, weights, totals):
        cols = pl.ds(head * HEAD_DIM, HEAD_DIM)
        halo_ref = left_ref if slot == 0 else right_ref
        values = jnp.concatenate([own_ref[slot, 2, :, cols], halo_ref[1, :, cols]], axis=0)
        probabilities = (weight * (1.0 / total)).astype(jnp.bfloat16)
        mixed = jnp.dot(probabilities, values, preferred_element_type=jnp.float32)
        out_ref[slot, :, cols] = jnp.where(row_pos < where_ref[4 + slot], mixed, 0.0).astype(
            jnp.bfloat16
        )


def attention(where, own, left, right, stream):
    slots, _, tile_len, width = own.shape
    block = HEADS_AT_ONCE * HEAD_DIM
    own_spec = pl.BlockSpec((slots, 3, tile_len, block), lambda h, c: (0, 0, 0, h))
    halo_spec = pl.BlockSpec((None, 2, tile_len, block), lambda h, c: (stream, 0, 0, h))
    return pl.pallas_call(
        attend_kernel,
        grid_spec=pltpu.PrefetchScalarGridSpec(
            num_scalar_prefetch=1,
            grid=(width // block,),
            in_specs=[own_spec, halo_spec, halo_spec],
            out_specs=pl.BlockSpec((slots, tile_len, block), lambda h, c: (0, 0, h)),
        ),
        out_shape=jax.ShapeDtypeStruct((slots, tile_len, width), jnp.bfloat16),
        compiler_params=pltpu.CompilerParams(vmem_limit_bytes=48 * 1024 * 1024),
        cost_estimate=pl.CostEstimate(
            flops=0,
            bytes_accessed=0,
            transcendentals=0,
        ),
        name="attention",
    )(where, own, right, left)


def whole_lanes(columns):
    return -(-columns // LANES) * LANES


def on_diagonal():
    row = lax.broadcasted_iota(jnp.int32, (LANES, LANES), 0)
    return row == lax.broadcasted_iota(jnp.int32, (LANES, LANES), 1)


def project(where, gathered, shards, total, columns, peers):
    stream_count = len(gathered)
    home = [
        {key: (n, at) for n, (keys, _) in enumerate(stacks) for at, key in enumerate(keys)}
        for stacks in gathered
    ]
    clip_count = 1 + max(clip for _, clip in home[0])
    place_count = 1 + max(place for place, _ in home[0])
    _, block_rows, depth = gathered[0][0][1].shape
    lanes = whole_lanes(columns)
    row_count = stream_count * block_rows
    shard_total = len(shards)
    flat = [array for stacks in gathered for _, array in stacks]
    base = [sum(len(stacks) for stacks in gathered[:n]) for n in range(stream_count)]

    def kernel(where_ref, *refs):
        slab, model, own_clip = where_ref[0], where_ref[1], where_ref[2]
        block_refs = refs[: len(flat)]
        weight_refs = refs[len(flat) : len(flat) + shard_total]
        total_ref = refs[len(flat) + shard_total] if total is not None else None
        rows = refs[-1]
        out_ref = refs[len(operands)]
        squares_ref = refs[len(operands) + 1]
        if total is None:
            out_ref[...] = jnp.zeros_like(out_ref)
        else:
            out_ref[...] = total_ref[...]

        for shard, (first, array, place_of, exists) in enumerate(shards):

            @pl.when(exists(slab))
            def _():
                held = rows.at[shard % 2]
                for place in range(place_count):

                    @pl.when((place_of(slab) ^ model) == place)
                    def _():
                        for clip in range(clip_count):
                            for stream in range(stream_count):
                                stack, at = home[stream][place, clip]
                                begin = (clip ^ own_clip) * row_count + stream * block_rows
                                held[pl.ds(pl.multiple_of(begin, 16), block_rows)] = block_refs[
                                    base[stream] + stack
                                ][at]

                out_ref[:, pl.ds(first, array.shape[0])] += lax.dot_general(
                    held[...],
                    weight_refs[shard][...],
                    (((1,), (1,)), ((), ())),
                    preferred_element_type=jnp.float32,
                )

        if peers:
            diagonal = on_diagonal()
            for first in range(0, clip_count * row_count, LANES):
                piece = out_ref[pl.ds(first, LANES)]
                sums = jnp.sum(piece * piece, axis=1, keepdims=True)
                sums = jnp.sum(jnp.where(diagonal, sums, 0.0), axis=0, keepdims=True)
                squares_ref[:, :, pl.ds(first, LANES)] = jnp.broadcast_to(
                    sums[None], (peers, 1, LANES)
                )

    operands = [*flat, *(array for _, array, _, _ in shards)]
    aliases = {}
    if total is not None:
        operands.append(total)
        aliases = {len(operands): 0}
    in_specs = [pl.BlockSpec(memory_space=pltpu.VMEM) for _ in operands]
    out_shape = [jax.ShapeDtypeStruct((clip_count * row_count, lanes), jnp.float32)]
    if peers:
        out_shape.append(jax.ShapeDtypeStruct((peers, 1, clip_count * row_count), jnp.float32))
    return pl.pallas_call(
        kernel,
        in_specs=[pl.BlockSpec(memory_space=pltpu.SMEM)] + in_specs,
        out_specs=[pl.BlockSpec(memory_space=pltpu.VMEM)] * len(out_shape),
        out_shape=out_shape,
        scratch_shapes=[pltpu.VMEM((2, clip_count * row_count, depth), jnp.bfloat16)],
        input_output_aliases=aliases,
        compiler_params=pltpu.CompilerParams(vmem_limit_bytes=(16 + shard_total) * 1024 * 1024),
        cost_estimate=pl.CostEstimate(
            flops=0,
            bytes_accessed=0,
            transcendentals=0,
        ),
        name="project",
    )(where, *operands)


def row_scales(squares_ref, clip, row_count, model_width):
    diagonal = on_diagonal()
    scales = []
    for first in range(0, row_count, LANES):
        at = pl.ds(clip * row_count + first, LANES)
        mean = jnp.sum(squares_ref[:, :, at], axis=0) / model_width
        scale = jnp.broadcast_to(lax.rsqrt(mean + epsilon), (LANES, LANES))
        scales.append(jnp.sum(jnp.where(diagonal, scale, 0.0), axis=1, keepdims=True))
    return jnp.concatenate(scales, axis=0)


def finish(total, squares, gain, clip_count, columns, model_width, devices):
    rows, lanes = total.shape
    row_count = rows // clip_count
    near_rows = row_count // 2

    def kernel(total_ref, squares_ref, gain_ref, row_ref):
        lane = lax.broadcasted_iota(jnp.int32, (1, lanes), 1)
        row = jnp.zeros((1, lanes), jnp.float32)
        for clip in range(clip_count):
            scale = row_scales(squares_ref, clip, row_count, model_width)
            clean = total_ref[pl.ds(clip * row_count, near_rows)] * scale[:near_rows]
            difference = total_ref[pl.ds(clip * row_count + near_rows, near_rows)] * scale[near_rows:] - clean
            sums = jnp.sum(difference * difference, axis=0, keepdims=True)
            penalty = jnp.sum(sums * gain_ref[...] * gain_ref[...], axis=1, keepdims=True)
            row = row + sums + jnp.where(lane == columns + clip, penalty, 0.0)
        row_ref[...] = jnp.broadcast_to(row[None], row_ref.shape)

    return pl.pallas_call(
        kernel,
        out_shape=jax.ShapeDtypeStruct((devices, 1, lanes), jnp.float32),
        compiler_params=pltpu.CompilerParams(vmem_limit_bytes=16 * 1024 * 1024),
        name="finish",
    )(total, squares, gain)


def make_features(total, squares, gain, clip_count, model_width):
    rows, lanes = total.shape
    row_count = rows // clip_count
    near_rows = row_count // 2

    def kernel(total_ref, squares_ref, gain_ref, features_ref):
        for clip in range(clip_count):
            scale = row_scales(squares_ref, clip, row_count, model_width)
            clean = total_ref[pl.ds(clip * row_count, near_rows)] * scale[:near_rows]
            features_ref[clip] = (clean * gain_ref[...]).astype(jnp.bfloat16)

    return pl.pallas_call(
        kernel,
        out_shape=jax.ShapeDtypeStruct((clip_count, near_rows, lanes), jnp.bfloat16),
        compiler_params=pltpu.CompilerParams(vmem_limit_bytes=16 * 1024 * 1024),
        cost_estimate=pl.CostEstimate(
            flops=10**10, bytes_accessed=0, transcendentals=0
        ),
        name="make_features",
    )(total, squares, gain)


def conclude(rows, where, gain, model_count, clip_count, tokens):
    devices, _, lanes = rows.shape
    columns = gain.shape[1] // clip_count
    model_width = gain.shape[1] * model_count

    def kernel(where_ref, rows_ref, gain_ref, penalty_ref, grad_ref):
        row = lax.broadcasted_iota(jnp.int32, (devices, 1, lanes), 0)
        model = (row // clip_count) % model_count
        sums = []
        for clip in range(clip_count):
            mine = (model == where_ref[1]) & (row % clip_count == clip)
            sums.append(jnp.sum(jnp.where(mine, rows_ref[...], 0.0), axis=0)[:, :columns])
        sums = jnp.concatenate(sums, axis=1)
        grad = gain_ref[...] * sums / (sigma_noise * sigma_noise * tokens)
        grad_ref[...] = grad.reshape(grad_ref.shape)
        lane = lax.broadcasted_iota(jnp.int32, (devices, 1, lanes), 2)
        own = jnp.where(lane == columns + where_ref[2], rows_ref[...], 0.0)
        penalty_ref[0] = jnp.sum(own) / (sigma_noise * sigma_noise * tokens * model_width)

    return pl.pallas_call(
        kernel,
        in_specs=[pl.BlockSpec(memory_space=pltpu.SMEM)]
        + [pl.BlockSpec(memory_space=pltpu.VMEM)] * 2,
        out_specs=[
            pl.BlockSpec(memory_space=pltpu.SMEM),
            pl.BlockSpec(memory_space=pltpu.VMEM),
        ],
        out_shape=[
            jax.ShapeDtypeStruct((1,), jnp.float32),
            jax.ShapeDtypeStruct((gain.shape[1],), jnp.float32),
        ],
        compiler_params=pltpu.CompilerParams(vmem_limit_bytes=4 * 1024 * 1024),
        name="conclude",
    )(where, rows, gain)


def swap(array, axis, distance):
    count = lax.axis_size(axis)
    return lax.ppermute(array, axis, [(i, i ^ distance) for i in range(count)])


def distances(axis):
    count = lax.axis_size(axis)
    return [(axis, 1 << bit) for bit in reversed(range(count.bit_length() - 1))]


def spread(block, order, before_step):
    stacks = [([(0, 0)], block[None])]
    for step, (axis, distance) in enumerate(order):
        if step < len(order) - 1 and len(stacks) > 1:
            keys = [key for some, _ in stacks for key in some]
            stacks = [(keys, jnp.concatenate([array for _, array in stacks]))]
        elif len(stacks) > 1:
            arrays = lax.optimization_barrier([array for _, array in stacks])
            stacks = [(keys, array) for (keys, _), array in zip(stacks, arrays)]
        received = []
        for part, (keys, array) in enumerate(stacks):
            keys = [(m ^ distance, c) if axis == "mp" else (m, c ^ distance) for m, c in keys]
            received.append((keys, swap(before_step(step, part, array), axis, distance)))
        stacks = stacks + received
    return stacks


def collect(rows, axes):
    return lax.all_to_all(rows, axes, split_axis=0, concat_axis=0, tiled=True)


def pick(options, index):
    return lax.select_n(index, *options) if len(options) > 1 else options[0]


def local(projections, perturbation, out_weight, norm_gain, live_counts):
    tile_len = projections.shape[2]
    local_width = projections.shape[4]
    slots = projections.shape[1]
    slab_count = lax.axis_size("frames")
    slab_index = lax.axis_index("frames")
    model_count = lax.axis_size("mp")
    model_index = lax.axis_index("mp")
    clip_count = lax.axis_size("dp")
    clip_index = lax.axis_index("dp")
    model_width = local_width * model_count
    token_total = slots * slab_count * tile_len
    half = local_width // clip_count
    near_rows = slots * tile_len

    def own_columns(array):
        return pick(
            [array[..., n * half : (n + 1) * half] for n in range(clip_count)], clip_index
        )

    clean = projections[0].transpose(0, 2, 1, 3)
    noise = perturbation[0].transpose(0, 2, 1, 3)
    up = [(i, i + 1) for i in range(slab_count - 1)]
    down = [(i + 1, i) for i in range(slab_count - 1)]

    tail, head = prepare_halo(clean, noise, (slots - 1, 0))
    tail, head, clean, noise, out_weight = lax.optimization_barrier(
        (tail, head, clean, noise, out_weight)
    )
    right = lax.ppermute(head, "frames", down)
    left = lax.ppermute(tail, "frames", up)
    streams = (clean, perturb(clean, noise))
    counts = jnp.pad(live_counts[0], (1, 1))
    nearby = lax.dynamic_slice_in_dim(counts, slots * slab_index, slots + 2)
    where = jnp.concatenate(
        [jnp.stack([slab_index, model_index, clip_index]).astype(jnp.int32), nearby]
    )
    gain_row = jnp.pad(own_columns(norm_gain), (0, whole_lanes(half) - half))[None]
    gain_all = norm_gain[None]

    own_weight = prepare_weight(where, out_weight, clip_count)
    line = slab_count == model_count and slab_count == 4
    last = slab_count - 1
    near, passed, across = [], [], None

    if line:
        near = [lax.ppermute(own_weight, "frames", pairs) for pairs in (down, up)]
        across = lax.ppermute(own_weight, "frames", [(0, last), (last, 0)])

    def before_step(stream, step, part, value):
        nonlocal near, passed, gain_row, gain_all
        if line and stream == 0 and step == 1:
            value, near, gain_row, gain_all = lax.optimization_barrier(
                (value, near, gain_row, gain_all)
            )
            passed = [
                lax.ppermute(near[0], "frames", down[:2]),
                lax.ppermute(near[1], "frames", up[1:]),
            ]
        if line and stream == 1 and step == 2 and part == 1:
            value, passed = lax.optimization_barrier((value, passed))
        return value

    gathered = []
    orders = (
        distances("dp") + distances("mp"),
        distances("mp")[:1] + distances("dp") + distances("mp")[1:],
    )
    for n, order in enumerate(orders):
        attended = attention(where, streams[n], left, right, n).reshape(near_rows, local_width)
        gathered.append(
            spread(attended, order, lambda *at, n=n: before_step(n, *at))
        )

    peers = model_count * clip_count
    if line:
        shards = [
            (0, own_weight, lambda slab: slab, lambda slab: slab >= 0),
            (0, near[0], lambda slab: jnp.minimum(slab + 1, last), lambda slab: slab < last),
            (0, near[1], lambda slab: jnp.maximum(slab - 1, 0), lambda slab: slab > 0),
            (0, passed[0], lambda slab: jnp.minimum(slab + 2, last), lambda slab: slab < 2),
            (0, passed[1], lambda slab: jnp.maximum(slab - 2, 0), lambda slab: slab >= 2),
        ]
        shards.append(
            (0, across, lambda slab: last - slab, lambda slab: (slab == 0) | (slab == last))
        )
        (total,) = project(where, gathered, shards[:-1], None, half, 0)
        total, squares = project(where, gathered, shards[-1:], total, half, peers)
    else:
        weight = lax.all_gather(own_weight, "frames", axis=1, tiled=True)
        shards = [
            (
                0,
                lax.dynamic_slice_in_dim(weight, m * local_width, local_width, axis=1),
                lambda slab, m=m: m,
                lambda slab: slab >= 0,
            )
            for m in range(model_count)
        ]
        total, squares = project(where, gathered, shards, None, half, peers)

    squares = collect(squares, ("mp", "dp"))
    sums = finish(
        total,
        squares,
        gain_row,
        clip_count,
        half,
        model_width,
        slab_count * model_count * clip_count,
    )
    features = make_features(total, squares, gain_row, clip_count, model_width)
    sums = collect(sums, ("frames", "mp", "dp"))

    features = features[..., :half].reshape(clip_count, slots, tile_len, half)
    columns = [pick([features[d] for d in range(clip_count)], clip_index)]
    for distance in range(1, clip_count):
        sent = pick([features[d ^ distance] for d in range(clip_count)], clip_index)
        columns.append(swap(sent, "dp", distance))
    features = jnp.concatenate(
        [
            pick([columns[n ^ d] for d in range(clip_count)], clip_index)
            for n in range(clip_count)
        ],
        axis=-1,
    )[None]
    sums, features = lax.optimization_barrier((sums, features))
    penalty, gain_grad = conclude(
        sums, where, gain_all, model_count, clip_count, token_total
    )
    return (features, penalty, gain_grad)


def solution(mesh):
    placed = (
        P("dp", "frames", None, None, "mp"),
        P("dp", "frames", None, None, "mp"),
        P("frames", "mp"),
        P("mp"),
        P("dp", None),
    )
    return jax.shard_map(
        local,
        mesh=mesh,
        in_specs=placed,
        out_specs=(P("dp", "frames", None, "mp"), P("dp"), P("mp")),
        check_vma=False,
    )
```

```python
import math

import jax
import jax.numpy as jnp
from jax import lax
from jax.experimental import pallas as pl
from jax.experimental.pallas import tpu as pltpu
from jax.sharding import PartitionSpec as P

HEAD_DIM = 128
HEADS_AT_ONCE = 1
LANES = 128


sigma_noise = 0.25
epsilon = 1e-06


def perturb(clean, noise):
    return (clean.astype(jnp.float32) + sigma_noise * noise.astype(jnp.float32)).astype(jnp.bfloat16)


def prepare_halo(clean, noise, slots):
    _, _, tile_len, width = clean.shape

    def kernel(clean_ref, noise_ref, *refs):
        out_refs, (keep, add, in_sems, out_sems) = refs[: len(slots)], refs[len(slots) :]
        pieces = [(n, slot, part) for n, slot in enumerate(slots) for part in range(2)]
        loads, stores = [], []
        for n, slot, part in pieces:
            for m, (source, target) in enumerate(((clean_ref, keep), (noise_ref, add))):
                loads.append(
                    pltpu.make_async_copy(
                        source.at[slot, 1 + part], target.at[n, part], in_sems.at[n, part, m]
                    )
                )
                loads[-1].start()
        for at, (n, slot, part) in enumerate(pieces):
            loads[2 * at].wait()
            loads[2 * at + 1].wait()
            add[n, part] = perturb(keep[n, part], add[n, part])
            for m, source in enumerate((keep, add)):
                stores.append(
                    pltpu.make_async_copy(
                        source.at[n, part], out_refs[n].at[m, part], out_sems.at[n, part, m]
                    )
                )
                stores[-1].start()
        for store in stores:
            store.wait()

    scratch = pltpu.VMEM((len(slots), 2, tile_len, width), jnp.bfloat16)
    return pl.pallas_call(
        kernel,
        in_specs=[pl.BlockSpec(memory_space=pl.ANY)] * 2,
        out_specs=[pl.BlockSpec(memory_space=pl.ANY)] * len(slots),
        out_shape=[jax.ShapeDtypeStruct((2, 2, tile_len, width), jnp.bfloat16)] * len(slots),
        scratch_shapes=[
            scratch,
            scratch,
            pltpu.SemaphoreType.DMA((len(slots), 2, 2)),
            pltpu.SemaphoreType.DMA((len(slots), 2, 2)),
        ],
        compiler_params=pltpu.CompilerParams(vmem_limit_bytes=60 * 1024 * 1024),
        name="prepare_halo",
    )(clean, noise)


def prepare_weight(where, weight, clip_count, cut):
    depth, width = weight.shape
    half = width // clip_count

    def kernel(where_ref, weight_ref, whole_ref, early_ref, late_ref):
        for clip in range(clip_count):

            @pl.when(where_ref[2] == clip)
            def _():
                begin, end = clip * half, (clip + 1) * half
                for first in range(begin // LANES * LANES, end, LANES):
                    low, high = max(first, begin), min(first + LANES, end)
                    turned = weight_ref[:, pl.ds(first, LANES)].T
                    whole_ref[pl.ds(low - begin, high - low)] = turned[low - first : high - first]

        early_ref[...] = whole_ref[:cut]
        late_ref[...] = whole_ref[cut:]

    return pl.pallas_call(
        kernel,
        in_specs=[
            pl.BlockSpec(memory_space=pltpu.SMEM),
            pl.BlockSpec(memory_space=pltpu.VMEM),
        ],
        out_specs=[pl.BlockSpec(memory_space=pltpu.VMEM)] * 3,
        out_shape=[
            jax.ShapeDtypeStruct((rows, depth), weight.dtype) for rows in (half, cut, half - cut)
        ],
        compiler_params=pltpu.CompilerParams(vmem_limit_bytes=60 * 1024 * 1024),
        name="prepare_weight",
    )(where, weight)


def attend_kernel(where_ref, own_ref, right_ref, left_ref, out_ref):
    slots, _, tile_len, width = own_ref.shape
    key_pos = lax.broadcasted_iota(jnp.int32, (1, 2 * tile_len), 1)
    live = []
    for slot in range(slots):
        own_count = where_ref[4 + slot]
        far_count = where_ref[3 if slot == 0 else slots + 4]
        live.append((key_pos < own_count) | ((key_pos >= tile_len) & (key_pos < tile_len + far_count)))
    row_pos = lax.broadcasted_iota(jnp.int32, (tile_len, 1), 0)
    units = [(slot, head) for head in range(width // HEAD_DIM) for slot in range(slots)]

    scores = []
    for slot, head in units:
        cols = pl.ds(head * HEAD_DIM, HEAD_DIM)
        halo_ref = left_ref if slot == 0 else right_ref
        keys = jnp.concatenate([own_ref[slot, 1, :, cols], halo_ref[0, :, cols]], axis=0)
        raw = lax.dot_general(
            own_ref[slot, 0, :, cols],
            keys,
            (((1,), (1,)), ((), ())),
            preferred_element_type=jnp.float32,
        )
        scores.append(jnp.where(live[slot], raw * (1.0 / math.sqrt(HEAD_DIM)), jnp.float32(-1e30)))
    largest = [jnp.max(s, axis=-1, keepdims=True) for s in scores]
    weights = [jnp.exp(s - top) for s, top in zip(scores, largest)]
    totals = [jnp.sum(w, axis=-1, keepdims=True) for w in weights]
    for (slot, head), weight, total in zip(units, weights, totals):
        cols = pl.ds(head * HEAD_DIM, HEAD_DIM)
        halo_ref = left_ref if slot == 0 else right_ref
        values = jnp.concatenate([own_ref[slot, 2, :, cols], halo_ref[1, :, cols]], axis=0)
        probabilities = (weight * (1.0 / total)).astype(jnp.bfloat16)
        mixed = jnp.dot(probabilities, values, preferred_element_type=jnp.float32)
        out_ref[slot, :, cols] = jnp.where(row_pos < where_ref[4 + slot], mixed, 0.0).astype(
            jnp.bfloat16
        )


def attention(where, own, left, right, stream):
    slots, _, tile_len, width = own.shape
    block = HEADS_AT_ONCE * HEAD_DIM
    own_spec = pl.BlockSpec((slots, 3, tile_len, block), lambda h, c: (0, 0, 0, h))
    halo_spec = pl.BlockSpec((None, 2, tile_len, block), lambda h, c: (stream, 0, 0, h))
    return pl.pallas_call(
        attend_kernel,
        grid_spec=pltpu.PrefetchScalarGridSpec(
            num_scalar_prefetch=1,
            grid=(width // block,),
            in_specs=[own_spec, halo_spec, halo_spec],
            out_specs=pl.BlockSpec((slots, tile_len, block), lambda h, c: (0, 0, h)),
        ),
        out_shape=jax.ShapeDtypeStruct((slots, tile_len, width), jnp.bfloat16),
        compiler_params=pltpu.CompilerParams(vmem_limit_bytes=48 * 1024 * 1024),
        cost_estimate=pl.CostEstimate(
            flops=0,
            bytes_accessed=0,
            transcendentals=0,
        ),
        name="attention",
    )(where, own, right, left)


def whole_lanes(columns):
    return -(-columns // LANES) * LANES


def on_diagonal():
    row = lax.broadcasted_iota(jnp.int32, (LANES, LANES), 0)
    return row == lax.broadcasted_iota(jnp.int32, (LANES, LANES), 1)


def project(where, gathered, shards, columns, peers, ahead=None):
    stream_count = len(gathered)
    home = [
        {key: (n, at) for n, (keys, _) in enumerate(stacks) for at, key in enumerate(keys)}
        for stacks in gathered
    ]
    clip_count = 1 + max(clip for _, clip in home[0])
    place_count = 1 + max(place for place, _ in home[0])
    _, block_rows, depth = gathered[0][0][1].shape
    lanes = whole_lanes(columns)
    row_count = stream_count * block_rows
    flat = [array for stacks in gathered for _, array in stacks]
    base = [sum(len(stacks) for stacks in gathered[:n]) for n in range(stream_count)]

    def kernel(where_ref, *refs):
        slab, model, own_clip = where_ref[0], where_ref[1], where_ref[2]
        block_refs = refs[: len(flat)]
        weight_refs = refs[len(flat) : len(operands)]
        out_ref, other_ref, rows = refs[len(operands) :]
        out_ref[...] = jnp.zeros_like(out_ref)

        def gather_rows(wanted, held):
            for place in range(place_count):

                @pl.when((wanted ^ model) == place)
                def _():
                    for clip in range(clip_count):
                        for stream in range(stream_count):
                            stack, at = home[stream][place, clip]
                            begin = (clip ^ own_clip) * row_count + stream * block_rows
                            held[pl.ds(pl.multiple_of(begin, 16), block_rows)] = block_refs[
                                base[stream] + stack
                            ][at]

        for shard, (first, array, place_of, exists) in enumerate(shards):

            @pl.when(exists(slab))
            def _():
                held = rows.at[shard % 2]
                gather_rows(place_of(slab), held)
                out_ref[:, pl.ds(first, array.shape[0])] += lax.dot_general(
                    held[...],
                    weight_refs[shard][...],
                    (((1,), (1,)), ((), ())),
                    preferred_element_type=jnp.float32,
                )

        if ahead is None:
            put_squares(out_ref, other_ref)
        else:
            gather_rows(ahead(slab), other_ref)

    operands = [*flat, *(array for _, array, _, _ in shards)]
    total_shape = (clip_count * row_count, lanes)
    if ahead is None:
        other = jax.ShapeDtypeStruct((peers, 1, total_shape[0]), jnp.float32)
    else:
        other = jax.ShapeDtypeStruct((total_shape[0], depth), jnp.bfloat16)
    return pl.pallas_call(
        kernel,
        in_specs=[pl.BlockSpec(memory_space=pltpu.SMEM)]
        + [pl.BlockSpec(memory_space=pltpu.VMEM) for _ in operands],
        out_specs=[pl.BlockSpec(memory_space=pltpu.VMEM)] * 2,
        out_shape=[jax.ShapeDtypeStruct(total_shape, jnp.float32), other],
        scratch_shapes=[pltpu.VMEM((2, total_shape[0], depth), jnp.bfloat16)],
        compiler_params=pltpu.CompilerParams(vmem_limit_bytes=24 * 1024 * 1024),
        cost_estimate=pl.CostEstimate(flops=0, bytes_accessed=0, transcendentals=0),
        name="project",
    )(where, *operands)


def put_squares(total_ref, squares_ref):
    diagonal = on_diagonal()
    for first in range(0, total_ref.shape[0], LANES):
        piece = total_ref[pl.ds(first, LANES)]
        sums = jnp.sum(piece * piece, axis=1, keepdims=True)
        sums = jnp.sum(jnp.where(diagonal, sums, 0.0), axis=0, keepdims=True)
        squares_ref[:, :, pl.ds(first, LANES)] = jnp.broadcast_to(
            sums[None], (squares_ref.shape[0], 1, LANES)
        )


def project_last(where, rows, first, weight, exists, total, peers):
    size = weight.shape[0]

    def kernel(where_ref, rows_ref, weight_ref, total_ref, out_ref, squares_ref):
        present = exists(where_ref[0])

        @pl.when(present)
        def _():
            out_ref[:, :first] = total_ref[:, :first]
            out_ref[:, first + size :] = total_ref[:, first + size :]
            out_ref[:, pl.ds(first, size)] = total_ref[:, pl.ds(first, size)] + lax.dot_general(
                rows_ref[...],
                weight_ref[...],
                (((1,), (1,)), ((), ())),
                preferred_element_type=jnp.float32,
            )

        @pl.when(jnp.logical_not(present))
        def _():
            out_ref[...] = total_ref[...]

        put_squares(out_ref, squares_ref)

    return pl.pallas_call(
        kernel,
        in_specs=[pl.BlockSpec(memory_space=pltpu.SMEM)]
        + [pl.BlockSpec(memory_space=pltpu.VMEM)] * 3,
        out_specs=[pl.BlockSpec(memory_space=pltpu.VMEM)] * 2,
        out_shape=[
            jax.ShapeDtypeStruct(total.shape, jnp.float32),
            jax.ShapeDtypeStruct((peers, 1, total.shape[0]), jnp.float32),
        ],
        input_output_aliases={3: 0},
        compiler_params=pltpu.CompilerParams(vmem_limit_bytes=12 * 1024 * 1024),
        cost_estimate=pl.CostEstimate(flops=0, bytes_accessed=0, transcendentals=0),
        name="project_last",
    )(where, rows, weight, total)


def row_scales(squares_ref, clip, row_count, model_width):
    diagonal = on_diagonal()
    scales = []
    for first in range(0, row_count, LANES):
        at = pl.ds(clip * row_count + first, LANES)
        mean = jnp.sum(squares_ref[:, :, at], axis=0) / model_width
        scale = jnp.broadcast_to(lax.rsqrt(mean + epsilon), (LANES, LANES))
        scales.append(jnp.sum(jnp.where(diagonal, scale, 0.0), axis=1, keepdims=True))
    return jnp.concatenate(scales, axis=0)


def finish(total, squares, gain, clip_count, columns, model_width, devices):
    rows, lanes = total.shape
    row_count = rows // clip_count
    near_rows = row_count // 2

    def kernel(total_ref, squares_ref, gain_ref, row_ref):
        lane = lax.broadcasted_iota(jnp.int32, (1, lanes), 1)
        row = jnp.zeros((1, lanes), jnp.float32)
        for clip in range(clip_count):
            scale = row_scales(squares_ref, clip, row_count, model_width)
            clean = total_ref[pl.ds(clip * row_count, near_rows)] * scale[:near_rows]
            difference = total_ref[pl.ds(clip * row_count + near_rows, near_rows)] * scale[near_rows:] - clean
            sums = jnp.sum(difference * difference, axis=0, keepdims=True)
            penalty = jnp.sum(sums * gain_ref[...] * gain_ref[...], axis=1, keepdims=True)
            row = row + sums + jnp.where(lane == columns + clip, penalty, 0.0)
        row_ref[...] = jnp.broadcast_to(row[None], row_ref.shape)

    return pl.pallas_call(
        kernel,
        out_shape=jax.ShapeDtypeStruct((devices, 1, lanes), jnp.float32),
        compiler_params=pltpu.CompilerParams(vmem_limit_bytes=16 * 1024 * 1024),
        name="finish",
    )(total, squares, gain)


def make_features(total, squares, gain, after, clip_count, model_width):
    rows, lanes = total.shape
    row_count = rows // clip_count
    near_rows = row_count // 2

    def kernel(total_ref, squares_ref, gain_ref, after_ref, features_ref):
        for clip in range(clip_count):
            scale = row_scales(squares_ref, clip, row_count, model_width)
            clean = total_ref[pl.ds(clip * row_count, near_rows)] * scale[:near_rows]
            features_ref[clip] = (clean * gain_ref[...]).astype(jnp.bfloat16)

    return pl.pallas_call(
        kernel,
        in_specs=[pl.BlockSpec(memory_space=pltpu.VMEM)] * 3 + [pl.BlockSpec(memory_space=pl.ANY)],
        out_shape=jax.ShapeDtypeStruct((clip_count, near_rows, lanes), jnp.bfloat16),
        compiler_params=pltpu.CompilerParams(vmem_limit_bytes=16 * 1024 * 1024),
        cost_estimate=pl.CostEstimate(flops=0, bytes_accessed=0, transcendentals=0),
        name="make_features",
    )(total, squares, gain, after)


def conclude(rows, where, gain, model_count, clip_count, tokens):
    devices, _, lanes = rows.shape
    columns = gain.shape[1] // clip_count
    model_width = gain.shape[1] * model_count

    def kernel(where_ref, rows_ref, gain_ref, penalty_ref, grad_ref):
        row = lax.broadcasted_iota(jnp.int32, (devices, 1, lanes), 0)
        model = (row // clip_count) % model_count
        sums = []
        for clip in range(clip_count):
            mine = (model == where_ref[1]) & (row % clip_count == clip)
            sums.append(jnp.sum(jnp.where(mine, rows_ref[...], 0.0), axis=0)[:, :columns])
        sums = jnp.concatenate(sums, axis=1)
        grad = gain_ref[...] * sums / (sigma_noise * sigma_noise * tokens)
        grad_ref[...] = grad.reshape(grad_ref.shape)
        lane = lax.broadcasted_iota(jnp.int32, (devices, 1, lanes), 2)
        own = jnp.where(lane == columns + where_ref[2], rows_ref[...], 0.0)
        penalty_ref[0] = jnp.sum(own) / (sigma_noise * sigma_noise * tokens * model_width)

    return pl.pallas_call(
        kernel,
        in_specs=[pl.BlockSpec(memory_space=pltpu.SMEM)]
        + [pl.BlockSpec(memory_space=pltpu.VMEM)] * 2,
        out_specs=[
            pl.BlockSpec(memory_space=pltpu.SMEM),
            pl.BlockSpec(memory_space=pltpu.VMEM),
        ],
        out_shape=[
            jax.ShapeDtypeStruct((1,), jnp.float32),
            jax.ShapeDtypeStruct((gain.shape[1],), jnp.float32),
        ],
        compiler_params=pltpu.CompilerParams(vmem_limit_bytes=4 * 1024 * 1024),
        name="conclude",
    )(where, rows, gain)


def swap(array, axis, distance):
    count = lax.axis_size(axis)
    return lax.ppermute(array, axis, [(i, i ^ distance) for i in range(count)])


def distances(axis):
    count = lax.axis_size(axis)
    return [(axis, 1 << bit) for bit in reversed(range(count.bit_length() - 1))]


def spread(block, order, before_step):
    stacks = [([(0, 0)], block[None])]
    for step, (axis, distance) in enumerate(order):
        if step < len(order) - 1 and len(stacks) > 1:
            keys = [key for some, _ in stacks for key in some]
            stacks = [(keys, jnp.concatenate([array for _, array in stacks]))]
        received = []
        for part, (keys, array) in enumerate(stacks):
            keys = [(m ^ distance, c) if axis == "mp" else (m, c ^ distance) for m, c in keys]
            received.append((keys, swap(before_step(step, part, array), axis, distance)))
        stacks = stacks + received
    return stacks


def collect(rows, axes):
    return lax.all_to_all(rows, axes, split_axis=0, concat_axis=0, tiled=True)


def pick(options, index):
    return lax.select_n(index, *options) if len(options) > 1 else options[0]


def local(projections, perturbation, out_weight, norm_gain, live_counts):
    tile_len = projections.shape[2]
    local_width = projections.shape[4]
    slots = projections.shape[1]
    slab_count = lax.axis_size("frames")
    slab_index = lax.axis_index("frames")
    model_count = lax.axis_size("mp")
    model_index = lax.axis_index("mp")
    clip_count = lax.axis_size("dp")
    clip_index = lax.axis_index("dp")
    model_width = local_width * model_count
    token_total = slots * slab_count * tile_len
    half = local_width // clip_count
    near_rows = slots * tile_len

    def own_columns(array):
        return pick(
            [array[..., n * half : (n + 1) * half] for n in range(clip_count)], clip_index
        )

    clean = projections[0].transpose(0, 2, 1, 3)
    noise = perturbation[0].transpose(0, 2, 1, 3)
    up = [(i, i + 1) for i in range(slab_count - 1)]
    down = [(i + 1, i) for i in range(slab_count - 1)]

    tail, head = prepare_halo(clean, noise, (slots - 1, 0))
    tail, head, clean, noise, out_weight = lax.optimization_barrier(
        (tail, head, clean, noise, out_weight)
    )
    right = lax.ppermute(head, "frames", down)
    left = lax.ppermute(tail, "frames", up)
    streams = (clean, perturb(clean, noise))
    counts = jnp.pad(live_counts[0], (1, 1))
    nearby = lax.dynamic_slice_in_dim(counts, slots * slab_index, slots + 2)
    where = jnp.concatenate(
        [jnp.stack([slab_index, model_index, clip_index]).astype(jnp.int32), nearby]
    )
    gain_row = jnp.pad(own_columns(norm_gain), (0, whole_lanes(half) - half))[None]
    gain_all = norm_gain[None]

    cut = min(LANES, half // 2)
    own_weight, *parts = prepare_weight(where, out_weight, clip_count, cut)
    line = slab_count == model_count and slab_count == 4
    last = slab_count - 1
    near, passed, across = [], [], []

    if line:
        near = [lax.ppermute(own_weight, "frames", pairs) for pairs in (down, up)]
        across = [
            lax.ppermute(block, "frames", [(0, last), (last, 0)]) for block in parts
        ]

    def before_step(stream, step, part, value):
        nonlocal near, passed, gain_row, gain_all
        if line and stream == 0 and step == 1:
            value, near, gain_row, gain_all = lax.optimization_barrier(
                (value, near, gain_row, gain_all)
            )
            passed = [
                lax.ppermute(near[0], "frames", down[:2]),
                lax.ppermute(near[1], "frames", up[1:]),
            ]
        if line and stream == 1 and step == 1:
            value, across[0] = lax.optimization_barrier((value, across[0]))
        if line and stream == 1 and step == 2 and part == 1:
            value, passed = lax.optimization_barrier((value, passed))
        return value

    gathered = []
    orders = (
        distances("dp") + distances("mp"),
        distances("mp")[:1] + distances("dp") + distances("mp")[1:],
    )
    for n, order in enumerate(orders):
        attended = attention(where, streams[n], left, right, n).reshape(near_rows, local_width)
        gathered.append(
            spread(attended, order, lambda *at, n=n: before_step(n, *at))
        )

    peers = model_count * clip_count
    if line:
        shards = [
            (0, own_weight, lambda slab: slab, lambda slab: slab >= 0),
            (0, near[0], lambda slab: jnp.minimum(slab + 1, last), lambda slab: slab < last),
            (0, near[1], lambda slab: jnp.maximum(slab - 1, 0), lambda slab: slab > 0),
            (0, passed[0], lambda slab: jnp.minimum(slab + 2, last), lambda slab: slab < 2),
            (0, passed[1], lambda slab: jnp.maximum(slab - 2, 0), lambda slab: slab >= 2),
        ]
        for first, block in zip((0, cut), across):
            shards.append(
                (first, block, lambda slab: last - slab, lambda slab: (slab == 0) | (slab == last))
            )
        first, block, place_of, exists = shards.pop()
        total, rows = project(where, gathered, shards, half, peers, ahead=place_of)
        total, squares = project_last(where, rows, first, block, exists, total, peers)
    else:
        weight = lax.all_gather(own_weight, "frames", axis=1, tiled=True)
        shards = [
            (
                0,
                lax.dynamic_slice_in_dim(weight, m * local_width, local_width, axis=1),
                lambda slab, m=m: m,
                lambda slab: slab >= 0,
            )
            for m in range(model_count)
        ]
        total, squares = project(where, gathered, shards, half, peers)

    squares = collect(squares, ("mp", "dp"))
    sums = finish(
        total,
        squares,
        gain_row,
        clip_count,
        half,
        model_width,
        slab_count * model_count * clip_count,
    )
    features = make_features(total, squares, gain_row, sums, clip_count, model_width)
    sums = collect(sums, ("frames", "mp", "dp"))

    features = features[..., :half].reshape(clip_count, slots, tile_len, half)
    columns = [pick([features[d] for d in range(clip_count)], clip_index)]
    for distance in range(1, clip_count):
        sent = pick([features[d ^ distance] for d in range(clip_count)], clip_index)
        parts = jnp.split(sent.reshape(near_rows, half), 4)
        parts = [swap(part, "dp", distance) for part in parts]
        columns.append(jnp.concatenate(parts).reshape(sent.shape))
    features = jnp.concatenate(
        [
            pick([columns[n ^ d] for d in range(clip_count)], clip_index)
            for n in range(clip_count)
        ],
        axis=-1,
    )[None]
    sums, features = lax.optimization_barrier((sums, features))
    penalty, gain_grad = conclude(
        sums, where, gain_all, model_count, clip_count, token_total
    )
    return (features, penalty, gain_grad)


def solution(mesh):
    placed = (
        P("dp", "frames", None, None, "mp"),
        P("dp", "frames", None, None, "mp"),
        P("frames", "mp"),
        P("mp"),
        P("dp", None),
    )
    return jax.shard_map(
        local,
        mesh=mesh,
        in_specs=placed,
        out_specs=(P("dp", "frames", None, "mp"), P("dp"), P("mp")),
        check_vma=False,
    )
```

```python
import math

import jax
import jax.numpy as jnp
from jax import lax
from jax.experimental import pallas as pl
from jax.experimental.pallas import tpu as pltpu
from jax.sharding import PartitionSpec as P

HEAD_DIM = 128
HEADS_AT_ONCE = 1
LANES = 128


sigma_noise = 0.25
epsilon = 1e-06


def perturb(clean, noise):
    return (clean.astype(jnp.float32) + sigma_noise * noise.astype(jnp.float32)).astype(jnp.bfloat16)


def prepare_halo(clean, noise, slots):
    _, _, tile_len, width = clean.shape

    def kernel(clean_ref, noise_ref, *refs):
        out_refs, (keep, add, in_sems, out_sems) = refs[: len(slots)], refs[len(slots) :]
        pieces = [(n, slot, part) for n, slot in enumerate(slots) for part in range(2)]
        loads, stores = [], []
        for n, slot, part in pieces:
            for m, (source, target) in enumerate(((clean_ref, keep), (noise_ref, add))):
                loads.append(
                    pltpu.make_async_copy(
                        source.at[slot, 1 + part], target.at[n, part], in_sems.at[n, part, m]
                    )
                )
                loads[-1].start()
        for at, (n, slot, part) in enumerate(pieces):
            loads[2 * at].wait()
            loads[2 * at + 1].wait()
            add[n, part] = perturb(keep[n, part], add[n, part])
            for m, source in enumerate((keep, add)):
                stores.append(
                    pltpu.make_async_copy(
                        source.at[n, part], out_refs[n].at[m, part], out_sems.at[n, part, m]
                    )
                )
                stores[-1].start()
        for store in stores:
            store.wait()

    scratch = pltpu.VMEM((len(slots), 2, tile_len, width), jnp.bfloat16)
    return pl.pallas_call(
        kernel,
        in_specs=[pl.BlockSpec(memory_space=pl.ANY)] * 2,
        out_specs=[pl.BlockSpec(memory_space=pl.ANY)] * len(slots),
        out_shape=[jax.ShapeDtypeStruct((2, 2, tile_len, width), jnp.bfloat16)] * len(slots),
        scratch_shapes=[
            scratch,
            scratch,
            pltpu.SemaphoreType.DMA((len(slots), 2, 2)),
            pltpu.SemaphoreType.DMA((len(slots), 2, 2)),
        ],
        compiler_params=pltpu.CompilerParams(vmem_limit_bytes=60 * 1024 * 1024),
        name="prepare_halo",
    )(clean, noise)


def prepare_weight(where, weight, clip_count, cut):
    depth, width = weight.shape
    half = width // clip_count

    def kernel(where_ref, weight_ref, whole_ref, early_ref, late_ref):
        for clip in range(clip_count):

            @pl.when(where_ref[2] == clip)
            def _():
                begin, end = clip * half, (clip + 1) * half
                for first in range(begin // LANES * LANES, end, LANES):
                    low, high = max(first, begin), min(first + LANES, end)
                    turned = weight_ref[:, pl.ds(first, LANES)].T
                    whole_ref[pl.ds(low - begin, high - low)] = turned[low - first : high - first]

        early_ref[...] = whole_ref[:cut]
        late_ref[...] = whole_ref[cut:]

    return pl.pallas_call(
        kernel,
        in_specs=[
            pl.BlockSpec(memory_space=pltpu.SMEM),
            pl.BlockSpec(memory_space=pltpu.VMEM),
        ],
        out_specs=[pl.BlockSpec(memory_space=pltpu.VMEM)] * 3,
        out_shape=[
            jax.ShapeDtypeStruct((rows, depth), weight.dtype) for rows in (half, cut, half - cut)
        ],
        compiler_params=pltpu.CompilerParams(vmem_limit_bytes=60 * 1024 * 1024),
        name="prepare_weight",
    )(where, weight)


def attend_kernel(where_ref, own_ref, left_ref, right_ref, out_ref):
    slots, _, tile_len, width = own_ref.shape
    key_pos = lax.broadcasted_iota(jnp.int32, (1, 2 * tile_len), 1)
    live = []
    for slot in range(slots):
        own_count = where_ref[4 + slot]
        far_count = where_ref[3 if slot == 0 else slots + 4]
        live.append((key_pos < own_count) | ((key_pos >= tile_len) & (key_pos < tile_len + far_count)))
    row_pos = lax.broadcasted_iota(jnp.int32, (tile_len, 1), 0)
    units = [(slot, head) for head in range(width // HEAD_DIM) for slot in range(slots)]

    scores = []
    for slot, head in units:
        cols = pl.ds(head * HEAD_DIM, HEAD_DIM)
        halo_ref = left_ref if slot == 0 else right_ref
        keys = jnp.concatenate([own_ref[slot, 1, :, cols], halo_ref[0, :, cols]], axis=0)
        raw = lax.dot_general(
            own_ref[slot, 0, :, cols],
            keys,
            (((1,), (1,)), ((), ())),
            preferred_element_type=jnp.float32,
        )
        scores.append(jnp.where(live[slot], raw * (1.0 / math.sqrt(HEAD_DIM)), jnp.float32(-1e30)))
    largest = [jnp.max(s, axis=-1, keepdims=True) for s in scores]
    weights = [jnp.exp(s - top) for s, top in zip(scores, largest)]
    totals = [jnp.sum(w, axis=-1, keepdims=True) for w in weights]
    for (slot, head), weight, total in zip(units, weights, totals):
        cols = pl.ds(head * HEAD_DIM, HEAD_DIM)
        halo_ref = left_ref if slot == 0 else right_ref
        values = jnp.concatenate([own_ref[slot, 2, :, cols], halo_ref[1, :, cols]], axis=0)
        probabilities = (weight * (1.0 / total)).astype(jnp.bfloat16)
        mixed = jnp.dot(probabilities, values, preferred_element_type=jnp.float32)
        out_ref[slot, :, cols] = jnp.where(row_pos < where_ref[4 + slot], mixed, 0.0).astype(
            jnp.bfloat16
        )


def attention(where, own, left, right, stream):
    slots, _, tile_len, width = own.shape
    block = HEADS_AT_ONCE * HEAD_DIM
    own_spec = pl.BlockSpec((slots, 3, tile_len, block), lambda h, c: (0, 0, 0, h))
    halo_spec = pl.BlockSpec((None, 2, tile_len, block), lambda h, c: (stream, 0, 0, h))
    return pl.pallas_call(
        attend_kernel,
        grid_spec=pltpu.PrefetchScalarGridSpec(
            num_scalar_prefetch=1,
            grid=(width // block,),
            in_specs=[own_spec, halo_spec, halo_spec],
            out_specs=pl.BlockSpec((slots, tile_len, block), lambda h, c: (0, 0, h)),
        ),
        out_shape=jax.ShapeDtypeStruct((slots, tile_len, width), jnp.bfloat16),
        compiler_params=pltpu.CompilerParams(vmem_limit_bytes=48 * 1024 * 1024),
        cost_estimate=pl.CostEstimate(
            flops=0,
            bytes_accessed=0,
            transcendentals=0,
        ),
        name="attention",
    )(where, own, left, right)


def whole_lanes(columns):
    return -(-columns // LANES) * LANES


def on_diagonal():
    row = lax.broadcasted_iota(jnp.int32, (LANES, LANES), 0)
    return row == lax.broadcasted_iota(jnp.int32, (LANES, LANES), 1)


def project(where, gathered, shards, total, columns, peers):
    stream_count = len(gathered)
    home = [
        {key: (n, at) for n, (keys, _) in enumerate(stacks) for at, key in enumerate(keys)}
        for stacks in gathered
    ]
    clip_count = 1 + max(clip for _, clip in home[0])
    place_count = 1 + max(place for place, _ in home[0])
    _, block_rows, depth = gathered[0][0][1].shape
    lanes = whole_lanes(columns)
    row_count = stream_count * block_rows
    shard_total = len(shards)
    flat = [array for stacks in gathered for _, array in stacks]
    base = [sum(len(stacks) for stacks in gathered[:n]) for n in range(stream_count)]

    def kernel(where_ref, *refs):
        slab, model, own_clip = where_ref[0], where_ref[1], where_ref[2]
        block_refs = refs[: len(flat)]
        weight_refs = refs[len(flat) : len(flat) + shard_total]
        total_ref = refs[len(flat) + shard_total] if total is not None else None
        rows = refs[-1]
        out_ref = refs[len(operands)]
        squares_ref = refs[len(operands) + 1]
        if total is None:
            out_ref[...] = jnp.zeros_like(out_ref)
        else:
            out_ref[...] = total_ref[...]

        for shard, (first, array, place_of, exists) in enumerate(shards):

            @pl.when(exists(slab))
            def _():
                held = rows.at[shard % 2]
                for place in range(place_count):

                    @pl.when((place_of(slab) ^ model) == place)
                    def _():
                        for clip in range(clip_count):
                            for stream in range(stream_count):
                                stack, at = home[stream][place, clip]
                                begin = (clip ^ own_clip) * row_count + stream * block_rows
                                held[pl.ds(pl.multiple_of(begin, 16), block_rows)] = block_refs[
                                    base[stream] + stack
                                ][at]

                out_ref[:, pl.ds(first, array.shape[0])] += lax.dot_general(
                    held[...],
                    weight_refs[shard][...],
                    (((1,), (1,)), ((), ())),
                    preferred_element_type=jnp.float32,
                )

        if peers:
            diagonal = on_diagonal()
            for first in range(0, clip_count * row_count, LANES):
                piece = out_ref[pl.ds(first, LANES)]
                sums = jnp.sum(piece * piece, axis=1, keepdims=True)
                sums = jnp.sum(jnp.where(diagonal, sums, 0.0), axis=0, keepdims=True)
                squares_ref[:, :, pl.ds(first, LANES)] = jnp.broadcast_to(
                    sums[None], (peers, 1, LANES)
                )

    operands = [*flat, *(array for _, array, _, _ in shards)]
    aliases = {}
    if total is not None:
        operands.append(total)
        aliases = {len(operands): 0}
    in_specs = [pl.BlockSpec(memory_space=pltpu.VMEM) for _ in operands]
    out_shape = [jax.ShapeDtypeStruct((clip_count * row_count, lanes), jnp.float32)]
    if peers:
        out_shape.append(jax.ShapeDtypeStruct((peers, 1, clip_count * row_count), jnp.float32))
    return pl.pallas_call(
        kernel,
        in_specs=[pl.BlockSpec(memory_space=pltpu.SMEM)] + in_specs,
        out_specs=[pl.BlockSpec(memory_space=pltpu.VMEM)] * len(out_shape),
        out_shape=out_shape,
        scratch_shapes=[pltpu.VMEM((2, clip_count * row_count, depth), jnp.bfloat16)],
        input_output_aliases=aliases,
        compiler_params=pltpu.CompilerParams(vmem_limit_bytes=(16 + shard_total) * 1024 * 1024),
        cost_estimate=pl.CostEstimate(
            flops=0,
            bytes_accessed=0,
            transcendentals=0,
        ),
        name="project",
    )(where, *operands)


def row_scales(squares_ref, clip, row_count, model_width):
    diagonal = on_diagonal()
    scales = []
    for first in range(0, row_count, LANES):
        at = pl.ds(clip * row_count + first, LANES)
        mean = jnp.sum(squares_ref[:, :, at], axis=0) / model_width
        scale = jnp.broadcast_to(lax.rsqrt(mean + epsilon), (LANES, LANES))
        scales.append(jnp.sum(jnp.where(diagonal, scale, 0.0), axis=1, keepdims=True))
    return jnp.concatenate(scales, axis=0)


def finish(total, squares, gain, clip_count, columns, model_width, devices):
    rows, lanes = total.shape
    row_count = rows // clip_count
    near_rows = row_count // 2

    def kernel(total_ref, squares_ref, gain_ref, row_ref):
        lane = lax.broadcasted_iota(jnp.int32, (1, lanes), 1)
        row = jnp.zeros((1, lanes), jnp.float32)
        for clip in range(clip_count):
            scale = row_scales(squares_ref, clip, row_count, model_width)
            clean = total_ref[pl.ds(clip * row_count, near_rows)] * scale[:near_rows]
            difference = total_ref[pl.ds(clip * row_count + near_rows, near_rows)] * scale[near_rows:] - clean
            sums = jnp.sum(difference * difference, axis=0, keepdims=True)
            penalty = jnp.sum(sums * gain_ref[...] * gain_ref[...], axis=1, keepdims=True)
            row = row + sums + jnp.where(lane == columns + clip, penalty, 0.0)
        row_ref[...] = jnp.broadcast_to(row[None], row_ref.shape)

    return pl.pallas_call(
        kernel,
        out_shape=jax.ShapeDtypeStruct((devices, 1, lanes), jnp.float32),
        compiler_params=pltpu.CompilerParams(vmem_limit_bytes=16 * 1024 * 1024),
        name="finish",
    )(total, squares, gain)


def make_features(total, squares, gain, clip_count, model_width):
    rows, lanes = total.shape
    row_count = rows // clip_count
    near_rows = row_count // 2

    def kernel(total_ref, squares_ref, gain_ref, features_ref):
        for clip in range(clip_count):
            scale = row_scales(squares_ref, clip, row_count, model_width)
            clean = total_ref[pl.ds(clip * row_count, near_rows)] * scale[:near_rows]
            features_ref[clip] = (clean * gain_ref[...]).astype(jnp.bfloat16)

    return pl.pallas_call(
        kernel,
        out_shape=jax.ShapeDtypeStruct((clip_count, near_rows, lanes), jnp.bfloat16),
        compiler_params=pltpu.CompilerParams(vmem_limit_bytes=16 * 1024 * 1024),
        cost_estimate=pl.CostEstimate(
            flops=10**10, bytes_accessed=0, transcendentals=0
        ),
        name="make_features",
    )(total, squares, gain)


def conclude(rows, where, gain, model_count, clip_count, tokens):
    devices, _, lanes = rows.shape
    columns = gain.shape[1] // clip_count
    model_width = gain.shape[1] * model_count

    def kernel(where_ref, rows_ref, gain_ref, penalty_ref, grad_ref):
        row = lax.broadcasted_iota(jnp.int32, (devices, 1, lanes), 0)
        model = (row // clip_count) % model_count
        sums = []
        for clip in range(clip_count):
            mine = (model == where_ref[1]) & (row % clip_count == clip)
            sums.append(jnp.sum(jnp.where(mine, rows_ref[...], 0.0), axis=0)[:, :columns])
        sums = jnp.concatenate(sums, axis=1)
        grad = gain_ref[...] * sums / (sigma_noise * sigma_noise * tokens)
        grad_ref[...] = grad.reshape(grad_ref.shape)
        lane = lax.broadcasted_iota(jnp.int32, (devices, 1, lanes), 2)
        own = jnp.where(lane == columns + where_ref[2], rows_ref[...], 0.0)
        penalty_ref[0] = jnp.sum(own) / (sigma_noise * sigma_noise * tokens * model_width)

    return pl.pallas_call(
        kernel,
        in_specs=[pl.BlockSpec(memory_space=pltpu.SMEM)]
        + [pl.BlockSpec(memory_space=pltpu.VMEM)] * 2,
        out_specs=[
            pl.BlockSpec(memory_space=pltpu.SMEM),
            pl.BlockSpec(memory_space=pltpu.VMEM),
        ],
        out_shape=[
            jax.ShapeDtypeStruct((1,), jnp.float32),
            jax.ShapeDtypeStruct((gain.shape[1],), jnp.float32),
        ],
        compiler_params=pltpu.CompilerParams(vmem_limit_bytes=4 * 1024 * 1024),
        name="conclude",
    )(where, rows, gain)


def swap(array, axis, distance):
    count = lax.axis_size(axis)
    return lax.ppermute(array, axis, [(i, i ^ distance) for i in range(count)])


def distances(axis):
    count = lax.axis_size(axis)
    return [(axis, 1 << bit) for bit in reversed(range(count.bit_length() - 1))]


def spread(block, order, before_step):
    stacks = [([(0, 0)], block[None])]
    for step, (axis, distance) in enumerate(order):
        if step < len(order) - 1 and len(stacks) > 1:
            keys = [key for some, _ in stacks for key in some]
            stacks = [(keys, jnp.concatenate([array for _, array in stacks]))]
        received = []
        for part, (keys, array) in enumerate(stacks):
            keys = [(m ^ distance, c) if axis == "mp" else (m, c ^ distance) for m, c in keys]
            received.append((keys, swap(before_step(step, part, array), axis, distance)))
        stacks = stacks + received
    return stacks


def collect(rows, axes):
    return lax.all_to_all(rows, axes, split_axis=0, concat_axis=0, tiled=True)


def pick(options, index):
    return lax.select_n(index, *options) if len(options) > 1 else options[0]


def local(projections, perturbation, out_weight, norm_gain, live_counts):
    tile_len = projections.shape[2]
    local_width = projections.shape[4]
    slots = projections.shape[1]
    slab_count = lax.axis_size("frames")
    slab_index = lax.axis_index("frames")
    model_count = lax.axis_size("mp")
    model_index = lax.axis_index("mp")
    clip_count = lax.axis_size("dp")
    clip_index = lax.axis_index("dp")
    model_width = local_width * model_count
    token_total = slots * slab_count * tile_len
    half = local_width // clip_count
    near_rows = slots * tile_len

    def own_columns(array):
        return pick(
            [array[..., n * half : (n + 1) * half] for n in range(clip_count)], clip_index
        )

    clean = projections[0].transpose(0, 2, 1, 3)
    noise = perturbation[0].transpose(0, 2, 1, 3)
    up = [(i, i + 1) for i in range(slab_count - 1)]
    down = [(i + 1, i) for i in range(slab_count - 1)]

    tail, head = prepare_halo(clean, noise, (slots - 1, 0))
    tail, head, clean, noise, out_weight = lax.optimization_barrier(
        (tail, head, clean, noise, out_weight)
    )
    right = lax.ppermute(head, "frames", down)
    left = lax.ppermute(tail, "frames", up)
    streams = (clean, perturb(clean, noise))
    counts = jnp.pad(live_counts[0], (1, 1))
    nearby = lax.dynamic_slice_in_dim(counts, slots * slab_index, slots + 2)
    where = jnp.concatenate(
        [jnp.stack([slab_index, model_index, clip_index]).astype(jnp.int32), nearby]
    )
    gain_row = jnp.pad(own_columns(norm_gain), (0, whole_lanes(half) - half))[None]
    gain_all = norm_gain[None]

    cut = min(LANES, half // 2)
    own_weight, *parts = prepare_weight(where, out_weight, clip_count, cut)
    line = slab_count == model_count and slab_count == 4
    last = slab_count - 1
    near, passed, across = [], [], []

    if line:
        near = [lax.ppermute(own_weight, "frames", pairs) for pairs in (down, up)]
        across = [
            lax.ppermute(block, "frames", [(0, last), (last, 0)]) for block in parts
        ]

    def before_step(stream, step, part, value):
        nonlocal near, passed, gain_row, gain_all
        if line and stream == 0 and step == 1:
            value, near, gain_row, gain_all = lax.optimization_barrier(
                (value, near, gain_row, gain_all)
            )
            passed = [
                lax.ppermute(near[0], "frames", down[:2]),
                lax.ppermute(near[1], "frames", up[1:]),
            ]
        if line and stream == 1 and step == 1:
            value, across[0] = lax.optimization_barrier((value, across[0]))
        if line and stream == 1 and step == 2 and part == 1:
            value, passed = lax.optimization_barrier((value, passed))
        return value

    gathered = []
    orders = (
        distances("dp") + distances("mp"),
        distances("mp")[:1] + distances("dp") + distances("mp")[1:],
    )
    for n, order in enumerate(orders):
        attended = attention(where, streams[n], left, right, n).reshape(near_rows, local_width)
        gathered.append(
            spread(attended, order, lambda *at, n=n: before_step(n, *at))
        )

    peers = model_count * clip_count
    if line:
        shards = [
            (0, own_weight, lambda slab: slab, lambda slab: slab >= 0),
            (0, near[0], lambda slab: jnp.minimum(slab + 1, last), lambda slab: slab < last),
            (0, near[1], lambda slab: jnp.maximum(slab - 1, 0), lambda slab: slab > 0),
            (0, passed[0], lambda slab: jnp.minimum(slab + 2, last), lambda slab: slab < 2),
            (0, passed[1], lambda slab: jnp.maximum(slab - 2, 0), lambda slab: slab >= 2),
        ]
        for first, block in zip((0, cut), across):
            shards.append(
                (first, block, lambda slab: last - slab, lambda slab: (slab == 0) | (slab == last))
            )
        (total,) = project(where, gathered, shards[:-1], None, half, 0)
        total, squares = project(where, gathered, shards[-1:], total, half, peers)
    else:
        weight = lax.all_gather(own_weight, "frames", axis=1, tiled=True)
        shards = [
            (
                0,
                lax.dynamic_slice_in_dim(weight, m * local_width, local_width, axis=1),
                lambda slab, m=m: m,
                lambda slab: slab >= 0,
            )
            for m in range(model_count)
        ]
        total, squares = project(where, gathered, shards, None, half, peers)

    squares = collect(squares, ("mp", "dp"))
    sums = finish(
        total,
        squares,
        gain_row,
        clip_count,
        half,
        model_width,
        slab_count * model_count * clip_count,
    )
    features = make_features(total, squares, gain_row, clip_count, model_width)
    sums = collect(sums, ("frames", "mp", "dp"))

    features = features[..., :half].reshape(clip_count, slots, tile_len, half)
    columns = [pick([features[d] for d in range(clip_count)], clip_index)]
    for distance in range(1, clip_count):
        sent = pick([features[d ^ distance] for d in range(clip_count)], clip_index)
        columns.append(swap(sent, "dp", distance))
    features = jnp.concatenate(
        [
            pick([columns[n ^ d] for d in range(clip_count)], clip_index)
            for n in range(clip_count)
        ],
        axis=-1,
    )[None]
    sums, features = lax.optimization_barrier((sums, features))
    penalty, gain_grad = conclude(
        sums, where, gain_all, model_count, clip_count, token_total
    )
    return (features, penalty, gain_grad)


def solution(mesh):
    placed = (
        P("dp", "frames", None, None, "mp"),
        P("dp", "frames", None, None, "mp"),
        P("frames", "mp"),
        P("mp"),
        P("dp", None),
    )
    return jax.shard_map(
        local,
        mesh=mesh,
        in_specs=placed,
        out_specs=(P("dp", "frames", None, "mp"), P("dp"), P("mp")),
        check_vma=False,
    )
```

```python
import math

import jax
import jax.numpy as jnp
from jax import lax
from jax.experimental import pallas as pl
from jax.experimental.pallas import tpu as pltpu
from jax.sharding import PartitionSpec as P

HEAD_DIM = 128
HEADS_AT_ONCE = 1
LANES = 128


sigma_noise = 0.25
epsilon = 1e-06


def perturb(clean, noise):
    return (clean.astype(jnp.float32) + sigma_noise * noise.astype(jnp.float32)).astype(jnp.bfloat16)


def prepare_halo(clean, noise, slots):
    _, _, tile_len, width = clean.shape

    def kernel(clean_ref, noise_ref, *refs):
        out_refs, (keep, add, in_sems, out_sems) = refs[: len(slots)], refs[len(slots) :]
        pieces = [(n, slot, part) for n, slot in enumerate(slots) for part in range(2)]
        loads, stores = [], []
        for n, slot, part in pieces:
            for m, (source, target) in enumerate(((clean_ref, keep), (noise_ref, add))):
                loads.append(
                    pltpu.make_async_copy(
                        source.at[slot, 1 + part], target.at[n, part], in_sems.at[n, part, m]
                    )
                )
                loads[-1].start()
        for at, (n, slot, part) in enumerate(pieces):
            loads[2 * at].wait()
            loads[2 * at + 1].wait()
            add[n, part] = perturb(keep[n, part], add[n, part])
            for m, source in enumerate((keep, add)):
                stores.append(
                    pltpu.make_async_copy(
                        source.at[n, part], out_refs[n].at[m, part], out_sems.at[n, part, m]
                    )
                )
                stores[-1].start()
        for store in stores:
            store.wait()

    scratch = pltpu.VMEM((len(slots), 2, tile_len, width), jnp.bfloat16)
    return pl.pallas_call(
        kernel,
        in_specs=[pl.BlockSpec(memory_space=pl.ANY)] * 2,
        out_specs=[pl.BlockSpec(memory_space=pl.ANY)] * len(slots),
        out_shape=[jax.ShapeDtypeStruct((2, 2, tile_len, width), jnp.bfloat16)] * len(slots),
        scratch_shapes=[
            scratch,
            scratch,
            pltpu.SemaphoreType.DMA((len(slots), 2, 2)),
            pltpu.SemaphoreType.DMA((len(slots), 2, 2)),
        ],
        compiler_params=pltpu.CompilerParams(vmem_limit_bytes=60 * 1024 * 1024),
        name="prepare_halo",
    )(clean, noise)


def prepare_weight(where, weight, clip_count, cut):
    depth, width = weight.shape
    half = width // clip_count

    def kernel(where_ref, weight_ref, whole_ref, early_ref, late_ref):
        for clip in range(clip_count):

            @pl.when(where_ref[2] == clip)
            def _():
                begin, end = clip * half, (clip + 1) * half
                for first in range(begin // LANES * LANES, end, LANES):
                    low, high = max(first, begin), min(first + LANES, end)
                    turned = weight_ref[:, pl.ds(first, LANES)].T
                    whole_ref[pl.ds(low - begin, high - low)] = turned[low - first : high - first]

        early_ref[...] = whole_ref[:cut]
        late_ref[...] = whole_ref[cut:]

    return pl.pallas_call(
        kernel,
        in_specs=[
            pl.BlockSpec(memory_space=pltpu.SMEM),
            pl.BlockSpec(memory_space=pltpu.VMEM),
        ],
        out_specs=[pl.BlockSpec(memory_space=pltpu.VMEM)] * 3,
        out_shape=[
            jax.ShapeDtypeStruct((rows, depth), weight.dtype) for rows in (half, cut, half - cut)
        ],
        compiler_params=pltpu.CompilerParams(vmem_limit_bytes=60 * 1024 * 1024),
        name="prepare_weight",
    )(where, weight)


def attend_kernel(where_ref, own_ref, right_ref, left_ref, out_ref):
    slots, _, tile_len, width = own_ref.shape
    key_pos = lax.broadcasted_iota(jnp.int32, (1, 2 * tile_len), 1)
    live = []
    for slot in range(slots):
        own_count = where_ref[4 + slot]
        far_count = where_ref[3 if slot == 0 else slots + 4]
        live.append((key_pos < own_count) | ((key_pos >= tile_len) & (key_pos < tile_len + far_count)))
    row_pos = lax.broadcasted_iota(jnp.int32, (tile_len, 1), 0)
    units = [(slot, head) for head in range(width // HEAD_DIM) for slot in range(slots)]

    scores = []
    for slot, head in units:
        cols = pl.ds(head * HEAD_DIM, HEAD_DIM)
        halo_ref = left_ref if slot == 0 else right_ref
        keys = jnp.concatenate([own_ref[slot, 1, :, cols], halo_ref[0, :, cols]], axis=0)
        raw = lax.dot_general(
            own_ref[slot, 0, :, cols],
            keys,
            (((1,), (1,)), ((), ())),
            preferred_element_type=jnp.float32,
        )
        scores.append(jnp.where(live[slot], raw * (1.0 / math.sqrt(HEAD_DIM)), jnp.float32(-1e30)))
    largest = [jnp.max(s, axis=-1, keepdims=True) for s in scores]
    weights = [jnp.exp(s - top) for s, top in zip(scores, largest)]
    totals = [jnp.sum(w, axis=-1, keepdims=True) for w in weights]
    for (slot, head), weight, total in zip(units, weights, totals):
        cols = pl.ds(head * HEAD_DIM, HEAD_DIM)
        halo_ref = left_ref if slot == 0 else right_ref
        values = jnp.concatenate([own_ref[slot, 2, :, cols], halo_ref[1, :, cols]], axis=0)
        probabilities = (weight * (1.0 / total)).astype(jnp.bfloat16)
        mixed = jnp.dot(probabilities, values, preferred_element_type=jnp.float32)
        out_ref[slot, :, cols] = jnp.where(row_pos < where_ref[4 + slot], mixed, 0.0).astype(
            jnp.bfloat16
        )


def attention(where, own, left, right, stream):
    slots, _, tile_len, width = own.shape
    block = HEADS_AT_ONCE * HEAD_DIM
    own_spec = pl.BlockSpec((slots, 3, tile_len, block), lambda h, c: (0, 0, 0, h))
    halo_spec = pl.BlockSpec((None, 2, tile_len, block), lambda h, c: (stream, 0, 0, h))
    return pl.pallas_call(
        attend_kernel,
        grid_spec=pltpu.PrefetchScalarGridSpec(
            num_scalar_prefetch=1,
            grid=(width // block,),
            in_specs=[own_spec, halo_spec, halo_spec],
            out_specs=pl.BlockSpec((slots, tile_len, block), lambda h, c: (0, 0, h)),
        ),
        out_shape=jax.ShapeDtypeStruct((slots, tile_len, width), jnp.bfloat16),
        compiler_params=pltpu.CompilerParams(vmem_limit_bytes=48 * 1024 * 1024),
        cost_estimate=pl.CostEstimate(
            flops=0,
            bytes_accessed=0,
            transcendentals=0,
        ),
        name="attention",
    )(where, own, right, left)


def whole_lanes(columns):
    return -(-columns // LANES) * LANES


def on_diagonal():
    row = lax.broadcasted_iota(jnp.int32, (LANES, LANES), 0)
    return row == lax.broadcasted_iota(jnp.int32, (LANES, LANES), 1)


def project(where, gathered, shards, total, columns, peers):
    stream_count = len(gathered)
    home = [
        {key: (n, at) for n, (keys, _) in enumerate(stacks) for at, key in enumerate(keys)}
        for stacks in gathered
    ]
    clip_count = 1 + max(clip for _, clip in home[0])
    place_count = 1 + max(place for place, _ in home[0])
    _, block_rows, depth = gathered[0][0][1].shape
    lanes = whole_lanes(columns)
    row_count = stream_count * block_rows
    shard_total = len(shards)
    flat = [array for stacks in gathered for _, array in stacks]
    base = [sum(len(stacks) for stacks in gathered[:n]) for n in range(stream_count)]

    def kernel(where_ref, *refs):
        slab, model, own_clip = where_ref[0], where_ref[1], where_ref[2]
        block_refs = refs[: len(flat)]
        weight_refs = refs[len(flat) : len(flat) + shard_total]
        total_ref = refs[len(flat) + shard_total] if total is not None else None
        rows = refs[-1]
        out_ref = refs[len(operands)]
        squares_ref = refs[len(operands) + 1]
        if total is None:
            out_ref[...] = jnp.zeros_like(out_ref)
        else:
            out_ref[...] = total_ref[...]

        for shard, (first, array, place_of, exists) in enumerate(shards):

            @pl.when(exists(slab))
            def _():
                held = rows.at[shard % 2]
                for place in range(place_count):

                    @pl.when((place_of(slab) ^ model) == place)
                    def _():
                        for clip in range(clip_count):
                            for stream in range(stream_count):
                                stack, at = home[stream][place, clip]
                                begin = (clip ^ own_clip) * row_count + stream * block_rows
                                held[pl.ds(pl.multiple_of(begin, 16), block_rows)] = block_refs[
                                    base[stream] + stack
                                ][at]

                out_ref[:, pl.ds(first, array.shape[0])] += lax.dot_general(
                    held[...],
                    weight_refs[shard][...],
                    (((1,), (1,)), ((), ())),
                    preferred_element_type=jnp.float32,
                )

        if peers:
            diagonal = on_diagonal()
            for first in range(0, clip_count * row_count, LANES):
                piece = out_ref[pl.ds(first, LANES)]
                sums = jnp.sum(piece * piece, axis=1, keepdims=True)
                sums = jnp.sum(jnp.where(diagonal, sums, 0.0), axis=0, keepdims=True)
                squares_ref[:, :, pl.ds(first, LANES)] = jnp.broadcast_to(
                    sums[None], (peers, 1, LANES)
                )

    operands = [*flat, *(array for _, array, _, _ in shards)]
    aliases = {}
    if total is not None:
        operands.append(total)
        aliases = {len(operands): 0}
    in_specs = [pl.BlockSpec(memory_space=pltpu.VMEM) for _ in operands]
    out_shape = [jax.ShapeDtypeStruct((clip_count * row_count, lanes), jnp.float32)]
    if peers:
        out_shape.append(jax.ShapeDtypeStruct((peers, 1, clip_count * row_count), jnp.float32))
    return pl.pallas_call(
        kernel,
        in_specs=[pl.BlockSpec(memory_space=pltpu.SMEM)] + in_specs,
        out_specs=[pl.BlockSpec(memory_space=pltpu.VMEM)] * len(out_shape),
        out_shape=out_shape,
        scratch_shapes=[pltpu.VMEM((2, clip_count * row_count, depth), jnp.bfloat16)],
        input_output_aliases=aliases,
        compiler_params=pltpu.CompilerParams(vmem_limit_bytes=(16 + shard_total) * 1024 * 1024),
        cost_estimate=pl.CostEstimate(
            flops=0,
            bytes_accessed=0,
            transcendentals=0,
        ),
        name="project",
    )(where, *operands)


def row_scales(squares_ref, clip, row_count, model_width):
    diagonal = on_diagonal()
    scales = []
    for first in range(0, row_count, LANES):
        at = pl.ds(clip * row_count + first, LANES)
        mean = jnp.sum(squares_ref[:, :, at], axis=0) / model_width
        scale = jnp.broadcast_to(lax.rsqrt(mean + epsilon), (LANES, LANES))
        scales.append(jnp.sum(jnp.where(diagonal, scale, 0.0), axis=1, keepdims=True))
    return jnp.concatenate(scales, axis=0)


def finish(total, squares, gain, clip_count, columns, model_width, devices):
    rows, lanes = total.shape
    row_count = rows // clip_count
    near_rows = row_count // 2

    def kernel(total_ref, squares_ref, gain_ref, row_ref):
        lane = lax.broadcasted_iota(jnp.int32, (1, lanes), 1)
        row = jnp.zeros((1, lanes), jnp.float32)
        for clip in range(clip_count):
            scale = row_scales(squares_ref, clip, row_count, model_width)
            clean = total_ref[pl.ds(clip * row_count, near_rows)] * scale[:near_rows]
            difference = total_ref[pl.ds(clip * row_count + near_rows, near_rows)] * scale[near_rows:] - clean
            sums = jnp.sum(difference * difference, axis=0, keepdims=True)
            penalty = jnp.sum(sums * gain_ref[...] * gain_ref[...], axis=1, keepdims=True)
            row = row + sums + jnp.where(lane == columns + clip, penalty, 0.0)
        row_ref[...] = jnp.broadcast_to(row[None], row_ref.shape)

    return pl.pallas_call(
        kernel,
        out_shape=jax.ShapeDtypeStruct((devices, 1, lanes), jnp.float32),
        compiler_params=pltpu.CompilerParams(vmem_limit_bytes=16 * 1024 * 1024),
        name="finish",
    )(total, squares, gain)


def make_features(total, squares, gain, clip_count, model_width):
    rows, lanes = total.shape
    row_count = rows // clip_count
    near_rows = row_count // 2

    def kernel(total_ref, squares_ref, gain_ref, features_ref):
        for clip in range(clip_count):
            scale = row_scales(squares_ref, clip, row_count, model_width)
            clean = total_ref[pl.ds(clip * row_count, near_rows)] * scale[:near_rows]
            features_ref[clip] = (clean * gain_ref[...]).astype(jnp.bfloat16)

    return pl.pallas_call(
        kernel,
        out_shape=jax.ShapeDtypeStruct((clip_count, near_rows, lanes), jnp.bfloat16),
        compiler_params=pltpu.CompilerParams(vmem_limit_bytes=16 * 1024 * 1024),
        cost_estimate=pl.CostEstimate(
            flops=10**10, bytes_accessed=0, transcendentals=0
        ),
        name="make_features",
    )(total, squares, gain)


def conclude(rows, where, gain, model_count, clip_count, tokens):
    devices, _, lanes = rows.shape
    columns = gain.shape[1] // clip_count
    model_width = gain.shape[1] * model_count

    def kernel(where_ref, rows_ref, gain_ref, penalty_ref, grad_ref):
        row = lax.broadcasted_iota(jnp.int32, (devices, 1, lanes), 0)
        model = (row // clip_count) % model_count
        sums = []
        for clip in range(clip_count):
            mine = (model == where_ref[1]) & (row % clip_count == clip)
            sums.append(jnp.sum(jnp.where(mine, rows_ref[...], 0.0), axis=0)[:, :columns])
        sums = jnp.concatenate(sums, axis=1)
        grad = gain_ref[...] * sums / (sigma_noise * sigma_noise * tokens)
        grad_ref[...] = grad.reshape(grad_ref.shape)
        lane = lax.broadcasted_iota(jnp.int32, (devices, 1, lanes), 2)
        own = jnp.where(lane == columns + where_ref[2], rows_ref[...], 0.0)
        penalty_ref[0] = jnp.sum(own) / (sigma_noise * sigma_noise * tokens * model_width)

    return pl.pallas_call(
        kernel,
        in_specs=[pl.BlockSpec(memory_space=pltpu.SMEM)]
        + [pl.BlockSpec(memory_space=pltpu.VMEM)] * 2,
        out_specs=[
            pl.BlockSpec(memory_space=pltpu.SMEM),
            pl.BlockSpec(memory_space=pltpu.VMEM),
        ],
        out_shape=[
            jax.ShapeDtypeStruct((1,), jnp.float32),
            jax.ShapeDtypeStruct((gain.shape[1],), jnp.float32),
        ],
        compiler_params=pltpu.CompilerParams(vmem_limit_bytes=4 * 1024 * 1024),
        name="conclude",
    )(where, rows, gain)


def swap(array, axis, distance):
    count = lax.axis_size(axis)
    return lax.ppermute(array, axis, [(i, i ^ distance) for i in range(count)])


def distances(axis):
    count = lax.axis_size(axis)
    return [(axis, 1 << bit) for bit in reversed(range(count.bit_length() - 1))]


def spread(block, order, before_step):
    stacks = [([(0, 0)], block[None])]
    for step, (axis, distance) in enumerate(order):
        if step < len(order) - 1 and len(stacks) > 1:
            keys = [key for some, _ in stacks for key in some]
            stacks = [(keys, jnp.concatenate([array for _, array in stacks]))]
        received = []
        for part, (keys, array) in enumerate(stacks):
            keys = [(m ^ distance, c) if axis == "mp" else (m, c ^ distance) for m, c in keys]
            received.append((keys, swap(before_step(step, part, array), axis, distance)))
        stacks = stacks + received
    return stacks


def collect(rows, axes):
    return lax.all_to_all(rows, axes, split_axis=0, concat_axis=0, tiled=True)


def pick(options, index):
    return lax.select_n(index, *options) if len(options) > 1 else options[0]


def local(projections, perturbation, out_weight, norm_gain, live_counts):
    tile_len = projections.shape[2]
    local_width = projections.shape[4]
    slots = projections.shape[1]
    slab_count = lax.axis_size("frames")
    slab_index = lax.axis_index("frames")
    model_count = lax.axis_size("mp")
    model_index = lax.axis_index("mp")
    clip_count = lax.axis_size("dp")
    clip_index = lax.axis_index("dp")
    model_width = local_width * model_count
    token_total = slots * slab_count * tile_len
    half = local_width // clip_count
    near_rows = slots * tile_len

    def own_columns(array):
        return pick(
            [array[..., n * half : (n + 1) * half] for n in range(clip_count)], clip_index
        )

    clean = projections[0].transpose(0, 2, 1, 3)
    noise = perturbation[0].transpose(0, 2, 1, 3)
    up = [(i, i + 1) for i in range(slab_count - 1)]
    down = [(i + 1, i) for i in range(slab_count - 1)]

    tail, head = prepare_halo(clean, noise, (slots - 1, 0))
    tail, head, clean, noise, out_weight = lax.optimization_barrier(
        (tail, head, clean, noise, out_weight)
    )
    right = lax.ppermute(head, "frames", down)
    left = lax.ppermute(tail, "frames", up)
    streams = (clean, perturb(clean, noise))
    counts = jnp.pad(live_counts[0], (1, 1))
    nearby = lax.dynamic_slice_in_dim(counts, slots * slab_index, slots + 2)
    where = jnp.concatenate(
        [jnp.stack([slab_index, model_index, clip_index]).astype(jnp.int32), nearby]
    )
    gain_row = jnp.pad(own_columns(norm_gain), (0, whole_lanes(half) - half))[None]
    gain_all = norm_gain[None]

    cut = whole_lanes(half) // 2
    own_weight, *parts = prepare_weight(where, out_weight, clip_count, cut)
    line = slab_count == model_count and slab_count == 4
    last = slab_count - 1
    near, passed, across = [], [], []

    if line:
        near = [lax.ppermute(own_weight, "frames", pairs) for pairs in (down, up)]
        across = [
            lax.ppermute(block, "frames", [(0, last), (last, 0)]) for block in parts
        ]

    def before_step(stream, step, part, value):
        nonlocal near, passed, gain_row, gain_all
        if line and stream == 0 and step == 1:
            value, near, gain_row, gain_all = lax.optimization_barrier(
                (value, near, gain_row, gain_all)
            )
            passed = [
                lax.ppermute(near[0], "frames", down[:2]),
                lax.ppermute(near[1], "frames", up[1:]),
            ]
        if line and stream == 1 and step == 1:
            value, across[0] = lax.optimization_barrier((value, across[0]))
        if line and stream == 1 and step == 2 and part == 1:
            value, passed = lax.optimization_barrier((value, passed))
        return value

    gathered = []
    orders = (
        distances("dp") + distances("mp"),
        distances("mp")[:1] + distances("dp") + distances("mp")[1:],
    )
    for n, order in enumerate(orders):
        attended = attention(where, streams[n], left, right, n).reshape(near_rows, local_width)
        gathered.append(
            spread(attended, order, lambda *at, n=n: before_step(n, *at))
        )

    peers = model_count * clip_count
    if line:
        shards = [
            (0, own_weight, lambda slab: slab, lambda slab: slab >= 0),
            (0, near[0], lambda slab: jnp.minimum(slab + 1, last), lambda slab: slab < last),
            (0, near[1], lambda slab: jnp.maximum(slab - 1, 0), lambda slab: slab > 0),
            (0, passed[0], lambda slab: jnp.minimum(slab + 2, last), lambda slab: slab < 2),
            (0, passed[1], lambda slab: jnp.maximum(slab - 2, 0), lambda slab: slab >= 2),
        ]
        for first, block in zip((0, cut), across):
            shards.append(
                (first, block, lambda slab: last - slab, lambda slab: (slab == 0) | (slab == last))
            )
        (total,) = project(where, gathered, shards[:-1], None, half, 0)
        total, squares = project(where, gathered, shards[-1:], total, half, peers)
    else:
        weight = lax.all_gather(own_weight, "frames", axis=1, tiled=True)
        shards = [
            (
                0,
                lax.dynamic_slice_in_dim(weight, m * local_width, local_width, axis=1),
                lambda slab, m=m: m,
                lambda slab: slab >= 0,
            )
            for m in range(model_count)
        ]
        total, squares = project(where, gathered, shards, None, half, peers)

    squares = collect(squares, ("mp", "dp"))
    sums = finish(
        total,
        squares,
        gain_row,
        clip_count,
        half,
        model_width,
        slab_count * model_count * clip_count,
    )
    features = make_features(total, squares, gain_row, clip_count, model_width)
    sums = collect(sums, ("frames", "mp", "dp"))

    features = features[..., :half].reshape(clip_count, slots, tile_len, half)
    columns = [pick([features[d] for d in range(clip_count)], clip_index)]
    for distance in range(1, clip_count):
        sent = pick([features[d ^ distance] for d in range(clip_count)], clip_index)
        columns.append(swap(sent, "dp", distance))
    features = jnp.concatenate(
        [
            pick([columns[n ^ d] for d in range(clip_count)], clip_index)
            for n in range(clip_count)
        ],
        axis=-1,
    )[None]
    sums, features = lax.optimization_barrier((sums, features))
    penalty, gain_grad = conclude(
        sums, where, gain_all, model_count, clip_count, token_total
    )
    return (features, penalty, gain_grad)


def solution(mesh):
    placed = (
        P("dp", "frames", None, None, "mp"),
        P("dp", "frames", None, None, "mp"),
        P("frames", "mp"),
        P("mp"),
        P("dp", None),
    )
    return jax.shard_map(
        local,
        mesh=mesh,
        in_specs=placed,
        out_specs=(P("dp", "frames", None, "mp"), P("dp"), P("mp")),
        check_vma=False,
    )
```
